128 devices in a mesh: seq: 32 (over z, x, core), batch: 4 (over y).
Axes of the slice: x: 4, y: 4, z: 4, core: 2. Of those that a mesh axis runs over, the one named last changes fastest.
Arguments:
- inputs: bfloat16 [131072, 768], P(('batch', 'seq')), parts along dimension 0, may hold values from -6 to 6
- token_rates: float32 [131072], P(('batch', 'seq')), parts along dimension 0, may hold values from 0.1 to 1
- proj_query: bfloat16 [768, 256], replicated, may hold values from -0.21875 to 0.21875
- proj_key: bfloat16 [768, 256], replicated, may hold values from -0.21875 to 0.21875
- proj_value: bfloat16 [768, 256], replicated, may hold values from -0.21875 to 0.21875
- proj_output: bfloat16 [256, 768], replicated, may hold values from -0.375 to 0.375
- fast_in: float32 [256, 512], replicated, may hold values from -0.375 to 0.375
- fast_up: float32 [256, 512], replicated, may hold values from -0.375 to 0.375
- fast_out: float32 [512, 256], replicated, may hold values from -0.25 to 0.25
- cotangent: bfloat16 [131072, 768], P(('batch', 'seq')), parts along dimension 0, may hold values from -6 to 6
Outputs:
- back_inputs: bfloat16 [131072, 768], P(('batch', 'seq')), parts along dimension 0
- back_rate: float32 [131072], P(('batch', 'seq')), parts along dimension 0
- grad_in: float32 [1024, 512], P('batch'), parts along dimension 0
- grad_up: float32 [1024, 512], P('batch'), parts along dimension 0
- grad_out: float32 [2048, 256], P('batch'), parts along dimension 0
- grad_query: float32 [768, 1024], P('seq', 'batch'), parts along dimension 1
- grad_key: float32 [768, 1024], P('seq', 'batch'), parts along dimension 1
- grad_value: float32 [768, 1024], P('seq', 'batch'), parts along dimension 1
- grad_output: float32 [1024, 768], P('batch', 'seq'), parts along dimension 0
The draws below stay inside these ranges and needn't reach their ends.
There are 4 independent parts, one for each index of `batch`. The reference program is written for one: setup_inputs(seed, part) draws one part's arguments, and reference() takes and returns one part's arrays. A program takes and returns all parts, laid end to end along the dimension named above; an argument that names none is the same for every part. Nothing has to cross between parts.
All inputs are finite; a program needn't handle non-finite values.
Results may differ from the reference program's by a relative error of at most 0.029.
Values may be sent and summed in bfloat16 or wider, within the bound.
No kernel may reach another device: no remote copies, remote signals or barrier semaphores. Data moves between devices by JAX's collectives and lax.ppermute only.
A program may use at most 128 MiB of HBM per device.

```python
import math
import jax
import jax.numpy as jnp
from jax import lax

D = 768
H = 256
F = 512
NS_STEPS = 5
TOKENS = 32768


def raised(array, key, source, target, parts, factor):
    owner, partner = [(jnp.arange(array.shape[axis_at]) // (array.shape[axis_at] // parts)).reshape([-1 if axis == axis_at else 1 for axis in range(array.ndim)]) for axis_at in (source, target)]
    chosen = jax.random.permutation(key, parts)[partner]
    strong = (owner == chosen) | (owner == (partner + parts // 2) % parts)
    return jnp.where(strong, factor * array, array)


def shard_levels(stream_key, shape, split, low, largest):
    gain = 1.0
    for position, parts in split:
        steps = jax.random.uniform(jax.random.fold_in(jax.random.fold_in(stream_key, 6), position), (parts,), jnp.float32, low / len(split), largest / len(split))
        gain = gain * jnp.repeat(jnp.exp(steps), shape[position] // parts).reshape((-1,) + (1,) * (len(shape) - 1 - position))
    return gain


def gaussian(stream_key, dims, width, limit, cuts=(), held_as=jnp.bfloat16):
    array = width * jax.random.normal(stream_key, dims, jnp.float32)
    if cuts:
        array = array * shard_levels(stream_key, dims, cuts, -0.22, 0.18)
    return jnp.clip(array, -limit, limit).astype(held_as)


def bell_draw_with(key, extent, scale, limit, cuts, heavy, kind=jnp.bfloat16):
    drawn = scale * jax.random.normal(key, extent, jnp.float32)
    if cuts:
        drawn = drawn * shard_levels(key, extent, cuts, -0.22, 0.18)
    return jnp.clip(raised(drawn, jax.random.fold_in(key, 3), *heavy), -limit, limit).astype(kind)


def setup_inputs(seed: int = 0, part: int = 0) -> dict:
    key_list = jax.random.split(jax.random.key(seed), 11)
    part_keys = jax.random.split(jax.random.fold_in(key_list[10], part), 11)
    return {
        "inputs": bell_draw_with(part_keys[0], (TOKENS, D), 1.0, 6.0, ((0, 32),), (0, 1, 32, 2.75)),
        "token_rates": jnp.clip(jnp.exp(math.log(1.0) - 2.3025851 * jax.random.uniform(part_keys[1], (TOKENS,), jnp.float32) ** shard_levels(part_keys[1], (TOKENS,), ((0, 32),), -0.2, 0.2)), 0.1, 1.0),
        "proj_query": gaussian(key_list[2], (D, H), D ** -0.5, 0.21875),
        "proj_key": gaussian(key_list[3], (D, H), D ** -0.5, 0.21875),
        "proj_value": gaussian(key_list[4], (D, H), D ** -0.5, 0.21875),
        "proj_output": gaussian(key_list[5], (H, D), H ** -0.5, 0.375),
        "fast_in": gaussian(key_list[6], (H, F), H ** -0.5, 0.375, (), jnp.float32),
        "fast_up": gaussian(key_list[7], (H, F), H ** -0.5, 0.375, (), jnp.float32),
        "fast_out": gaussian(key_list[8], (F, H), F ** -0.5, 0.25, (), jnp.float32),
        "cotangent": bell_draw_with(part_keys[9], (TOKENS, D), 1.0, 6.0, ((0, 32),), (0, 1, 32, 2.75)),
    }


def rounded(value):
    return value.astype(jnp.bfloat16)

def product(left, right):
    return jnp.dot(left, right, preferred_element_type=jnp.float32)

def token_sum(left, right):
    return lax.dot_general(left, right, (((0,), (0,)), ((), ())), preferred_element_type=jnp.float32)

def times_transpose(left, right):
    return lax.dot_general(left, right, (((1,), (1,)), ((), ())), preferred_element_type=jnp.float32)

def silu_parts(pre_act):
    sigma_val = jax.nn.sigmoid(pre_act)
    activation = pre_act * sigma_val
    slope_val = sigma_val * (1.0 + pre_act * (1.0 - sigma_val))
    curvature = sigma_val * (1.0 - sigma_val) * (2.0 + pre_act * (1.0 - 2.0 * sigma_val))
    return (activation, slope_val, curvature)

def orthogonalize(matrix):
    highest = lax.Precision.HIGHEST
    current = matrix / (jnp.sqrt(jnp.sum(matrix * matrix)) + 1e-07)
    for sweep in range(NS_STEPS):
        gramian = jnp.dot(current, current.T, precision=highest)
        polynom = -4.775 * gramian + 2.0315 * jnp.dot(gramian, gramian, precision=highest)
        current = 3.4445 * current + jnp.dot(polynom, current, precision=highest)
    return current

def project(inputs, proj_query, proj_key, proj_value):
    return (rounded(product(inputs, proj_query)), rounded(product(inputs, proj_key)), rounded(product(inputs, proj_value)))

def update_section(key_rows, value_rows, token_rates, fast_in, fast_up, fast_out):
    w_in, w_up, w_out = (rounded(fast_in), rounded(fast_up), rounded(fast_out))
    scaled = rounded(token_rates[:, None] * value_rows.astype(jnp.float32))
    pre_in = product(key_rows, w_in)
    pre_up = product(key_rows, w_up)
    activation, slope_val, curvature = silu_parts(pre_in)
    hidden = rounded(activation * pre_up)
    upstream = times_transpose(scaled, w_out)
    grad_in_rows = rounded(upstream * pre_up * slope_val)
    grad_up_rows = rounded(upstream * activation)
    partial_value = jnp.stack([token_sum(key_rows, grad_in_rows), token_sum(key_rows, grad_up_rows), token_sum(scaled, hidden)])
    saved = (w_in, w_up, w_out, scaled, pre_in, pre_up, hidden, upstream, grad_in_rows, grad_up_rows)
    return (partial_value, saved)

def query_section(query_rows, cotangent, proj_output, new_in, new_up, new_out):
    n_in, n_up, n_out = (rounded(new_in), rounded(new_up), rounded(new_out))
    pre_p = product(query_rows, n_in)
    pre_r = product(query_rows, n_up)
    activation_q, slope_q, unused_curve = silu_parts(pre_p)
    hidden_q = rounded(activation_q * pre_r)
    output_rows = rounded(product(hidden_q, n_out))
    back_output = rounded(times_transpose(cotangent, proj_output))
    back_hidden = times_transpose(back_output, n_out)
    back_p = rounded(back_hidden * pre_r * slope_q)
    back_r = rounded(back_hidden * activation_q)
    partial_value = jnp.stack([token_sum(query_rows, back_p), token_sum(query_rows, back_r), token_sum(back_output, hidden_q)])
    query_grad = rounded(times_transpose(back_p, n_in) + times_transpose(back_r, n_up))
    return (partial_value, query_grad, output_rows)

def update_backward(saved, key_rows, value_rows, token_rates, back_totals):
    w_in, w_up, w_out, scaled, pre_in, pre_up, hidden, upstream, grad_in_rows, grad_up_rows = saved
    activation, slope_val, curvature = silu_parts(pre_in)
    b_in = rounded(back_totals[0])
    b_up = rounded(back_totals[1])
    b_out = rounded(back_totals[2])
    press_in = product(key_rows, b_in)
    press_up = product(key_rows, b_up)
    back_hid = product(scaled, b_out)
    back_upstream = rounded(press_in * pre_up * slope_val + press_up * activation)
    back_pre_up = rounded(press_in * upstream * slope_val + back_hid * activation)
    back_pre_in = rounded(press_in * upstream * pre_up * curvature + press_up * upstream * slope_val + back_hid * pre_up * slope_val)
    back_scaled = times_transpose(hidden, b_out) + product(back_upstream, w_out)
    back_rate = lax.optimization_barrier(jnp.sum(back_scaled * value_rows.astype(jnp.float32), axis=1))
    contrib = (token_sum(key_rows, back_pre_in), token_sum(key_rows, back_pre_up), token_sum(back_upstream, scaled))
    key_sum = times_transpose(grad_in_rows, b_in) + times_transpose(grad_up_rows, b_up)
    key_sum = key_sum + times_transpose(back_pre_in, w_in) + times_transpose(back_pre_up, w_up)
    key_grad = rounded(key_sum)
    value_grad = rounded(token_rates[:, None] * back_scaled)
    return (contrib, key_grad, value_grad, back_rate)

def input_back(query_grad, key_grad, value_grad, proj_query, proj_key, proj_value):
    total = times_transpose(query_grad, proj_query) + times_transpose(key_grad, proj_key)
    return rounded(total + times_transpose(value_grad, proj_value))

def reference(inputs, token_rates, proj_query, proj_key, proj_value, proj_output, fast_in, fast_up, fast_out, cotangent):
    query_rows, key_rows, value_rows = project(inputs, proj_query, proj_key, proj_value)
    totals, saved = update_section(key_rows, value_rows, token_rates, fast_in, fast_up, fast_out)
    ortho, ns_back = jax.vjp(jax.vmap(orthogonalize), totals)
    new_in = fast_in + ortho[0]
    new_up = fast_up + ortho[1]
    new_out = fast_out + ortho[2].T
    adjoint, query_grad, output_rows = query_section(query_rows, cotangent, proj_output, new_in, new_up, new_out)
    back_totals = ns_back(adjoint)[0]
    contrib, key_grad, value_grad, back_rate = update_backward(saved, key_rows, value_rows, token_rates, back_totals)
    grad_in = adjoint[0] + contrib[0]
    grad_up = adjoint[1] + contrib[1]
    grad_out = adjoint[2].T + contrib[2]
    back_inputs = input_back(query_grad, key_grad, value_grad, proj_query, proj_key, proj_value)
    grad_query = token_sum(inputs, query_grad)
    grad_key = token_sum(inputs, key_grad)
    grad_value = token_sum(inputs, value_grad)
    grad_output = token_sum(output_rows, cotangent)
    return (back_inputs, back_rate, grad_in, grad_up, grad_out, grad_query, grad_key, grad_value, grad_output)
```

```python
import jax
import jax.numpy as jnp
from jax import lax
from jax.sharding import PartitionSpec as P

NS_STEPS = 5


def rounded(value):
    return value.astype(jnp.bfloat16)


def product(left, right):
    return jnp.dot(left, right, preferred_element_type=jnp.float32)


def token_sum(left, right):
    return lax.dot_general(
        left, right, (((0,), (0,)), ((), ())), preferred_element_type=jnp.float32
    )


def times_transpose(left, right):
    return lax.dot_general(
        left, right, (((1,), (1,)), ((), ())), preferred_element_type=jnp.float32
    )


def silu_parts(pre_act):
    sigma_val = jax.nn.sigmoid(pre_act)
    activation = pre_act * sigma_val
    slope_val = sigma_val * (1.0 + pre_act * (1.0 - sigma_val))
    curvature = sigma_val * (1.0 - sigma_val) * (2.0 + pre_act * (1.0 - 2.0 * sigma_val))
    return (activation, slope_val, curvature)


def orthogonalize(matrix):
    highest = lax.Precision.HIGHEST
    current = matrix / (jnp.sqrt(jnp.sum(matrix * matrix)) + 1e-07)
    for sweep in range(NS_STEPS):
        gramian = jnp.dot(current, current.T, precision=highest)
        polynom = -4.775 * gramian + 2.0315 * jnp.dot(gramian, gramian, precision=highest)
        current = 3.4445 * current + jnp.dot(polynom, current, precision=highest)
    return current


def project(inputs, proj_query, proj_key, proj_value):
    return (
        rounded(product(inputs, proj_query)),
        rounded(product(inputs, proj_key)),
        rounded(product(inputs, proj_value)),
    )


def update_section(key_rows, value_rows, token_rates, fast_in, fast_up, fast_out):
    w_in, w_up, w_out = (rounded(fast_in), rounded(fast_up), rounded(fast_out))
    scaled = rounded(token_rates[:, None] * value_rows.astype(jnp.float32))
    pre_in = product(key_rows, w_in)
    pre_up = product(key_rows, w_up)
    activation, slope_val, curvature = silu_parts(pre_in)
    hidden = rounded(activation * pre_up)
    upstream = times_transpose(scaled, w_out)
    grad_in_rows = rounded(upstream * pre_up * slope_val)
    grad_up_rows = rounded(upstream * activation)
    partial_value = jnp.stack(
        [
            token_sum(key_rows, grad_in_rows),
            token_sum(key_rows, grad_up_rows),
            token_sum(scaled, hidden),
        ]
    )
    saved = (
        w_in,
        w_up,
        w_out,
        scaled,
        pre_in,
        pre_up,
        hidden,
        upstream,
        grad_in_rows,
        grad_up_rows,
    )
    return (partial_value, saved)


def query_section(query_rows, cotangent, proj_output, new_in, new_up, new_out):
    n_in, n_up, n_out = (rounded(new_in), rounded(new_up), rounded(new_out))
    pre_p = product(query_rows, n_in)
    pre_r = product(query_rows, n_up)
    activation_q, slope_q, unused_curve = silu_parts(pre_p)
    hidden_q = rounded(activation_q * pre_r)
    output_rows = rounded(product(hidden_q, n_out))
    back_output = rounded(times_transpose(cotangent, proj_output))
    back_hidden = times_transpose(back_output, n_out)
    back_p = rounded(back_hidden * pre_r * slope_q)
    back_r = rounded(back_hidden * activation_q)
    partial_value = jnp.stack(
        [
            token_sum(query_rows, back_p),
            token_sum(query_rows, back_r),
            token_sum(back_output, hidden_q),
        ]
    )
    query_grad = rounded(times_transpose(back_p, n_in) + times_transpose(back_r, n_up))
    return (partial_value, query_grad, output_rows)


def update_backward(saved, key_rows, value_rows, token_rates, back_totals):
    w_in, w_up, w_out, scaled, pre_in, pre_up, hidden, upstream, grad_in_rows, grad_up_rows = saved
    activation, slope_val, curvature = silu_parts(pre_in)
    b_in = rounded(back_totals[0])
    b_up = rounded(back_totals[1])
    b_out = rounded(back_totals[2])
    press_in = product(key_rows, b_in)
    press_up = product(key_rows, b_up)
    back_hid = product(scaled, b_out)
    back_upstream = rounded(press_in * pre_up * slope_val + press_up * activation)
    back_pre_up = rounded(press_in * upstream * slope_val + back_hid * activation)
    back_pre_in = rounded(
        press_in * upstream * pre_up * curvature
        + press_up * upstream * slope_val
        + back_hid * pre_up * slope_val
    )
    back_scaled = times_transpose(hidden, b_out) + product(back_upstream, w_out)
    back_rate = jnp.sum(back_scaled * value_rows.astype(jnp.float32), axis=1)
    contrib = jnp.stack(
        [
            token_sum(key_rows, back_pre_in),
            token_sum(key_rows, back_pre_up),
            token_sum(scaled, back_upstream),
        ]
    )
    key_sum = times_transpose(grad_in_rows, b_in) + times_transpose(grad_up_rows, b_up)
    key_sum = key_sum + times_transpose(back_pre_in, w_in) + times_transpose(back_pre_up, w_up)
    key_grad = rounded(key_sum)
    value_grad = rounded(token_rates[:, None] * back_scaled)
    return (contrib, key_grad, value_grad, back_rate)


def input_back(query_grad, key_grad, value_grad, proj_query, proj_key, proj_value):
    total = times_transpose(query_grad, proj_query) + times_transpose(key_grad, proj_key)
    return rounded(total + times_transpose(value_grad, proj_value))


def ring_pairs(first, offset):
    pairs = []
    for index in range(32):
        z, x, core = index // 8, (index // 2) % 4, index % 2
        if (core == 0) == first:
            x = (x + offset) % 4
        else:
            z = (z + offset) % 4
        pairs.append((index, z * 8 + x * 2 + core))
    return pairs


def swap_cores(value):
    return lax.ppermute(value, "seq", [(index, index ^ 1) for index in range(32)])


def places():
    me = lax.axis_index("seq")
    z, x, core = me // 8, (me // 2) % 4, me % 2
    return core, jnp.where(core == 0, x, z), jnp.where(core == 0, z, x)


def pick(which, parts):
    return lax.select_n(which, *parts)


def sum_over_cores(low, high, core):
    sent = jnp.where(core == 0, rounded(high), rounded(low))
    return jnp.where(core == 0, low, high) + swap_cores(sent).astype(jnp.float32)


def scatter_four(parts, place, first):
    received = [
        lax.ppermute(pick((place + offset) % 4, [rounded(p) for p in parts]), "seq", ring_pairs(first, offset))
        for offset in (1, 2, 3)
    ]
    total = pick(place, parts)
    for block in received:
        total = total + block.astype(jnp.float32)
    return total


def exchange_four(block, first):
    return [block] + [lax.ppermute(block, "seq", ring_pairs(first, offset)) for offset in (1, 2, 3)]


def reduce_four(value, first):
    a, b, c, d = [block.astype(jnp.float32) for block in exchange_four(rounded(value), first)]
    return (a + c) + (b + d)


def gather_four(block, place, first):
    blocks = exchange_four(block, first)
    return [pick((place - j) % 4, blocks) for j in range(4)]


def gather_total(value):
    core, place, _ = places()
    half = jnp.concatenate(gather_four(rounded(value), place, True), axis=0)
    other = swap_cores(half)
    return jnp.concatenate([jnp.where(core == 0, half, other), jnp.where(core == 0, other, half)], axis=0)


def all_sum(value):
    core, place, _ = places()
    flat = value.reshape(768, 512)
    half = sum_over_cores(flat[:384], flat[384:], core)
    quarter = scatter_four([half[96 * j : 96 * (j + 1)] for j in range(4)], place, True)
    return gather_total(reduce_four(quarter, False)).astype(jnp.float32).reshape(3, 256, 512)


def row_shares(pair):
    return jnp.concatenate([part.reshape(4, 4, 2, 24, 256) for part in pair], axis=3)


def row_sums(pair):
    core, place, second = places()
    shares = row_shares(pair)
    half = sum_over_cores(shares[:, :, 0].transpose(1, 0, 2, 3), shares[:, :, 1], core)
    quarter = scatter_four([half[j] for j in range(4)], place, True)
    mine = scatter_four([quarter[j] for j in range(4)], second, False)
    return mine[:24], mine[24:]


def body(
    inputs,
    token_rates,
    proj_query,
    proj_key,
    proj_value,
    proj_output,
    fast_in,
    fast_up,
    fast_out,
    cotangent,
):
    query_rows, key_rows, value_rows = project(inputs, proj_query, proj_key, proj_value)
    partial_value, saved = update_section(
        key_rows, value_rows, token_rates, fast_in, fast_up, fast_out
    )
    totals = all_sum(partial_value)
    ortho, ns_back = jax.vjp(jax.vmap(orthogonalize), totals)
    new_in = fast_in + ortho[0]
    new_up = fast_up + ortho[1]
    new_out = fast_out + ortho[2].T
    adjoint_part, query_grad, output_rows = query_section(
        query_rows, cotangent, proj_output, new_in, new_up, new_out
    )
    adjoint = all_sum(adjoint_part)
    back_totals = ns_back(adjoint)[0]
    contrib, key_grad, value_grad, back_rate = update_backward(
        saved, key_rows, value_rows, token_rates, back_totals
    )
    summed = all_sum(contrib)
    grad_in = adjoint[0] + summed[0]
    grad_up = adjoint[1] + summed[1]
    grad_out = (adjoint[2] + summed[2]).T
    back_inputs = input_back(query_grad, key_grad, value_grad, proj_query, proj_key, proj_value)
    grad_query, grad_output = row_sums((token_sum(inputs, query_grad), token_sum(cotangent, output_rows)))
    grad_key, grad_value = row_sums((token_sum(inputs, key_grad), token_sum(inputs, value_grad)))
    grad_output = grad_output.T
    return (
        back_inputs,
        back_rate,
        grad_in,
        grad_up,
        grad_out,
        grad_query,
        grad_key,
        grad_value,
        grad_output,
    )


def solution(mesh):
    in_specs = (
        P(("batch", "seq"), None),
        P(("batch", "seq")),
        P(),
        P(),
        P(),
        P(),
        P(),
        P(),
        P(),
        P(("batch", "seq"), None),
    )
    out_specs = (
        P(("batch", "seq"), None),
        P(("batch", "seq")),
        P("batch", None),
        P("batch", None),
        P("batch", None),
        P("seq", "batch"),
        P("seq", "batch"),
        P("seq", "batch"),
        P("batch", "seq"),
    )
    return jax.shard_map(body, mesh=mesh, in_specs=in_specs, out_specs=out_specs, check_vma=False)
```

```python
import jax
import jax.numpy as jnp
from jax import lax
from jax.experimental import pallas as pl
from jax.experimental.pallas import tpu as pltpu
from jax.sharding import PartitionSpec as P

NS_STEPS = 5
TILE = 512
F32 = jnp.float32
BF16 = jnp.bfloat16
VMEM_BYTES = 56 * 1024 * 1024


def rounded(value):
    return value.astype(jnp.bfloat16)


def product(left, right):
    return jnp.dot(left, right, preferred_element_type=jnp.float32)


def token_sum(left, right):
    return lax.dot_general(
        left, right, (((0,), (0,)), ((), ())), preferred_element_type=jnp.float32
    )


def times_transpose(left, right):
    return lax.dot_general(
        left, right, (((1,), (1,)), ((), ())), preferred_element_type=jnp.float32
    )


def sigmoid(value):
    return 1.0 / (1.0 + jnp.exp(-value))


def rows_of(columns):
    return pl.BlockSpec((TILE, columns), lambda step: (step, 0))


def whole(*shape):
    return pl.BlockSpec(shape, lambda step: (0,) * len(shape))


SCALAR = pl.BlockSpec(memory_space=pltpu.SMEM)


def params():
    return pltpu.CompilerParams(vmem_limit_bytes=VMEM_BYTES)


def cost(flops, moved):
    return pl.CostEstimate(flops=flops, bytes_accessed=moved, transcendentals=0)


def shape(dims, kind):
    return jax.ShapeDtypeStruct(dims, kind)


def add_sums(sums, parts):
    for index, part in enumerate(parts):
        rows = pl.ds(256 * index, 256)
        sums[rows, :] = sums[rows, :] + part


def start_sums(sums):
    @pl.when(pl.program_id(0) == 0)
    def _():
        sums[...] = jnp.zeros_like(sums)


def hand_out(core_ref, sums, kept_ref, sent_ref):
    @pl.when(pl.program_id(0) == pl.num_programs(0) - 1)
    def _():
        core = core_ref[0]
        kept_ref[...] = sums[pl.ds(pl.multiple_of(core * 384, 384), 384), :]
        sent_ref[...] = rounded(sums[pl.ds(pl.multiple_of((1 - core) * 384, 384), 384), :])


def update_kernel(core_ref, x_ref, rate_ref, pk_ref, pv_ref, wi_ref, wu_ref, wo_ref, k_ref, v_ref, s_ref, kept_ref, sent_ref, sums):
    start_sums(sums)
    x = x_ref[...]
    key_rows = rounded(product(x, pk_ref[...]))
    value_rows = rounded(product(x, pv_ref[...]))
    scaled = rounded(rate_ref[...] * value_rows.astype(F32))
    k_ref[...] = key_rows
    v_ref[...] = value_rows
    s_ref[...] = scaled
    pre_in = product(key_rows, wi_ref[...])
    pre_up = product(key_rows, wu_ref[...])
    upstream = times_transpose(scaled, wo_ref[...])
    sigma = sigmoid(pre_in)
    activation = pre_in * sigma
    slope = sigma * (1.0 + pre_in * (1.0 - sigma))
    hidden = rounded(activation * pre_up)
    grad_in_rows = rounded(upstream * pre_up * slope)
    grad_up_rows = rounded(upstream * activation)
    add_sums(sums, (token_sum(key_rows, grad_in_rows), token_sum(key_rows, grad_up_rows), token_sum(scaled, hidden)))
    hand_out(core_ref, sums, kept_ref, sent_ref)


def update_rows(core, inputs, rates, proj_key, proj_value, w_in, w_up, w_out):
    tokens = inputs.shape[0]
    return pl.pallas_call(
        update_kernel,
        grid=(tokens // TILE,),
        in_specs=[SCALAR, rows_of(768), rows_of(1), whole(768, 256), whole(768, 256), whole(256, 512), whole(256, 512), whole(512, 256)],
        out_specs=[rows_of(256)] * 3 + [whole(384, 512)] * 2,
        out_shape=[shape((tokens, 256), BF16)] * 3 + [shape((384, 512), F32), shape((384, 512), BF16)],
        scratch_shapes=[pltpu.VMEM((768, 512), F32)],
        compiler_params=params(),
        cost_estimate=cost(2400000000, 6000000),
        name="update_rows",
    )(core, inputs, rates, proj_key, proj_value, w_in, w_up, w_out)


def pair_kernel(x_ref, c_ref, pq_ref, po_ref, q_ref, bo_ref):
    q_ref[...] = rounded(product(x_ref[...], pq_ref[...]))
    bo_ref[...] = rounded(times_transpose(c_ref[...], po_ref[...]))


def query_inputs(inputs, cotangent, proj_query, proj_output):
    tokens = inputs.shape[0]
    return pl.pallas_call(
        pair_kernel,
        grid=(tokens // TILE,),
        in_specs=[rows_of(768), rows_of(768), whole(768, 256), whole(256, 768)],
        out_specs=[rows_of(256)] * 2,
        out_shape=[shape((tokens, 256), BF16)] * 2,
        compiler_params=params(),
        cost_estimate=cost(800000000, 5000000),
        name="query_inputs",
    )(inputs, cotangent, proj_query, proj_output)


def query_kernel(core_ref, q_ref, bo_ref, ni_ref, nu_ref, no_ref, bp_ref, br_ref, h_ref, kept_ref, sent_ref, sums):
    start_sums(sums)
    query_rows, back_output = q_ref[...], bo_ref[...]
    pre_p = product(query_rows, ni_ref[...])
    pre_r = product(query_rows, nu_ref[...])
    back_hidden = product(back_output, no_ref[...])
    sigma = sigmoid(pre_p)
    activation = pre_p * sigma
    slope = sigma * (1.0 + pre_p * (1.0 - sigma))
    hidden = rounded(activation * pre_r)
    back_p = rounded(back_hidden * pre_r * slope)
    back_r = rounded(back_hidden * activation)
    bp_ref[...] = back_p
    br_ref[...] = back_r
    h_ref[...] = hidden
    add_sums(sums, (token_sum(query_rows, back_p), token_sum(query_rows, back_r), token_sum(back_output, hidden)))
    hand_out(core_ref, sums, kept_ref, sent_ref)


def query_rows_back(core, query_rows, back_output, n_in, n_up, n_out):
    tokens = query_rows.shape[0]
    return pl.pallas_call(
        query_kernel,
        grid=(tokens // TILE,),
        in_specs=[SCALAR, rows_of(256), rows_of(256)] + [whole(256, 512)] * 3,
        out_specs=[rows_of(512)] * 3 + [whole(384, 512)] * 2,
        out_shape=[shape((tokens, 512), BF16)] * 3 + [shape((384, 512), F32), shape((384, 512), BF16)],
        scratch_shapes=[pltpu.VMEM((768, 512), F32)],
        compiler_params=params(),
        cost_estimate=cost(1600000000, 6000000),
        name="query_rows_back",
    )(core, query_rows, back_output, n_in, n_up, n_out)


def query_grad_kernel(bp_ref, br_ref, h_ref, ni_ref, nu_ref, no_ref, x_ref, c_ref, qg_ref, gq_ref, go_ref):
    @pl.when(pl.program_id(0) == 0)
    def _():
        gq_ref[...] = jnp.zeros_like(gq_ref)
        go_ref[...] = jnp.zeros_like(go_ref)

    query_grad = rounded(times_transpose(bp_ref[...], ni_ref[...]) + times_transpose(br_ref[...], nu_ref[...]))
    output_rows = rounded(times_transpose(h_ref[...], no_ref[...]))
    qg_ref[...] = query_grad
    gq_ref[...] += token_sum(x_ref[...], query_grad)
    go_ref[...] += token_sum(c_ref[...], output_rows)


def query_grads(back_p, back_r, hidden, n_in, n_up, n_out, inputs, cotangent):
    tokens = inputs.shape[0]
    return pl.pallas_call(
        query_grad_kernel,
        grid=(tokens // TILE,),
        in_specs=[rows_of(512)] * 3 + [whole(256, 512)] * 3 + [rows_of(768)] * 2,
        out_specs=[rows_of(256), whole(768, 256), whole(768, 256)],
        out_shape=[shape((tokens, 256), BF16), shape((768, 256), F32), shape((768, 256), F32)],
        compiler_params=params(),
        cost_estimate=cost(1600000000, 10000000),
        name="query_grads",
    )(back_p, back_r, hidden, n_in, n_up, n_out, inputs, cotangent)


def back_kernel(core_ref, k_ref, v_ref, s_ref, rate_ref, wi_ref, wu_ref, wo_ref, b_ref, bpi_ref, bpu_ref, gi_ref, gu_ref, vg_ref, rate_out, kept_ref, sent_ref, sums):
    start_sums(sums)
    key_rows, scaled = k_ref[...], s_ref[...]
    b_in, b_up, b_out = b_ref[0], b_ref[1], b_ref[2]
    pre_in = product(key_rows, wi_ref[...])
    pre_up = product(key_rows, wu_ref[...])
    upstream = times_transpose(scaled, wo_ref[...])
    press_in = product(key_rows, b_in)
    press_up = product(key_rows, b_up)
    back_hid = product(scaled, b_out)
    sigma = sigmoid(pre_in)
    activation = pre_in * sigma
    slope = sigma * (1.0 + pre_in * (1.0 - sigma))
    curvature = sigma * (1.0 - sigma) * (2.0 + pre_in * (1.0 - 2.0 * sigma))
    hidden = rounded(activation * pre_up)
    rise = pre_up * slope
    gi_ref[...] = rounded(upstream * rise)
    gu_ref[...] = rounded(upstream * activation)
    back_upstream = rounded(press_in * rise + press_up * activation)
    steep = upstream * slope
    back_pre_up = rounded(press_in * steep + back_hid * activation)
    back_pre_in = rounded(press_in * upstream * pre_up * curvature + press_up * steep + back_hid * rise)
    bpi_ref[...] = back_pre_in
    bpu_ref[...] = back_pre_up
    add_sums(sums, (token_sum(key_rows, back_pre_in), token_sum(key_rows, back_pre_up), token_sum(scaled, back_upstream)))
    hand_out(core_ref, sums, kept_ref, sent_ref)
    back_scaled = times_transpose(hidden, b_out) + product(back_upstream, wo_ref[...])
    rate_out[...] = jnp.sum(back_scaled * v_ref[...].astype(F32), axis=1, keepdims=True)
    vg_ref[...] = rounded(rate_ref[...] * back_scaled)


def update_back(core, key_rows, value_rows, scaled, rates, w_in, w_up, w_out, back):
    tokens = key_rows.shape[0]
    return pl.pallas_call(
        back_kernel,
        grid=(tokens // TILE,),
        in_specs=[SCALAR] + [rows_of(256)] * 3 + [rows_of(1), whole(256, 512), whole(256, 512), whole(512, 256), whole(3, 256, 512)],
        out_specs=[rows_of(512)] * 4 + [rows_of(256), rows_of(1)] + [whole(384, 512)] * 2,
        out_shape=[shape((tokens, 512), BF16)] * 4
        + [shape((tokens, 256), BF16), shape((tokens, 1), F32), shape((384, 512), F32), shape((384, 512), BF16)],
        scratch_shapes=[pltpu.VMEM((768, 512), F32)],
        compiler_params=params(),
        cost_estimate=cost(3000000000, 8000000),
        name="update_back",
    )(core, key_rows, value_rows, scaled, rates, w_in, w_up, w_out, back)


def key_grad_kernel(gi_ref, gu_ref, bpi_ref, bpu_ref, vg_ref, b_ref, wi_ref, wu_ref, x_ref, kg_ref, gk_ref, gv_ref):
    @pl.when(pl.program_id(0) == 0)
    def _():
        gk_ref[...] = jnp.zeros_like(gk_ref)
        gv_ref[...] = jnp.zeros_like(gv_ref)

    key_sum = times_transpose(gi_ref[...], b_ref[0]) + times_transpose(gu_ref[...], b_ref[1])
    key_sum = key_sum + times_transpose(bpi_ref[...], wi_ref[...]) + times_transpose(bpu_ref[...], wu_ref[...])
    key_grad = rounded(key_sum)
    kg_ref[...] = key_grad
    x = x_ref[...]
    gk_ref[...] += token_sum(x, key_grad)
    gv_ref[...] += token_sum(x, vg_ref[...])


def key_grads(grad_in_rows, grad_up_rows, back_pre_in, back_pre_up, value_grad, back, w_in, w_up, inputs):
    tokens = inputs.shape[0]
    return pl.pallas_call(
        key_grad_kernel,
        grid=(tokens // TILE,),
        in_specs=[rows_of(512)] * 4 + [rows_of(256), whole(3, 256, 512), whole(256, 512), whole(256, 512), rows_of(768)],
        out_specs=[rows_of(256), whole(768, 256), whole(768, 256)],
        out_shape=[shape((tokens, 256), BF16), shape((768, 256), F32), shape((768, 256), F32)],
        compiler_params=params(),
        cost_estimate=cost(1900000000, 10000000),
        name="key_grads",
    )(grad_in_rows, grad_up_rows, back_pre_in, back_pre_up, value_grad, back, w_in, w_up, inputs)


def input_kernel(q_ref, k_ref, v_ref, pq_ref, pk_ref, pv_ref, out_ref):
    total = times_transpose(q_ref[...], pq_ref[...]) + times_transpose(k_ref[...], pk_ref[...])
    out_ref[...] = rounded(total + times_transpose(v_ref[...], pv_ref[...]))


def input_back(query_grad, key_grad, value_grad, proj_query, proj_key, proj_value):
    tokens = query_grad.shape[0]
    return pl.pallas_call(
        input_kernel,
        grid=(tokens // TILE,),
        in_specs=[rows_of(256)] * 3 + [whole(768, 256)] * 3,
        out_specs=rows_of(768),
        out_shape=shape((tokens, 768), BF16),
        compiler_params=params(),
        cost_estimate=cost(1200000000, 4000000),
        name="input_back",
    )(query_grad, key_grad, value_grad, proj_query, proj_key, proj_value)


def halves(value):
    high = rounded(value)
    return high, rounded(value - high.astype(F32))


def fine_product(left, right):
    return product(left[0], right[0]) + (product(left[0], right[1]) + product(left[1], right[0]))


def fine_transpose(left, right):
    return times_transpose(left[0], right[0]) + (times_transpose(left[0], right[1]) + times_transpose(left[1], right[0]))


def newton_schulz(current):
    split = halves(current)
    gram = fine_transpose(split, split)
    gram_split = halves(gram)
    poly = halves(-4.775 * gram + 2.0315 * fine_product(gram_split, gram_split))
    return 3.4445 * current + fine_product(poly, split), (split, gram_split, poly)


def newton_schulz_back(grad, split, gram_split, poly):
    grad_split = halves(grad)
    outer = fine_transpose(grad_split, split)
    outer = outer + outer.T
    square = fine_product(halves(outer), gram_split)
    inner = -4.775 * outer + 2.0315 * (square + square.T)
    return 3.4445 * grad + (fine_product(poly, grad_split) + fine_product(halves(inner), split))


def norm_of(matrix):
    return jnp.sqrt(jnp.sum(matrix * matrix))


def matrix_at(core, mine_ref, other_ref, scratch):
    scratch[pl.ds(pl.multiple_of(core * 384, 384), 384), :] = mine_ref[...].astype(F32)
    scratch[pl.ds(pl.multiple_of((1 - core) * 384, 384), 384), :] = other_ref[...].astype(F32)


def ortho_kernel(core_ref, mine_ref, other_ref, fi_ref, fu_ref, fo_ref, ni_ref, nu_ref, no_ref, scratch):
    matrix_at(core_ref[0], mine_ref, other_ref, scratch)
    current = []
    for index in range(3):
        matrix = scratch[256 * index : 256 * index + 256, :]
        current.append(matrix / (norm_of(matrix) + 1e-07))
    for _ in range(NS_STEPS):
        current = [newton_schulz(matrix)[0] for matrix in current]
    for matrix, fast_ref, out_ref in zip(current, (fi_ref, fu_ref, fo_ref), (ni_ref, nu_ref, no_ref)):
        out_ref[...] = rounded(fast_ref[...] + matrix)


def ortho(core, mine, other, fast_in, fast_up, fast_out_t):
    return pl.pallas_call(
        ortho_kernel,
        in_specs=[SCALAR] + [pl.BlockSpec(memory_space=pltpu.VMEM)] * 5,
        out_specs=[pl.BlockSpec(memory_space=pltpu.VMEM)] * 3,
        out_shape=[shape((256, 512), BF16)] * 3,
        scratch_shapes=[pltpu.VMEM((768, 512), F32)],
        compiler_params=params(),
        cost_estimate=cost(7500000000, 3000000),
        name="ortho",
    )(core, mine, other, fast_in, fast_up, fast_out_t)


def trail_kernel(core_ref, mine_ref, other_ref, x_ref, a_ref, p_ref, scratch):
    matrix_at(core_ref[0], mine_ref, other_ref, scratch)
    current = []
    for index in range(3):
        matrix = scratch[256 * index : 256 * index + 256, :]
        current.append(matrix / (norm_of(matrix) + 1e-07))
    for sweep in range(NS_STEPS):
        for index in range(3):
            current[index], kept = newton_schulz(current[index])
            for ref, pair in zip((x_ref, a_ref, p_ref), kept):
                ref[sweep, index, 0] = pair[0]
                ref[sweep, index, 1] = pair[1]


def ortho_trail(core, mine, other):
    return pl.pallas_call(
        trail_kernel,
        in_specs=[SCALAR] + [pl.BlockSpec(memory_space=pltpu.VMEM)] * 2,
        out_specs=[pl.BlockSpec(memory_space=pltpu.VMEM)] * 3,
        out_shape=[shape((NS_STEPS, 3, 2, 256, columns), BF16) for columns in (512, 256, 256)],
        scratch_shapes=[pltpu.VMEM((768, 512), F32)],
        compiler_params=params(),
        cost_estimate=cost(7500000000, 17000000),
        name="ortho_trail",
    )(core, mine, other)


def ortho_back_kernel(core_ref, tm_ref, to_ref, mine_ref, other_ref, x_ref, a_ref, p_ref, b_ref, scratch, totals):
    matrix_at(core_ref[0], mine_ref, other_ref, scratch)
    matrix_at(core_ref[0], tm_ref, to_ref, totals)
    grads = [scratch[256 * index : 256 * index + 256, :] for index in range(3)]
    for sweep in reversed(range(NS_STEPS)):
        for index in range(3):
            kept = [(ref[sweep, index, 0], ref[sweep, index, 1]) for ref in (x_ref, a_ref, p_ref)]
            grads[index] = newton_schulz_back(grads[index], *kept)
    for index in range(3):
        matrix = totals[256 * index : 256 * index + 256, :]
        norm = norm_of(matrix)
        scale = 1.0 / (norm + 1e-07)
        dot = jnp.sum(grads[index] * matrix)
        b_ref[index] = rounded(grads[index] * scale - matrix * (dot * scale * scale / norm))


def ortho_back(core, totals, adjoint, trail):
    return pl.pallas_call(
        ortho_back_kernel,
        in_specs=[SCALAR] + [pl.BlockSpec(memory_space=pltpu.VMEM)] * 7,
        out_specs=pl.BlockSpec(memory_space=pltpu.VMEM),
        out_shape=shape((3, 256, 512), BF16),
        scratch_shapes=[pltpu.VMEM((768, 512), F32)] * 2,
        compiler_params=params(),
        cost_estimate=cost(10500000000, 18000000),
        name="ortho_back",
    )(core, *totals, *adjoint, *trail)


def ring_pairs(first, offset):
    pairs = []
    for index in range(32):
        z, x, core = index // 8, (index // 2) % 4, index % 2
        if (core == 0) == first:
            x = (x + offset) % 4
        else:
            z = (z + offset) % 4
        pairs.append((index, z * 8 + x * 2 + core))
    return pairs


def swap_cores(value):
    return lax.ppermute(value, "seq", [(index, index ^ 1) for index in range(32)])


def places():
    me = lax.axis_index("seq")
    z, x, core = me // 8, (me // 2) % 4, me % 2
    return core, jnp.where(core == 0, x, z), jnp.where(core == 0, z, x)


def pick(which, parts):
    return lax.select_n(which, *parts)


def sum_over_cores(low, high, core):
    sent = jnp.where(core == 0, rounded(high), rounded(low))
    return jnp.where(core == 0, low, high) + swap_cores(sent).astype(jnp.float32)


def scatter_four(parts, place, first):
    received = [
        lax.ppermute(pick((place + offset) % 4, [rounded(p) for p in parts]), "seq", ring_pairs(first, offset))
        for offset in (1, 2, 3)
    ]
    total = pick(place, parts)
    for block in received:
        total = total + block.astype(jnp.float32)
    return total


def exchange_four(block, first):
    return [block] + [lax.ppermute(block, "seq", ring_pairs(first, offset)) for offset in (1, 2, 3)]


def reduce_four(value, first):
    a, b, c, d = [block.astype(jnp.float32) for block in exchange_four(rounded(value), first)]
    return (a + c) + (b + d)


def gather_four(block, place, first):
    blocks = exchange_four(block, first)
    return [pick((place - j) % 4, blocks) for j in range(4)]


def gather_halves(value):
    _, place, _ = places()
    half = jnp.concatenate(gather_four(rounded(value), place, True), axis=0)
    return half, swap_cores(half)


def core_sum(kept, sent):
    return kept + swap_cores(sent).astype(jnp.float32)


def quarter_sum(half):
    _, place, _ = places()
    return scatter_four([half[96 * j : 96 * (j + 1)] for j in range(4)], place, True)


def after(values, anchor):
    return lax.optimization_barrier((values, anchor))[0]


def joined(halves_pair, core):
    mine, other = halves_pair
    return jnp.concatenate([jnp.where(core == 0, mine, other), jnp.where(core == 0, other, mine)], axis=0)


def row_shares(pair):
    return jnp.concatenate([part.reshape(4, 4, 2, 24, 256) for part in pair], axis=3)


def row_sums(pair):
    core, place, second = places()
    shares = row_shares(pair)
    half = sum_over_cores(shares[:, :, 0].transpose(1, 0, 2, 3), shares[:, :, 1], core)
    quarter = scatter_four([half[j] for j in range(4)], place, True)
    mine = scatter_four([quarter[j] for j in range(4)], second, False)
    return mine[:24], mine[24:]


def body(
    inputs,
    token_rates,
    proj_query,
    proj_key,
    proj_value,
    proj_output,
    fast_in,
    fast_up,
    fast_out,
    cotangent,
):
    core_at, _, _ = places()
    core = core_at.reshape(1)
    rates = token_rates.reshape(-1, 1)
    w_in, w_up, w_out = rounded(fast_in), rounded(fast_up), rounded(fast_out)

    key_rows, value_rows, scaled, kept, sent = update_rows(
        core, inputs, rates, proj_key, proj_value, w_in, w_up, w_out
    )
    half = core_sum(kept, sent)
    query_rows, back_output = query_inputs(*after((inputs, cotangent), half), proj_query, proj_output)
    fast_out_t = after(fast_out, half).T
    quarter = quarter_sum(half)
    quarter, query_rows, back_output, fast_out_t = lax.optimization_barrier((quarter, query_rows, back_output, fast_out_t))
    totals = gather_halves(reduce_four(quarter, False))
    n_in, n_up, n_out = ortho(core, *totals, fast_in, fast_up, fast_out_t)

    back_p, back_r, hidden_q, kept, sent = query_rows_back(core, query_rows, back_output, n_in, n_up, n_out)
    half = core_sum(kept, sent)
    trail = ortho_trail(core, *after(totals, half))
    quarter = quarter_sum(half)
    quarter, trail = lax.optimization_barrier((quarter, trail))
    query_grad, grad_query, grad_output = query_grads(
        *after((back_p, back_r, hidden_q), quarter), n_in, n_up, n_out, inputs, cotangent
    )
    shared = reduce_four(quarter, False)
    shared, query_grad, grad_query, grad_output = lax.optimization_barrier((shared, query_grad, grad_query, grad_output))
    adjoint = gather_halves(shared)
    grad_query, grad_output = row_sums((grad_query, grad_output))
    back = ortho_back(core, totals, adjoint, trail)

    back_pre_in, back_pre_up, grad_in_rows, grad_up_rows, value_grad, back_rate, kept, sent = update_back(
        core, key_rows, value_rows, scaled, rates, w_in, w_up, w_out, back
    )
    half = core_sum(kept, sent)
    key_grad, grad_key, grad_value = key_grads(
        grad_in_rows, grad_up_rows, back_pre_in, back_pre_up, value_grad, back, w_in, w_up, inputs
    )
    quarter = quarter_sum(half)
    summed = gather_halves(reduce_four(quarter, False))
    total = (joined(adjoint, core_at).astype(F32) + joined(summed, core_at).astype(F32)).reshape(3, 256, 512)
    grad_key, grad_value = row_sums((grad_key, grad_value))
    back_inputs = input_back(query_grad, key_grad, value_grad, proj_query, proj_key, proj_value)
    return (
        back_inputs,
        back_rate.reshape(-1),
        total[0],
        total[1],
        total[2].T,
        grad_query,
        grad_key,
        grad_value,
        grad_output.T,
    )


def solution(mesh):
    in_specs = (
        P(("batch", "seq"), None),
        P(("batch", "seq")),
        P(),
        P(),
        P(),
        P(),
        P(),
        P(),
        P(),
        P(("batch", "seq"), None),
    )
    out_specs = (
        P(("batch", "seq"), None),
        P(("batch", "seq")),
        P("batch", None),
        P("batch", None),
        P("batch", None),
        P("seq", "batch"),
        P("seq", "batch"),
        P("seq", "batch"),
        P("batch", "seq"),
    )
    return jax.shard_map(body, mesh=mesh, in_specs=in_specs, out_specs=out_specs, check_vma=False)
```

```python
import jax
import jax.numpy as jnp
from jax import lax
from jax.experimental import pallas as pl
from jax.experimental.pallas import tpu as pltpu
from jax.sharding import PartitionSpec as P

NS_STEPS = 5
TILE = 512
LARGE = 1024
F32 = jnp.float32
BF16 = jnp.bfloat16
VMEM_BYTES = 56 * 1024 * 1024


def rounded(value):
    return value.astype(jnp.bfloat16)


def product(left, right):
    return jnp.dot(left, right, preferred_element_type=jnp.float32)


def token_sum(left, right):
    return lax.dot_general(
        left, right, (((0,), (0,)), ((), ())), preferred_element_type=jnp.float32
    )


def times_transpose(left, right):
    return lax.dot_general(
        left, right, (((1,), (1,)), ((), ())), preferred_element_type=jnp.float32
    )


def sigmoid(value):
    return 1.0 / (1.0 + jnp.exp(-value))


def column(row):
    wide = jnp.broadcast_to(row, (128, row.shape[1])).T
    return jnp.concatenate([wide, wide], axis=1)


def rows_of(columns, tile=TILE):
    return pl.BlockSpec((tile, columns), lambda step: (step, 0))


def row_block(tile):
    return pl.BlockSpec((1, tile), lambda step: (0, step))


def whole(*shape):
    return pl.BlockSpec(shape, lambda step: (0,) * len(shape))


SCALAR = pl.BlockSpec(memory_space=pltpu.SMEM)


def params():
    return pltpu.CompilerParams(vmem_limit_bytes=VMEM_BYTES)


def cost(flops, moved):
    return pl.CostEstimate(flops=flops, bytes_accessed=moved, transcendentals=0)


def shape(dims, kind):
    return jax.ShapeDtypeStruct(dims, kind)


def add_sums(sums, parts):
    for index, part in enumerate(parts):
        rows = pl.ds(256 * index, 256)
        sums[rows, :] = sums[rows, :] + part


def start_sums(sums):
    @pl.when(pl.program_id(0) == 0)
    def _():
        sums[...] = jnp.zeros_like(sums)


def hand_out(core_ref, sums, kept_ref, sent_ref):
    @pl.when(pl.program_id(0) == pl.num_programs(0) - 1)
    def _():
        core = core_ref[0]
        kept_ref[...] = sums[pl.ds(pl.multiple_of(core * 384, 384), 384), :]
        sent_ref[...] = rounded(sums[pl.ds(pl.multiple_of((1 - core) * 384, 384), 384), :])


def first_step(action):
    pl.when(pl.program_id(0) == 0)(action)


def last_step(action):
    pl.when(pl.program_id(0) == pl.num_programs(0) - 1)(action)


def in_order(core_ref, own_ref, other_ref, pair):
    core = core_ref[0]
    pair[pl.ds(pl.multiple_of(core * 256, 256), 256), :] = own_ref[...]
    pair[pl.ds(pl.multiple_of((1 - core) * 256, 256), 256), :] = other_ref[...]


def share_rows(core, total, kept_ref, sent_ref, start):
    for a in range(4):
        for b in (0, 2):
            low = [pl.multiple_of(jnp.where(core == 0, (c * 4 + a) * 48, (a * 4 + c) * 48 + 24), 8) for c in (b, b + 1)]
            high = [pl.multiple_of(jnp.where(core == 0, (a * 4 + c) * 48 + 24, (c * 4 + a) * 48), 8) for c in (b, b + 1)]
            at = start + 24 * b
            kept_ref[a, at : at + 48, :] = jnp.concatenate([total[pl.ds(row, 24), :] for row in low], axis=0)
            sent_ref[a, at : at + 48, :] = rounded(jnp.concatenate([total[pl.ds(row, 24), :] for row in high], axis=0))


def update_kernel(core_ref, x_ref, rate_ref, pk_ref, pv_ref, fi_ref, fu_ref, fo_ref, k_ref, v_ref, s_ref, kept_ref, sent_ref, sums, wi_ref, wu_ref, wo_ref):
    @first_step
    def _():
        sums[...] = jnp.zeros_like(sums)
        wi_ref[...] = rounded(fi_ref[...])
        wu_ref[...] = rounded(fu_ref[...])
        wo_ref[...] = rounded(fo_ref[...])

    x = x_ref[...]
    key_rows = rounded(product(x, pk_ref[...]))
    value_rows = rounded(product(x, pv_ref[...]))
    scaled = rounded(column(rate_ref[...]) * value_rows.astype(F32))
    k_ref[...] = key_rows
    v_ref[...] = value_rows
    s_ref[...] = scaled
    pre_in = product(key_rows, wi_ref[...])
    pre_up = product(key_rows, wu_ref[...])
    upstream = times_transpose(scaled, wo_ref[...])
    sigma = sigmoid(pre_in)
    activation = pre_in * sigma
    slope = sigma * (1.0 + pre_in * (1.0 - sigma))
    hidden = rounded(activation * pre_up)
    grad_in_rows = rounded(upstream * pre_up * slope)
    grad_up_rows = rounded(upstream * activation)
    add_sums(sums, (token_sum(key_rows, grad_in_rows), token_sum(key_rows, grad_up_rows), token_sum(scaled, hidden)))
    hand_out(core_ref, sums, kept_ref, sent_ref)


WEIGHTS = [((256, 512), BF16), ((256, 512), BF16), ((512, 256), BF16)]


def update_rows(core, inputs, rates, proj_key, proj_value, fast_in, fast_up, fast_out):
    tokens = inputs.shape[0]
    return pl.pallas_call(
        update_kernel,
        grid=(tokens // LARGE,),
        in_specs=[SCALAR, rows_of(768, LARGE), row_block(LARGE), whole(768, 256), whole(768, 256), whole(256, 512), whole(256, 512), whole(512, 256)],
        out_specs=[rows_of(256, LARGE)] * 3 + [whole(384, 512)] * 2,
        out_shape=[shape((tokens, 256), BF16)] * 3 + [shape((384, 512), F32), shape((384, 512), BF16)],
        scratch_shapes=[pltpu.VMEM((768, 512), F32)] + [pltpu.VMEM(*w) for w in WEIGHTS],
        compiler_params=params(),
        cost_estimate=cost(2400000000, 6000000),
        name="update_rows",
    )(core, inputs, rates, proj_key, proj_value, fast_in, fast_up, fast_out)


def project_kernel(x_ref, w_ref, out_ref):
    out_ref[...] = rounded(product(x_ref[...], w_ref[...]))


def project_back_kernel(x_ref, w_ref, out_ref):
    out_ref[...] = rounded(times_transpose(x_ref[...], w_ref[...]))


def projected(kernel, rows, weights, name):
    tokens = rows.shape[0]
    return pl.pallas_call(
        kernel,
        grid=(tokens // TILE,),
        in_specs=[rows_of(768), whole(*weights.shape)],
        out_specs=rows_of(256),
        out_shape=shape((tokens, 256), BF16),
        compiler_params=params(),
        cost_estimate=cost(400000000, 2500000),
        name=name,
    )(rows, weights)


def query_kernel(core_ref, q_ref, bo_ref, own_ref, other_ref, nu_ref, bp_ref, br_ref, h_ref, kept_ref, sent_ref, sums, pair):
    start_sums(sums)

    @first_step
    def _():
        in_order(core_ref, own_ref, other_ref, pair)

    query_rows, back_output = q_ref[...], bo_ref[...]
    pre_p = product(query_rows, pair[:256, :])
    pre_r = product(query_rows, nu_ref[...])
    back_hidden = product(back_output, pair[256:, :])
    sigma = sigmoid(pre_p)
    activation = pre_p * sigma
    slope = sigma * (1.0 + pre_p * (1.0 - sigma))
    hidden = rounded(activation * pre_r)
    back_p = rounded(back_hidden * pre_r * slope)
    back_r = rounded(back_hidden * activation)
    bp_ref[...] = back_p
    br_ref[...] = back_r
    h_ref[...] = hidden
    add_sums(sums, (token_sum(query_rows, back_p), token_sum(query_rows, back_r), token_sum(back_output, hidden)))
    hand_out(core_ref, sums, kept_ref, sent_ref)


def query_rows_back(core, query_rows, back_output, n_own, n_other, n_up):
    tokens = query_rows.shape[0]
    return pl.pallas_call(
        query_kernel,
        grid=(tokens // LARGE,),
        in_specs=[SCALAR, rows_of(256, LARGE), rows_of(256, LARGE)] + [whole(256, 512)] * 3,
        out_specs=[rows_of(512, LARGE)] * 3 + [whole(384, 512)] * 2,
        out_shape=[shape((tokens, 512), BF16)] * 3 + [shape((384, 512), F32), shape((384, 512), BF16)],
        scratch_shapes=[pltpu.VMEM((768, 512), F32), pltpu.VMEM((512, 512), BF16)],
        compiler_params=params(),
        cost_estimate=cost(1600000000, 6000000),
        name="query_rows_back",
    )(core, query_rows, back_output, n_own, n_other, n_up)


def out_grad_kernel(core_ref, h_ref, own_ref, other_ref, c_ref, kept_ref, sent_ref, go, pair):
    @first_step
    def _():
        in_order(core_ref, own_ref, other_ref, pair)
        go[...] = jnp.zeros_like(go)

    output_rows = rounded(times_transpose(h_ref[...], pair[256:, :]))
    go[...] += token_sum(c_ref[...], output_rows)

    @last_step
    def _():
        share_rows(core_ref[0], go, kept_ref, sent_ref, 0)


SHARES = [shape((4, 96, 256), F32), shape((4, 96, 256), BF16)]


def out_grads(core, hidden, n_own, n_other, cotangent):
    tokens = cotangent.shape[0]
    return pl.pallas_call(
        out_grad_kernel,
        grid=(tokens // TILE,),
        in_specs=[SCALAR, rows_of(512), whole(256, 512), whole(256, 512), rows_of(768)],
        out_specs=[whole(4, 96, 256)] * 2,
        out_shape=SHARES,
        scratch_shapes=[pltpu.VMEM((768, 256), F32), pltpu.VMEM((512, 512), BF16)],
        compiler_params=params(),
        cost_estimate=cost(700000000, 4000000),
        name="out_grads",
    )(core, hidden, n_own, n_other, cotangent)


def query_grad_kernel(core_ref, bp_ref, br_ref, own_ref, other_ref, nu_ref, x_ref, qg_ref, kept_ref, sent_ref, gq, pair):
    @first_step
    def _():
        in_order(core_ref, own_ref, other_ref, pair)
        gq[...] = jnp.zeros_like(gq)

    query_grad = rounded(times_transpose(bp_ref[...], pair[:256, :]) + times_transpose(br_ref[...], nu_ref[...]))
    qg_ref[...] = query_grad
    gq[...] += token_sum(x_ref[...], query_grad)

    @last_step
    def _():
        share_rows(core_ref[0], gq, kept_ref, sent_ref, 0)


def query_grads(core, back_p, back_r, n_own, n_other, n_up, inputs):
    tokens = inputs.shape[0]
    return pl.pallas_call(
        query_grad_kernel,
        grid=(tokens // TILE,),
        in_specs=[SCALAR] + [rows_of(512)] * 2 + [whole(256, 512)] * 3 + [rows_of(768)],
        out_specs=[rows_of(256)] + [whole(4, 96, 256)] * 2,
        out_shape=[shape((tokens, 256), BF16)] + SHARES,
        scratch_shapes=[pltpu.VMEM((768, 256), F32), pltpu.VMEM((512, 512), BF16)],
        compiler_params=params(),
        cost_estimate=cost(950000000, 5000000),
        name="query_grads",
    )(core, back_p, back_r, n_own, n_other, n_up, inputs)


def back_kernel(core_ref, x_ref, k_ref, v_ref, s_ref, rate_ref, fi_ref, fu_ref, fo_ref, own_ref, other_ref, bu_ref, kg_ref, vg_ref, rate_out, kept_ref, sent_ref, sums, gk, gv, pair, wi_ref, wu_ref, wo_ref):
    @first_step
    def _():
        sums[...] = jnp.zeros_like(sums)
        gk[...] = jnp.zeros_like(gk)
        gv[...] = jnp.zeros_like(gv)
        in_order(core_ref, own_ref, other_ref, pair)
        wi_ref[...] = rounded(fi_ref[...])
        wu_ref[...] = rounded(fu_ref[...])
        wo_ref[...] = rounded(fo_ref[...])

    key_rows, scaled = k_ref[...], s_ref[...]
    b_in, b_up, b_out = pair[:256, :], bu_ref[...], pair[256:, :]
    pre_in = product(key_rows, wi_ref[...])
    pre_up = product(key_rows, wu_ref[...])
    upstream = times_transpose(scaled, wo_ref[...])
    press_in = product(key_rows, b_in)
    press_up = product(key_rows, b_up)
    back_hid = product(scaled, b_out)
    sigma = sigmoid(pre_in)
    activation = pre_in * sigma
    fall = 1.0 - sigma
    slope = sigma * (1.0 + pre_in * fall)
    curvature = sigma * fall * (2.0 + pre_in * (1.0 - 2.0 * sigma))
    hidden = rounded(activation * pre_up)
    rise = pre_up * slope
    steep = upstream * slope
    grad_in_rows = rounded(upstream * rise)
    grad_up_rows = rounded(upstream * activation)
    back_upstream = rounded(press_in * rise + press_up * activation)
    back_pre_up = rounded(press_in * steep + back_hid * activation)
    back_pre_in = rounded(press_in * upstream * pre_up * curvature + press_up * steep + back_hid * rise)
    add_sums(sums, (token_sum(key_rows, back_pre_in), token_sum(key_rows, back_pre_up), token_sum(scaled, back_upstream)))
    back_scaled = times_transpose(hidden, b_out) + product(back_upstream, wo_ref[...])
    scores = jnp.sum(back_scaled * v_ref[...].astype(F32), axis=1, keepdims=True)
    rate_out[...] = jnp.broadcast_to(scores, (LARGE, 128)).T[:1, :]
    value_grad = rounded(column(rate_ref[...]) * back_scaled)
    vg_ref[...] = value_grad
    key_sum = times_transpose(grad_in_rows, b_in) + times_transpose(grad_up_rows, b_up)
    key_sum = key_sum + times_transpose(back_pre_in, wi_ref[...]) + times_transpose(back_pre_up, wu_ref[...])
    key_grad = rounded(key_sum)
    kg_ref[...] = key_grad
    x = x_ref[...]
    gk[...] += token_sum(x, key_grad)
    gv[...] += token_sum(x, value_grad)

    @last_step
    def _():
        core = core_ref[0]
        for a in range(4):
            mine = sums[pl.ds(pl.multiple_of(core * 384 + 96 * a, 96), 96), :]
            theirs = rounded(sums[pl.ds(pl.multiple_of((1 - core) * 384 + 96 * a, 96), 96), :])
            for side in range(2):
                kept_ref[a, 96 * side : 96 * side + 96, :] = mine[:, 256 * side : 256 * side + 256]
                sent_ref[a, 96 * side : 96 * side + 96, :] = theirs[:, 256 * side : 256 * side + 256]
        share_rows(core, gk, kept_ref, sent_ref, 192)
        share_rows(core, gv, kept_ref, sent_ref, 288)


def update_back(core, inputs, key_rows, value_rows, scaled, rates, fast_in, fast_up, fast_out, b_own, b_other, b_up):
    tokens = key_rows.shape[0]
    return pl.pallas_call(
        back_kernel,
        grid=(tokens // LARGE,),
        in_specs=[SCALAR, rows_of(768, LARGE)]
        + [rows_of(256, LARGE)] * 3
        + [row_block(LARGE), whole(256, 512), whole(256, 512), whole(512, 256)]
        + [whole(256, 512)] * 3,
        out_specs=[rows_of(256, LARGE)] * 2 + [row_block(LARGE), whole(4, 384, 256), whole(4, 384, 256)],
        out_shape=[shape((tokens, 256), BF16)] * 2
        + [shape((1, tokens), F32), shape((4, 384, 256), F32), shape((4, 384, 256), BF16)],
        scratch_shapes=[pltpu.VMEM((768, 512), F32), pltpu.VMEM((768, 256), F32), pltpu.VMEM((768, 256), F32), pltpu.VMEM((512, 512), BF16)]
        + [pltpu.VMEM(*w) for w in WEIGHTS],
        compiler_params=params(),
        cost_estimate=cost(5600000000, 10000000),
        name="update_back",
    )(core, inputs, key_rows, value_rows, scaled, rates, fast_in, fast_up, fast_out, b_own, b_other, b_up)


def input_kernel(q_ref, k_ref, v_ref, pq_ref, pk_ref, pv_ref, out_ref):
    total = times_transpose(q_ref[...], pq_ref[...]) + times_transpose(k_ref[...], pk_ref[...])
    out_ref[...] = rounded(total + times_transpose(v_ref[...], pv_ref[...]))


def input_back(query_grad, key_grad, value_grad, proj_query, proj_key, proj_value):
    tokens = query_grad.shape[0]
    return pl.pallas_call(
        input_kernel,
        grid=(tokens // TILE,),
        in_specs=[rows_of(256)] * 3 + [whole(768, 256)] * 3,
        out_specs=rows_of(768),
        out_shape=shape((tokens, 768), BF16),
        compiler_params=params(),
        cost_estimate=cost(1200000000, 4000000),
        name="input_back",
    )(query_grad, key_grad, value_grad, proj_query, proj_key, proj_value)


SHIFTS = (0.0, 0.05, 0.4, 0.9, 0.9)


def coefficients(shift):
    return 3.4445 - 4.775 * shift + 2.0315 * shift * shift, -4.775 + 2.0 * 2.0315 * shift, 2.0315


def on_diagonal(value):
    rows = lax.broadcasted_iota(jnp.int32, (256, 256), 0)
    columns = lax.broadcasted_iota(jnp.int32, (256, 256), 1)
    return jnp.where(rows == columns, value, 0.0)


def newton_schulz(current, shift):
    constant, linear, square = coefficients(shift)
    rows = rounded(current)
    excess = times_transpose(rows, rows)
    if shift:
        excess = excess - on_diagonal(shift)
    short = rounded(excess)
    poly = rounded(linear * excess + square * product(short, short))
    return constant * current + product(poly, rows), (rows, short, poly)


def newton_schulz_back(grad, rows, short, poly, shift):
    constant, linear, square = coefficients(shift)
    grad_rows = rounded(grad)
    outer = times_transpose(grad_rows, rows)
    outer = outer + outer.T
    inner = product(rounded(outer), short)
    inner = rounded(linear * outer + square * (inner + inner.T))
    return constant * grad + (product(poly, grad_rows) + product(inner, rows))


def norm_of(matrix):
    return jnp.sqrt(jnp.sum(matrix * matrix))


def two_matrices(core, half_ref, other_ref, middle):
    middle[pl.ds(pl.multiple_of(core * 128, 128), 128), :] = half_ref[pl.ds(pl.multiple_of((1 - core) * 256, 256), 128), :]
    middle[pl.ds(pl.multiple_of((1 - core) * 128, 128), 128), :] = other_ref[...]
    own = half_ref[pl.ds(pl.multiple_of(core * 128, 128), 256), :]
    return [own.astype(F32), middle[...].astype(F32)]


def ortho_kernel(core_ref, half_ref, other_ref, fast_own_ref, fast_up_ref, own_ref, up_ref, x_ref, a_ref, p_ref, middle):
    current = []
    for matrix in two_matrices(core_ref[0], half_ref, other_ref, middle):
        current.append(matrix * (1.0 / (norm_of(matrix) + 1e-07)))
    for sweep in range(NS_STEPS):
        for index in range(2):
            current[index], kept = newton_schulz(current[index], SHIFTS[sweep])
            for ref, value in zip((x_ref, a_ref, p_ref), kept):
                ref[sweep, index] = value
    own_ref[...] = rounded(fast_own_ref[...] + current[0])
    up_ref[...] = rounded(fast_up_ref[...] + current[1])


IN_VMEM = pl.BlockSpec(memory_space=pltpu.VMEM)


def ortho(core, half, other, fast_own, fast_up):
    return pl.pallas_call(
        ortho_kernel,
        in_specs=[SCALAR] + [IN_VMEM] * 4,
        out_specs=[IN_VMEM] * 5,
        out_shape=[shape((256, 512), BF16)] * 2 + [shape((NS_STEPS, 2, 256, columns), BF16) for columns in (512, 256, 256)],
        scratch_shapes=[pltpu.VMEM((256, 512), BF16)],
        compiler_params=params(),
        cost_estimate=cost(1700000000, 6000000),
        name="ortho",
    )(core, half, other, fast_own, fast_up)


def ortho_back_kernel(core_ref, th_ref, to_ref, half_ref, other_ref, x_ref, a_ref, p_ref, own_ref, up_ref, middle):
    grads = two_matrices(core_ref[0], half_ref, other_ref, middle)
    for sweep in reversed(range(NS_STEPS)):
        for index in range(2):
            kept = [ref[sweep, index] for ref in (x_ref, a_ref, p_ref)]
            grads[index] = newton_schulz_back(grads[index], *kept, SHIFTS[sweep])
    totals = two_matrices(core_ref[0], th_ref, to_ref, middle)
    for matrix, grad, out_ref in zip(totals, grads, (own_ref, up_ref)):
        norm = norm_of(matrix)
        scale = 1.0 / (norm + 1e-07)
        dot = jnp.sum(grad * matrix)
        out_ref[...] = rounded(grad * scale - matrix * (dot * scale * scale / norm))


def ortho_back(core, totals, adjoint, trail):
    return pl.pallas_call(
        ortho_back_kernel,
        in_specs=[SCALAR] + [IN_VMEM] * 7,
        out_specs=[IN_VMEM] * 2,
        out_shape=[shape((256, 512), BF16)] * 2,
        scratch_shapes=[pltpu.VMEM((256, 512), BF16)],
        compiler_params=params(),
        cost_estimate=cost(2700000000, 6000000),
        name="ortho_back",
    )(core, *totals, *adjoint, *trail)


def finish_kernel(core_ref, half_ref, other_ref, gi_ref, gu_ref, go_ref, scratch):
    core = core_ref[0]
    scratch[pl.ds(pl.multiple_of(core * 384, 384), 384), :] = half_ref[...]
    scratch[pl.ds(pl.multiple_of((1 - core) * 384, 384), 384), :] = other_ref[...]
    gi_ref[...] = scratch[:256, :].astype(F32)
    gu_ref[...] = scratch[256:512, :].astype(F32)
    go_ref[...] = scratch[512:, :].astype(F32).T


def finish(core, half, other):
    return pl.pallas_call(
        finish_kernel,
        in_specs=[SCALAR] + [IN_VMEM] * 2,
        out_specs=[IN_VMEM] * 3,
        out_shape=[shape((256, 512), F32)] * 2 + [shape((512, 256), F32)],
        scratch_shapes=[pltpu.VMEM((768, 512), BF16)],
        compiler_params=params(),
        cost_estimate=cost(1000000, 3000000),
        name="finish",
    )(core, half, other)


def ring_pairs(first, offset):
    pairs = []
    for index in range(32):
        z, x, core = index // 8, (index // 2) % 4, index % 2
        if (core == 0) == first:
            x = (x + offset) % 4
        else:
            z = (z + offset) % 4
        pairs.append((index, z * 8 + x * 2 + core))
    return pairs


def swap_cores(value):
    return lax.ppermute(value, "seq", [(index, index ^ 1) for index in range(32)])


def places():
    me = lax.axis_index("seq")
    z, x, core = me // 8, (me // 2) % 4, me % 2
    return core, jnp.where(core == 0, x, z), jnp.where(core == 0, z, x)


def pick(which, parts):
    return lax.select_n(which, *parts)


def part_at(parts, which):
    return lax.dynamic_index_in_dim(parts, which % 4, 0, keepdims=False)


def scatter_four(parts, place, first):
    received = [
        lax.ppermute(rounded(part_at(parts, place + offset)), "seq", ring_pairs(first, offset)) for offset in (1, 2, 3)
    ]
    total = part_at(parts, place)
    for block in received:
        total = total + block.astype(jnp.float32)
    return total


def exchange_four(block, first):
    return [block] + [lax.ppermute(block, "seq", ring_pairs(first, offset)) for offset in (1, 2, 3)]


def sum_four(blocks):
    a, b, c, d = [block.astype(jnp.float32) for block in blocks]
    return (a + c) + (b + d)


def in_places(blocks, place):
    return jnp.concatenate([pick((place - j) % 4, blocks) for j in range(4)], axis=0)


def middle_half(half, core):
    return swap_cores(jnp.where(core == 0, half[256:], half[:128]))


def together(*values):
    return lax.optimization_barrier(values)


def body(
    inputs,
    token_rates,
    proj_query,
    proj_key,
    proj_value,
    proj_output,
    fast_in,
    fast_up,
    fast_out,
    cotangent,
):
    core_at, place, second = places()
    core = core_at.reshape(1)
    rates = token_rates.reshape(1, -1)

    key_rows, value_rows, scaled, kept, sent = update_rows(
        core, inputs, rates, proj_key, proj_value, fast_in, fast_up, fast_out
    )
    query_rows = projected(project_kernel, together(sent, inputs)[1], proj_query, "query_rows")
    received, query_rows = together(swap_cores(sent), query_rows)
    half = (kept + received.astype(F32)).reshape(4, 96, 512)
    fast_own = jnp.where(core_at == 0, fast_in, together(half, fast_out)[1].T)
    quarter, fast_own = together(scatter_four(half, place, True), fast_own)
    shared = sum_four(exchange_four(rounded(quarter), False))
    back_output = projected(project_back_kernel, together(shared, cotangent)[1], proj_output, "back_output")
    blocks, back_output = together(exchange_four(rounded(shared), True), back_output)
    half = in_places(blocks, place)
    totals = half, middle_half(half, core_at)
    n_own, n_up, *trail = ortho(core, *totals, fast_own, fast_up)
    n_other = swap_cores(n_own)

    back_p, back_r, hidden_q, kept, sent = query_rows_back(core, query_rows, back_output, n_own, n_other, n_up)
    half = (kept + swap_cores(sent).astype(F32)).reshape(4, 96, 512)
    half, hidden_q, back_p, back_r = together(half, hidden_q, back_p, back_r)
    out_kept, out_sent = out_grads(core, hidden_q, n_own, n_other, cotangent)
    quarter, out_kept, out_sent, back_p, back_r = together(scatter_four(half, place, True), out_kept, out_sent, back_p, back_r)
    query_grad, query_kept, query_sent = query_grads(core, back_p, back_r, n_own, n_other, n_up, inputs)
    blocks, query_grad, query_kept, query_sent = together(
        exchange_four(rounded(quarter), False), query_grad, query_kept, query_sent
    )
    adjoint_share = sum_four(blocks)
    blocks = exchange_four(rounded(adjoint_share), True)
    early_sent = jnp.concatenate([query_sent, out_sent], axis=1)
    half = in_places(blocks, place)
    b_own, b_up = ortho_back(core, totals, (half, middle_half(half, core_at)), trail)
    b_other = swap_cores(b_own)
    early = jnp.concatenate([query_kept, out_kept], axis=1) + swap_cores(early_sent).astype(F32)

    key_grad, value_grad, back_rate, kept, sent = update_back(
        core, inputs, key_rows, value_rows, scaled, rates, fast_in, fast_up, fast_out, b_own, b_other, b_up
    )
    half = jnp.concatenate([kept + swap_cores(sent).astype(F32), early], axis=1)
    half, key_grad, value_grad = together(half, key_grad, value_grad)
    back_inputs = input_back(query_grad, key_grad, value_grad, proj_query, proj_key, proj_value)
    quarter, back_inputs = together(scatter_four(half, place, True), back_inputs)
    contrib = rounded(quarter[:192])
    shares = quarter[192:].reshape(4, 4, 24, 256)

    def shares_of(which):
        return lax.dynamic_index_in_dim(shares, which % 4, 1, keepdims=False).reshape(96, 256)

    received = [
        lax.ppermute(
            jnp.concatenate([contrib, rounded(shares_of(second + offset))], axis=0), "seq", ring_pairs(False, offset)
        )
        for offset in (1, 2, 3)
    ]
    summed = sum_four([contrib] + [block[:192] for block in received])
    mine = shares_of(second)
    for block in received:
        mine = mine + block[192:].astype(F32)
    grad_key, grad_value, grad_query, grad_output = [mine[24 * index : 24 * index + 24] for index in range(4)]
    share = adjoint_share + jnp.concatenate([summed[:96], summed[96:]], axis=1)
    blocks = exchange_four(rounded(share), True)
    half = in_places(blocks, place)
    grad_in, grad_up, grad_out = finish(core, half, swap_cores(half))
    return (
        back_inputs,
        back_rate.reshape(-1),
        grad_in,
        grad_up,
        grad_out,
        grad_query,
        grad_key,
        grad_value,
        grad_output.T,
    )


def solution(mesh):
    in_specs = (
        P(("batch", "seq"), None),
        P(("batch", "seq")),
        P(),
        P(),
        P(),
        P(),
        P(),
        P(),
        P(),
        P(("batch", "seq"), None),
    )
    out_specs = (
        P(("batch", "seq"), None),
        P(("batch", "seq")),
        P("batch", None),
        P("batch", None),
        P("batch", None),
        P("seq", "batch"),
        P("seq", "batch"),
        P("seq", "batch"),
        P("batch", "seq"),
    )
    return jax.shard_map(body, mesh=mesh, in_specs=in_specs, out_specs=out_specs, check_vma=False)
```

```python
import jax
import jax.numpy as jnp
from jax import lax
from jax.experimental import pallas as pl
from jax.experimental.pallas import tpu as pltpu
from jax.sharding import PartitionSpec as P

NS_STEPS = 5
TILE = 512
LARGE = 1024
F32 = jnp.float32
BF16 = jnp.bfloat16
VMEM_BYTES = 28 * 1024 * 1024


def rounded(value):
    return value.astype(jnp.bfloat16)


def product(left, right):
    return jnp.dot(left, right, preferred_element_type=jnp.float32)


def token_sum(left, right):
    return lax.dot_general(
        left, right, (((0,), (0,)), ((), ())), preferred_element_type=jnp.float32
    )


def times_transpose(left, right):
    return lax.dot_general(
        left, right, (((1,), (1,)), ((), ())), preferred_element_type=jnp.float32
    )


def sigmoid(value):
    return 1.0 / (1.0 + jnp.exp(-value))


def column(row):
    wide = jnp.broadcast_to(row, (128, row.shape[1])).T
    return jnp.concatenate([wide, wide], axis=1)


def rows_of(columns, tile=TILE):
    return pl.BlockSpec((tile, columns), lambda step: (step, 0))


def row_block(tile):
    return pl.BlockSpec((1, tile), lambda step: (0, step))


def whole(*shape):
    return pl.BlockSpec(shape, lambda step: (0,) * len(shape))


SCALAR = pl.BlockSpec(memory_space=pltpu.SMEM)


def params(limit=VMEM_BYTES):
    return pltpu.CompilerParams(vmem_limit_bytes=limit)


def cost(flops, moved):
    return pl.CostEstimate(flops=flops, bytes_accessed=moved, transcendentals=0)


def shape(dims, kind):
    return jax.ShapeDtypeStruct(dims, kind)


def add_sums(sums, parts):
    for index, part in enumerate(parts):
        rows = pl.ds(256 * index, 256)
        sums[rows, :] = sums[rows, :] + part


def start_sums(sums):
    @pl.when(pl.program_id(0) == 0)
    def _():
        sums[...] = jnp.zeros_like(sums)


def hand_out(core_ref, sums, kept_ref, sent_ref):
    @pl.when(pl.program_id(0) == pl.num_programs(0) - 1)
    def _():
        core = core_ref[0]
        kept_ref[...] = sums[pl.ds(pl.multiple_of(core * 384, 384), 384), :]
        sent_ref[...] = rounded(sums[pl.ds(pl.multiple_of((1 - core) * 384, 384), 384), :])


def first_step(action):
    pl.when(pl.program_id(0) == 0)(action)


def last_step(action):
    pl.when(pl.program_id(0) == pl.num_programs(0) - 1)(action)


def in_order(core_ref, own_ref, other_ref, pair):
    core = core_ref[0]
    pair[pl.ds(pl.multiple_of(core * 256, 256), 256), :] = own_ref[...]
    pair[pl.ds(pl.multiple_of((1 - core) * 256, 256), 256), :] = other_ref[...]


def share_rows(core, total, kept_ref, sent_ref, start):
    for a in range(4):
        for b in (0, 2):
            low = [pl.multiple_of(jnp.where(core == 0, (c * 4 + a) * 48, (a * 4 + c) * 48 + 24), 8) for c in (b, b + 1)]
            high = [pl.multiple_of(jnp.where(core == 0, (a * 4 + c) * 48 + 24, (c * 4 + a) * 48), 8) for c in (b, b + 1)]
            at = start + 24 * b
            kept_ref[a, at : at + 48, :] = jnp.concatenate([total[pl.ds(row, 24), :] for row in low], axis=0)
            sent_ref[a, at : at + 48, :] = rounded(jnp.concatenate([total[pl.ds(row, 24), :] for row in high], axis=0))


def update_kernel(core_ref, x_ref, rate_ref, pq_ref, pk_ref, pv_ref, fi_ref, fu_ref, fo_ref, q_ref, k_ref, v_ref, s_ref, kept_ref, sent_ref, sums, wi_ref, wu_ref, wo_ref):
    @first_step
    def _():
        sums[...] = jnp.zeros_like(sums)
        wi_ref[...] = rounded(fi_ref[...])
        wu_ref[...] = rounded(fu_ref[...])
        wo_ref[...] = rounded(fo_ref[...])

    x = x_ref[...]
    key_rows = rounded(product(x, pk_ref[...]))
    value_rows = rounded(product(x, pv_ref[...]))
    scaled = rounded(column(rate_ref[...]) * value_rows.astype(F32))
    q_ref[...] = rounded(product(x, pq_ref[...]))
    k_ref[...] = key_rows
    v_ref[...] = value_rows
    s_ref[...] = scaled
    pre_in = product(key_rows, wi_ref[...])
    pre_up = product(key_rows, wu_ref[...])
    upstream = times_transpose(scaled, wo_ref[...])
    sigma = sigmoid(pre_in)
    activation = pre_in * sigma
    slope = sigma * (1.0 + pre_in * (1.0 - sigma))
    hidden = rounded(activation * pre_up)
    grad_in_rows = rounded(upstream * pre_up * slope)
    grad_up_rows = rounded(upstream * activation)
    both = token_sum(key_rows, jnp.concatenate([grad_in_rows, grad_up_rows], axis=1))
    add_sums(sums, (both[:, :512], both[:, 512:], token_sum(scaled, hidden)))
    hand_out(core_ref, sums, kept_ref, sent_ref)


WEIGHTS = [((256, 512), BF16), ((256, 512), BF16), ((512, 256), BF16)]


def update_rows(core, inputs, rates, proj_query, proj_key, proj_value, fast_in, fast_up, fast_out):
    tokens = inputs.shape[0]
    return pl.pallas_call(
        update_kernel,
        grid=(tokens // LARGE,),
        in_specs=[SCALAR, rows_of(768, LARGE), row_block(LARGE)] + [whole(768, 256)] * 3 + [ whole(256, 512), whole(256, 512), whole(512, 256)],
        out_specs=[rows_of(256, LARGE)] * 4 + [whole(384, 512)] * 2,
        out_shape=[shape((tokens, 256), BF16)] * 4 + [shape((384, 512), F32), shape((384, 512), BF16)],
        scratch_shapes=[pltpu.VMEM((768, 512), F32)] + [pltpu.VMEM(*w) for w in WEIGHTS],
        compiler_params=params(60 * 1024 * 1024),
        cost_estimate=cost(2400000000, 6000000),
        name="update_rows",
    )(core, inputs, rates, proj_query, proj_key, proj_value, fast_in, fast_up, fast_out)


def project_back_kernel(x_ref, w_ref, out_ref):
    out_ref[...] = rounded(times_transpose(x_ref[...], w_ref[...]))


def projected(kernel, rows, weights, name):
    tokens = rows.shape[0]
    return pl.pallas_call(
        kernel,
        grid=(tokens // TILE,),
        in_specs=[rows_of(768), whole(*weights.shape)],
        out_specs=rows_of(256),
        out_shape=shape((tokens, 256), BF16),
        compiler_params=params(),
        cost_estimate=cost(400000000, 2500000),
        name=name,
    )(rows, weights)


def query_kernel(core_ref, q_ref, bo_ref, own_ref, other_ref, nu_ref, bp_ref, br_ref, h_ref, kept_ref, sent_ref, sums, pair):
    start_sums(sums)

    @first_step
    def _():
        in_order(core_ref, own_ref, other_ref, pair)

    query_rows, back_output = q_ref[...], bo_ref[...]
    pre_p = product(query_rows, pair[:256, :])
    pre_r = product(query_rows, nu_ref[...])
    back_hidden = product(back_output, pair[256:, :])
    sigma = sigmoid(pre_p)
    activation = pre_p * sigma
    slope = sigma * (1.0 + pre_p * (1.0 - sigma))
    hidden = rounded(activation * pre_r)
    back_p = rounded(back_hidden * pre_r * slope)
    back_r = rounded(back_hidden * activation)
    bp_ref[...] = back_p
    br_ref[...] = back_r
    h_ref[...] = hidden
    both = token_sum(query_rows, jnp.concatenate([back_p, back_r], axis=1))
    add_sums(sums, (both[:, :512], both[:, 512:], token_sum(back_output, hidden)))
    hand_out(core_ref, sums, kept_ref, sent_ref)


def query_rows_back(core, query_rows, back_output, n_own, n_other, n_up):
    tokens = query_rows.shape[0]
    return pl.pallas_call(
        query_kernel,
        grid=(tokens // LARGE,),
        in_specs=[SCALAR, rows_of(256, LARGE), rows_of(256, LARGE)] + [whole(256, 512)] * 3,
        out_specs=[rows_of(512, LARGE)] * 3 + [whole(384, 512)] * 2,
        out_shape=[shape((tokens, 512), BF16)] * 3 + [shape((384, 512), F32), shape((384, 512), BF16)],
        scratch_shapes=[pltpu.VMEM((768, 512), F32), pltpu.VMEM((512, 512), BF16)],
        compiler_params=params(),
        cost_estimate=cost(1600000000, 6000000),
        name="query_rows_back",
    )(core, query_rows, back_output, n_own, n_other, n_up)


def out_grad_kernel(core_ref, h_ref, own_ref, other_ref, c_ref, kept_ref, sent_ref, go, pair):
    @first_step
    def _():
        in_order(core_ref, own_ref, other_ref, pair)
        go[...] = jnp.zeros_like(go)

    output_rows = rounded(times_transpose(h_ref[...], pair[256:, :]))
    go[...] += token_sum(c_ref[...], output_rows)

    @last_step
    def _():
        share_rows(core_ref[0], go, kept_ref, sent_ref, 0)


SHARES = [shape((4, 96, 256), F32), shape((4, 96, 256), BF16)]


def out_grads(core, hidden, n_own, n_other, cotangent):
    tokens = cotangent.shape[0]
    return pl.pallas_call(
        out_grad_kernel,
        grid=(tokens // TILE,),
        in_specs=[SCALAR, rows_of(512), whole(256, 512), whole(256, 512), rows_of(768)],
        out_specs=[whole(4, 96, 256)] * 2,
        out_shape=SHARES,
        scratch_shapes=[pltpu.VMEM((768, 256), F32), pltpu.VMEM((512, 512), BF16)],
        compiler_params=params(),
        cost_estimate=cost(700000000, 4000000),
        name="out_grads",
    )(core, hidden, n_own, n_other, cotangent)


def query_grad_kernel(core_ref, bp_ref, br_ref, own_ref, other_ref, nu_ref, x_ref, qg_ref, kept_ref, sent_ref, gq, pair):
    @first_step
    def _():
        in_order(core_ref, own_ref, other_ref, pair)
        gq[...] = jnp.zeros_like(gq)

    query_grad = rounded(times_transpose(bp_ref[...], pair[:256, :]) + times_transpose(br_ref[...], nu_ref[...]))
    qg_ref[...] = query_grad
    gq[...] += token_sum(x_ref[...], query_grad)

    @last_step
    def _():
        share_rows(core_ref[0], gq, kept_ref, sent_ref, 0)


def query_grads(core, back_p, back_r, n_own, n_other, n_up, inputs):
    tokens = inputs.shape[0]
    return pl.pallas_call(
        query_grad_kernel,
        grid=(tokens // TILE,),
        in_specs=[SCALAR] + [rows_of(512)] * 2 + [whole(256, 512)] * 3 + [rows_of(768)],
        out_specs=[rows_of(256)] + [whole(4, 96, 256)] * 2,
        out_shape=[shape((tokens, 256), BF16)] + SHARES,
        scratch_shapes=[pltpu.VMEM((768, 256), F32), pltpu.VMEM((512, 512), BF16)],
        compiler_params=params(),
        cost_estimate=cost(950000000, 5000000),
        name="query_grads",
    )(core, back_p, back_r, n_own, n_other, n_up, inputs)


def back_kernel(core_ref, x_ref, k_ref, v_ref, s_ref, rate_ref, fi_ref, fu_ref, fo_ref, own_ref, other_ref, bu_ref, kg_ref, vg_ref, rate_out, kept_ref, sent_ref, sums, gk, gv, pair, wi_ref, wu_ref, wo_ref):
    @first_step
    def _():
        sums[...] = jnp.zeros_like(sums)
        gk[...] = jnp.zeros_like(gk)
        gv[...] = jnp.zeros_like(gv)
        in_order(core_ref, own_ref, other_ref, pair)
        wi_ref[...] = rounded(fi_ref[...])
        wu_ref[...] = rounded(fu_ref[...])
        wo_ref[...] = rounded(fo_ref[...])

    key_rows, scaled = k_ref[...], s_ref[...]
    b_in, b_up, b_out = pair[:256, :], bu_ref[...], pair[256:, :]
    pre_in = product(key_rows, wi_ref[...])
    pre_up = product(key_rows, wu_ref[...])
    upstream = times_transpose(scaled, wo_ref[...])
    press_in = product(key_rows, b_in)
    press_up = product(key_rows, b_up)
    back_hid = product(scaled, b_out)
    sigma = sigmoid(pre_in)
    activation = pre_in * sigma
    fall = 1.0 - sigma
    slope = sigma * (1.0 + pre_in * fall)
    curvature = sigma * fall * (2.0 + pre_in * (1.0 - 2.0 * sigma))
    hidden = rounded(activation * pre_up)
    rise = pre_up * slope
    steep = upstream * slope
    grad_in_rows = rounded(upstream * rise)
    grad_up_rows = rounded(upstream * activation)
    back_upstream = rounded(press_in * rise + press_up * activation)
    back_pre_up = rounded(press_in * steep + back_hid * activation)
    back_pre_in = rounded(press_in * upstream * pre_up * curvature + press_up * steep + back_hid * rise)
    both = token_sum(key_rows, jnp.concatenate([back_pre_in, back_pre_up], axis=1))
    add_sums(sums, (both[:, :512], both[:, 512:], token_sum(scaled, back_upstream)))
    back_scaled = times_transpose(hidden, b_out) + product(back_upstream, wo_ref[...])
    scores = jnp.sum(back_scaled * v_ref[...].astype(F32), axis=1, keepdims=True)
    rate_out[...] = jnp.broadcast_to(scores, (LARGE, 128)).T[:1, :]
    value_grad = rounded(column(rate_ref[...]) * back_scaled)
    vg_ref[...] = value_grad
    key_sum = times_transpose(grad_in_rows, b_in) + times_transpose(grad_up_rows, b_up)
    key_sum = key_sum + times_transpose(back_pre_in, wi_ref[...]) + times_transpose(back_pre_up, wu_ref[...])
    key_grad = rounded(key_sum)
    kg_ref[...] = key_grad
    both = token_sum(x_ref[...], jnp.concatenate([key_grad, value_grad], axis=1))
    gk[...] += both[:, :256]
    gv[...] += both[:, 256:]

    @last_step
    def _():
        core = core_ref[0]
        for a in range(4):
            mine = sums[pl.ds(pl.multiple_of(core * 384 + 96 * a, 96), 96), :]
            theirs = rounded(sums[pl.ds(pl.multiple_of((1 - core) * 384 + 96 * a, 96), 96), :])
            for side in range(2):
                kept_ref[a, 96 * side : 96 * side + 96, :] = mine[:, 256 * side : 256 * side + 256]
                sent_ref[a, 96 * side : 96 * side + 96, :] = theirs[:, 256 * side : 256 * side + 256]
        share_rows(core, gk, kept_ref, sent_ref, 192)
        share_rows(core, gv, kept_ref, sent_ref, 288)


def update_back(core, inputs, key_rows, value_rows, scaled, rates, fast_in, fast_up, fast_out, b_own, b_other, b_up):
    tokens = key_rows.shape[0]
    return pl.pallas_call(
        back_kernel,
        grid=(tokens // LARGE,),
        in_specs=[SCALAR, rows_of(768, LARGE)]
        + [rows_of(256, LARGE)] * 3
        + [row_block(LARGE), whole(256, 512), whole(256, 512), whole(512, 256)]
        + [whole(256, 512)] * 3,
        out_specs=[rows_of(256, LARGE)] * 2 + [row_block(LARGE), whole(4, 384, 256), whole(4, 384, 256)],
        out_shape=[shape((tokens, 256), BF16)] * 2
        + [shape((1, tokens), F32), shape((4, 384, 256), F32), shape((4, 384, 256), BF16)],
        scratch_shapes=[pltpu.VMEM((768, 512), F32), pltpu.VMEM((768, 256), F32), pltpu.VMEM((768, 256), F32), pltpu.VMEM((512, 512), BF16)]
        + [pltpu.VMEM(*w) for w in WEIGHTS],
        compiler_params=params(),
        cost_estimate=cost(5600000000, 10000000),
        name="update_back",
    )(core, inputs, key_rows, value_rows, scaled, rates, fast_in, fast_up, fast_out, b_own, b_other, b_up)


def input_kernel(q_ref, k_ref, v_ref, pq_ref, pk_ref, pv_ref, out_ref):
    total = times_transpose(q_ref[...], pq_ref[...]) + times_transpose(k_ref[...], pk_ref[...])
    out_ref[...] = rounded(total + times_transpose(v_ref[...], pv_ref[...]))


def input_back(query_grad, key_grad, value_grad, proj_query, proj_key, proj_value):
    tokens = query_grad.shape[0]
    return pl.pallas_call(
        input_kernel,
        grid=(tokens // TILE,),
        in_specs=[rows_of(256)] * 3 + [whole(768, 256)] * 3,
        out_specs=rows_of(768),
        out_shape=shape((tokens, 768), BF16),
        compiler_params=params(),
        cost_estimate=cost(1200000000, 4000000),
        name="input_back",
    )(query_grad, key_grad, value_grad, proj_query, proj_key, proj_value)


SHIFTS = (0.0, 0.05, 0.4, 0.9, 0.9)


def coefficients(shift):
    return 3.4445 - 4.775 * shift + 2.0315 * shift * shift, -4.775 + 2.0 * 2.0315 * shift, 2.0315


def on_diagonal(value):
    rows = lax.broadcasted_iota(jnp.int32, (256, 256), 0)
    columns = lax.broadcasted_iota(jnp.int32, (256, 256), 1)
    return jnp.where(rows == columns, value, 0.0)


def newton_schulz(current, shift):
    constant, linear, square = coefficients(shift)
    rows = rounded(current)
    excess = times_transpose(rows, rows)
    if shift:
        excess = excess - on_diagonal(shift)
    short = rounded(excess)
    poly = rounded(linear * excess + square * product(short, short))
    return constant * current + product(poly, rows), (rows, short, poly)


def newton_schulz_back(grad, rows, short, poly, shift):
    constant, linear, square = coefficients(shift)
    grad_rows = rounded(grad)
    outer = times_transpose(grad_rows, rows)
    outer = outer + outer.T
    inner = product(rounded(outer), short)
    inner = rounded(linear * outer + square * (inner + inner.T))
    return constant * grad + (product(poly, grad_rows) + product(inner, rows))


def norm_of(matrix):
    return jnp.sqrt(jnp.sum(matrix * matrix))


def two_matrices(core, half_ref, other_ref, middle):
    middle[pl.ds(pl.multiple_of(core * 128, 128), 128), :] = half_ref[pl.ds(pl.multiple_of((1 - core) * 256, 256), 128), :]
    middle[pl.ds(pl.multiple_of((1 - core) * 128, 128), 128), :] = other_ref[...]
    own = half_ref[pl.ds(pl.multiple_of(core * 128, 128), 256), :]
    return [own.astype(F32), middle[...].astype(F32)]


def ortho_kernel(core_ref, half_ref, other_ref, fast_own_ref, fast_up_ref, own_ref, up_ref, x_ref, a_ref, p_ref, middle):
    current = []
    for matrix in two_matrices(core_ref[0], half_ref, other_ref, middle):
        current.append(matrix * (1.0 / (norm_of(matrix) + 1e-07)))
    for sweep in range(NS_STEPS):
        for index in range(2):
            current[index], kept = newton_schulz(current[index], SHIFTS[sweep])
            for ref, value in zip((x_ref, a_ref, p_ref), kept):
                ref[sweep, index] = value
    own_ref[...] = rounded(fast_own_ref[...] + current[0])
    up_ref[...] = rounded(fast_up_ref[...] + current[1])


IN_VMEM = pl.BlockSpec(memory_space=pltpu.VMEM)


def ortho(core, half, other, fast_own, fast_up):
    return pl.pallas_call(
        ortho_kernel,
        in_specs=[SCALAR] + [IN_VMEM] * 4,
        out_specs=[IN_VMEM] * 5,
        out_shape=[shape((256, 512), BF16)] * 2 + [shape((NS_STEPS, 2, 256, columns), BF16) for columns in (512, 256, 256)],
        scratch_shapes=[pltpu.VMEM((256, 512), BF16)],
        compiler_params=params(),
        cost_estimate=cost(1700000000, 6000000),
        name="ortho",
    )(core, half, other, fast_own, fast_up)


def ortho_back_kernel(core_ref, th_ref, to_ref, half_ref, other_ref, x_ref, a_ref, p_ref, own_ref, up_ref, middle):
    grads = two_matrices(core_ref[0], half_ref, other_ref, middle)
    for sweep in reversed(range(NS_STEPS)):
        for index in range(2):
            kept = [ref[sweep, index] for ref in (x_ref, a_ref, p_ref)]
            grads[index] = newton_schulz_back(grads[index], *kept, SHIFTS[sweep])
    totals = two_matrices(core_ref[0], th_ref, to_ref, middle)
    for matrix, grad, out_ref in zip(totals, grads, (own_ref, up_ref)):
        norm = norm_of(matrix)
        scale = 1.0 / (norm + 1e-07)
        dot = jnp.sum(grad * matrix)
        out_ref[...] = rounded(grad * scale - matrix * (dot * scale * scale / norm))


def ortho_back(core, totals, adjoint, trail):
    return pl.pallas_call(
        ortho_back_kernel,
        in_specs=[SCALAR] + [IN_VMEM] * 7,
        out_specs=[IN_VMEM] * 2,
        out_shape=[shape((256, 512), BF16)] * 2,
        scratch_shapes=[pltpu.VMEM((256, 512), BF16)],
        compiler_params=params(),
        cost_estimate=cost(2700000000, 6000000),
        name="ortho_back",
    )(core, *totals, *adjoint, *trail)


def finish_kernel(core_ref, half_ref, other_ref, gi_ref, gu_ref, go_ref, scratch):
    core = core_ref[0]
    scratch[pl.ds(pl.multiple_of(core * 384, 384), 384), :] = half_ref[...]
    scratch[pl.ds(pl.multiple_of((1 - core) * 384, 384), 384), :] = other_ref[...]
    gi_ref[...] = scratch[:256, :].astype(F32)
    gu_ref[...] = scratch[256:512, :].astype(F32)
    go_ref[...] = scratch[512:, :].astype(F32).T


def finish(core, half, other):
    return pl.pallas_call(
        finish_kernel,
        in_specs=[SCALAR] + [IN_VMEM] * 2,
        out_specs=[IN_VMEM] * 3,
        out_shape=[shape((256, 512), F32)] * 2 + [shape((512, 256), F32)],
        scratch_shapes=[pltpu.VMEM((768, 512), BF16)],
        compiler_params=params(),
        cost_estimate=cost(1000000, 3000000),
        name="finish",
    )(core, half, other)


def ring_pairs(first, offset):
    pairs = []
    for index in range(32):
        z, x, core = index // 8, (index // 2) % 4, index % 2
        if (core == 0) == first:
            x = (x + offset) % 4
        else:
            z = (z + offset) % 4
        pairs.append((index, z * 8 + x * 2 + core))
    return pairs


def swap_cores(value):
    return lax.ppermute(value, "seq", [(index, index ^ 1) for index in range(32)])


def places():
    me = lax.axis_index("seq")
    z, x, core = me // 8, (me // 2) % 4, me % 2
    return core, jnp.where(core == 0, x, z), jnp.where(core == 0, z, x)


def pick(which, parts):
    return lax.select_n(which, *parts)


def part_at(parts, which):
    return lax.dynamic_index_in_dim(parts, which % 4, 0, keepdims=False)


def scatter_four(parts, place, first):
    received = [
        lax.ppermute(rounded(part_at(parts, place + offset)), "seq", ring_pairs(first, offset)) for offset in (1, 2, 3)
    ]
    total = part_at(parts, place)
    for block in received:
        total = total + block.astype(jnp.float32)
    return total


def exchange_four(block, first):
    return [block] + [lax.ppermute(block, "seq", ring_pairs(first, offset)) for offset in (1, 2, 3)]


def sum_four(blocks):
    a, b, c, d = [block.astype(jnp.float32) for block in blocks]
    return (a + c) + (b + d)


def in_places(blocks, place):
    return jnp.concatenate([pick((place - j) % 4, blocks) for j in range(4)], axis=0)


def middle_half(half, core):
    return swap_cores(jnp.where(core == 0, half[256:], half[:128]))


def together(*values):
    return lax.optimization_barrier(values)


def body(
    inputs,
    token_rates,
    proj_query,
    proj_key,
    proj_value,
    proj_output,
    fast_in,
    fast_up,
    fast_out,
    cotangent,
):
    core_at, place, second = places()
    core = core_at.reshape(1)
    rates = token_rates.reshape(1, -1)

    query_rows, key_rows, value_rows, scaled, kept, sent = update_rows(
        core, inputs, rates, proj_query, proj_key, proj_value, fast_in, fast_up, fast_out
    )
    fast_own = jnp.where(core_at == 0, fast_in, together(sent, fast_out)[1].T)
    received, fast_own = together(swap_cores(sent), fast_own)
    quarter = scatter_four((kept + received.astype(F32)).reshape(4, 96, 512), place, True)
    shared = sum_four(exchange_four(rounded(quarter), False))
    back_output = projected(project_back_kernel, together(shared, cotangent)[1], proj_output, "back_output")
    blocks, back_output = together(exchange_four(rounded(shared), True), back_output)
    half = in_places(blocks, place)
    totals = half, middle_half(half, core_at)
    n_own, n_up, *trail = ortho(core, *totals, fast_own, fast_up)
    n_other = swap_cores(n_own)

    back_p, back_r, hidden_q, kept, sent = query_rows_back(core, query_rows, back_output, n_own, n_other, n_up)
    half = (kept + swap_cores(sent).astype(F32)).reshape(4, 96, 512)
    half, hidden_q, back_p, back_r = together(half, hidden_q, back_p, back_r)
    out_kept, out_sent = out_grads(core, hidden_q, n_own, n_other, cotangent)
    quarter, out_kept, out_sent, back_p, back_r = together(scatter_four(half, place, True), out_kept, out_sent, back_p, back_r)
    query_grad, query_kept, query_sent = query_grads(core, back_p, back_r, n_own, n_other, n_up, inputs)
    blocks, query_grad, query_kept, query_sent = together(
        exchange_four(rounded(quarter), False), query_grad, query_kept, query_sent
    )
    adjoint_share = sum_four(blocks)
    blocks = exchange_four(rounded(adjoint_share), True)
    early_sent = jnp.concatenate([query_sent, out_sent], axis=1)
    half = in_places(blocks, place)
    b_own, b_up = ortho_back(core, totals, (half, middle_half(half, core_at)), trail)
    b_other = swap_cores(b_own)
    early = jnp.concatenate([query_kept, out_kept], axis=1) + swap_cores(early_sent).astype(F32)

    key_grad, value_grad, back_rate, kept, sent = update_back(
        core, inputs, key_rows, value_rows, scaled, rates, fast_in, fast_up, fast_out, b_own, b_other, b_up
    )
    half = jnp.concatenate([kept + swap_cores(sent).astype(F32), early], axis=1)
    half, key_grad, value_grad = together(half, key_grad, value_grad)
    back_inputs = input_back(query_grad, key_grad, value_grad, proj_query, proj_key, proj_value)
    quarter, back_inputs = together(scatter_four(half, place, True), back_inputs)
    contrib = rounded(quarter[:192])
    shares = quarter[192:].reshape(4, 4, 24, 256)

    def shares_of(which):
        return lax.dynamic_index_in_dim(shares, which % 4, 1, keepdims=False).reshape(96, 256)

    received = [
        lax.ppermute(
            jnp.concatenate([contrib, rounded(shares_of(second + offset))], axis=0), "seq", ring_pairs(False, offset)
        )
        for offset in (1, 2, 3)
    ]
    summed = sum_four([contrib] + [block[:192] for block in received])
    mine = shares_of(second)
    for block in received:
        mine = mine + block[192:].astype(F32)
    grad_key, grad_value, grad_query, grad_output = [mine[24 * index : 24 * index + 24] for index in range(4)]
    share = adjoint_share + jnp.concatenate([summed[:96], summed[96:]], axis=1)
    blocks = exchange_four(rounded(share), True)
    half = in_places(blocks, place)
    grad_in, grad_up, grad_out = finish(core, half, swap_cores(half))
    return (
        back_inputs,
        back_rate.reshape(-1),
        grad_in,
        grad_up,
        grad_out,
        grad_query,
        grad_key,
        grad_value,
        grad_output.T,
    )


def solution(mesh):
    in_specs = (
        P(("batch", "seq"), None),
        P(("batch", "seq")),
        P(),
        P(),
        P(),
        P(),
        P(),
        P(),
        P(),
        P(("batch", "seq"), None),
    )
    out_specs = (
        P(("batch", "seq"), None),
        P(("batch", "seq")),
        P("batch", None),
        P("batch", None),
        P("batch", None),
        P("seq", "batch"),
        P("seq", "batch"),
        P("seq", "batch"),
        P("batch", "seq"),
    )
    return jax.shard_map(body, mesh=mesh, in_specs=in_specs, out_specs=out_specs, check_vma=False)
```

```python
import jax
import jax.numpy as jnp
from jax import lax
from jax.experimental import pallas as pl
from jax.experimental.pallas import tpu as pltpu
from jax.sharding import PartitionSpec as P

NS_STEPS = 5
TILE = 512
LARGE = 1024
F32 = jnp.float32
BF16 = jnp.bfloat16
VMEM_BYTES = 28 * 1024 * 1024


def rounded(value):
    return value.astype(jnp.bfloat16)


def product(left, right):
    return jnp.dot(left, right, preferred_element_type=jnp.float32)


def token_sum(left, right):
    return lax.dot_general(
        left, right, (((0,), (0,)), ((), ())), preferred_element_type=jnp.float32
    )


def times_transpose(left, right):
    return lax.dot_general(
        left, right, (((1,), (1,)), ((), ())), preferred_element_type=jnp.float32
    )


def sigmoid(value):
    return 1.0 / (1.0 + jnp.exp(-value))


def column(row):
    wide = jnp.broadcast_to(row, (128, row.shape[1])).T
    return jnp.concatenate([wide, wide], axis=1)


def rows_of(columns, tile=TILE):
    return pl.BlockSpec((tile, columns), lambda step: (step, 0))


def row_block(tile):
    return pl.BlockSpec((1, tile), lambda step: (0, step))


def whole(*shape):
    return pl.BlockSpec(shape, lambda step: (0,) * len(shape))


SCALAR = pl.BlockSpec(memory_space=pltpu.SMEM)
IN_VMEM = pl.BlockSpec(memory_space=pltpu.VMEM)


def params(limit=VMEM_BYTES):
    return pltpu.CompilerParams(vmem_limit_bytes=limit)


def cost(flops, moved):
    return pl.CostEstimate(flops=flops, bytes_accessed=moved, transcendentals=0)


def shape(dims, kind):
    return jax.ShapeDtypeStruct(dims, kind)


def add_sums(sums, parts):
    for index, part in enumerate(parts):
        rows = pl.ds(256 * index, 256)
        sums[rows, :] = sums[rows, :] + part


def put_sums(sums, parts):
    for index, part in enumerate(parts):
        sums[256 * index : 256 * index + 256, :] = part


def hand_halves(core_ref, sums, kept_ref, sent_ref):
    core = core_ref[0]
    kept_ref[...] = sums[pl.ds(pl.multiple_of(core * 384, 384), 384), :]
    sent_ref[...] = rounded(sums[pl.ds(pl.multiple_of((1 - core) * 384, 384), 384), :])


def first_step(action):
    pl.when(pl.program_id(0) == 0)(action)


def last_step(action):
    pl.when(pl.program_id(0) == pl.num_programs(0) - 1)(action)


def in_order(core_ref, own_ref, other_ref, pair):
    core = core_ref[0]
    pair[pl.ds(pl.multiple_of(core * 256, 256), 256), :] = own_ref[...]
    pair[pl.ds(pl.multiple_of((1 - core) * 256, 256), 256), :] = other_ref[...]


def share_rows(core, total, kept_ref, sent_ref, start):
    for a in range(4):
        for b in (0, 2):
            low = [pl.multiple_of(jnp.where(core == 0, (c * 4 + a) * 48, (a * 4 + c) * 48 + 24), 8) for c in (b, b + 1)]
            high = [pl.multiple_of(jnp.where(core == 0, (a * 4 + c) * 48 + 24, (c * 4 + a) * 48), 8) for c in (b, b + 1)]
            at = start + 24 * b
            kept_ref[a, at : at + 48, :] = jnp.concatenate([total[pl.ds(row, 24), :] for row in low], axis=0)
            sent_ref[a, at : at + 48, :] = rounded(jnp.concatenate([total[pl.ds(row, 24), :] for row in high], axis=0))


def update_kernel(core_ref, x_ref, rate_ref, pq_ref, pk_ref, pv_ref, fi_ref, fu_ref, fo_ref, q_ref, k_ref, v_ref, s_ref, kept_ref, sent_ref, sums, wi_ref, wu_ref, wo_ref):
    @first_step
    def _():
        sums[...] = jnp.zeros_like(sums)
        wi_ref[...] = rounded(fi_ref[...])
        wu_ref[...] = rounded(fu_ref[...])
        wo_ref[...] = rounded(fo_ref[...])

    x = x_ref[...]
    key_rows = rounded(product(x, pk_ref[...]))
    value_rows = rounded(product(x, pv_ref[...]))
    scaled = rounded(column(rate_ref[...]) * value_rows.astype(F32))
    q_ref[...] = rounded(product(x, pq_ref[...]))
    k_ref[...] = key_rows
    v_ref[...] = value_rows
    s_ref[...] = scaled
    pre_in = product(key_rows, wi_ref[...])
    pre_up = product(key_rows, wu_ref[...])
    upstream = times_transpose(scaled, wo_ref[...])
    sigma = sigmoid(pre_in)
    activation = pre_in * sigma
    slope = sigma * (1.0 + pre_in * (1.0 - sigma))
    hidden = rounded(activation * pre_up)
    grad_in_rows = rounded(upstream * pre_up * slope)
    grad_up_rows = rounded(upstream * activation)
    both = token_sum(key_rows, jnp.concatenate([grad_in_rows, grad_up_rows], axis=1))
    add_sums(sums, (both[:, :512], both[:, 512:], token_sum(scaled, hidden)))
    last_step(lambda: hand_halves(core_ref, sums, kept_ref, sent_ref))


WEIGHTS = [((256, 512), BF16), ((256, 512), BF16), ((512, 256), BF16)]


def update_rows(core, inputs, rates, proj_query, proj_key, proj_value, fast_in, fast_up, fast_out):
    tokens = inputs.shape[0]
    return pl.pallas_call(
        update_kernel,
        grid=(tokens // LARGE,),
        in_specs=[SCALAR, rows_of(768, LARGE), row_block(LARGE)] + [whole(768, 256)] * 3 + [ whole(256, 512), whole(256, 512), whole(512, 256)],
        out_specs=[rows_of(256, LARGE)] * 4 + [whole(384, 512)] * 2,
        out_shape=[shape((tokens, 256), BF16)] * 4 + [shape((384, 512), F32), shape((384, 512), BF16)],
        scratch_shapes=[pltpu.VMEM((768, 512), F32)] + [pltpu.VMEM(*w) for w in WEIGHTS],
        compiler_params=params(60 * 1024 * 1024),
        cost_estimate=cost(2400000000, 6000000),
        name="update_rows",
    )(core, inputs, rates, proj_query, proj_key, proj_value, fast_in, fast_up, fast_out)


def back_output_kernel(core_ref, c_ref, po_ref, fi_ref, fo_ref, out_ref, own_ref):
    core = core_ref[0]

    @first_step
    def _():
        own_ref[...] = jnp.where(core == 0, fi_ref[...], fo_ref[...].T)

    out_ref[...] = rounded(times_transpose(c_ref[...], po_ref[...]))


def back_output_rows(core, cotangent, proj_output, fast_in, fast_out):
    tokens = cotangent.shape[0]
    return pl.pallas_call(
        back_output_kernel,
        grid=(tokens // TILE,),
        in_specs=[SCALAR, rows_of(768), whole(256, 768), whole(256, 512), whole(512, 256)],
        out_specs=[rows_of(256), whole(256, 512)],
        out_shape=[shape((tokens, 256), BF16), shape((256, 512), F32)],
        compiler_params=params(),
        cost_estimate=cost(400000000, 4000000),
        name="back_output",
    )(core, cotangent, proj_output, fast_in, fast_out)


def query_kernel(core_ref, q_ref, bo_ref, own_ref, other_ref, nu_ref, bp_ref, br_ref, h_ref, kept_ref, sent_ref, sums, pair):
    in_order(core_ref, own_ref, other_ref, pair)
    query_rows, back_output = q_ref[...], bo_ref[...]
    pre_p = product(query_rows, pair[:256, :])
    pre_r = product(query_rows, nu_ref[...])
    back_hidden = product(back_output, pair[256:, :])
    sigma = sigmoid(pre_p)
    activation = pre_p * sigma
    slope = sigma * (1.0 + pre_p * (1.0 - sigma))
    hidden = rounded(activation * pre_r)
    back_p = rounded(back_hidden * pre_r * slope)
    back_r = rounded(back_hidden * activation)
    bp_ref[...] = back_p
    br_ref[...] = back_r
    h_ref[...] = hidden
    both = token_sum(query_rows, jnp.concatenate([back_p, back_r], axis=1))
    put_sums(sums, (both[:, :512], both[:, 512:], token_sum(back_output, hidden)))
    hand_halves(core_ref, sums, kept_ref, sent_ref)


def query_rows_back(core, query_rows, back_output, n_own, n_other, n_up):
    tokens = query_rows.shape[0]
    return pl.pallas_call(
        query_kernel,
        in_specs=[SCALAR] + [IN_VMEM] * 5,
        out_specs=[IN_VMEM] * 5,
        out_shape=[shape((tokens, 512), BF16)] * 3 + [shape((384, 512), F32), shape((384, 512), BF16)],
        scratch_shapes=[pltpu.VMEM((768, 512), F32), pltpu.VMEM((512, 512), BF16)],
        compiler_params=params(),
        cost_estimate=cost(1600000000, 6000000),
        name="query_rows_back",
    )(core, query_rows, back_output, n_own, n_other, n_up)


def out_grad_kernel(core_ref, h_ref, own_ref, other_ref, c_ref, kept_ref, sent_ref, go, pair):
    @first_step
    def _():
        in_order(core_ref, own_ref, other_ref, pair)
        go[...] = jnp.zeros_like(go)

    output_rows = rounded(times_transpose(h_ref[...], pair[256:, :]))
    go[...] += token_sum(c_ref[...], output_rows)

    @last_step
    def _():
        share_rows(core_ref[0], go, kept_ref, sent_ref, 0)


SHARES = [shape((4, 96, 256), F32), shape((4, 96, 256), BF16)]


def out_grads(core, hidden, n_own, n_other, cotangent):
    tokens = cotangent.shape[0]
    return pl.pallas_call(
        out_grad_kernel,
        grid=(tokens // TILE,),
        in_specs=[SCALAR, rows_of(512), whole(256, 512), whole(256, 512), rows_of(768)],
        out_specs=[whole(4, 96, 256)] * 2,
        out_shape=SHARES,
        scratch_shapes=[pltpu.VMEM((768, 256), F32), pltpu.VMEM((512, 512), BF16)],
        compiler_params=params(),
        cost_estimate=cost(700000000, 4000000),
        name="out_grads",
    )(core, hidden, n_own, n_other, cotangent)


def query_grad_kernel(core_ref, bp_ref, br_ref, own_ref, other_ref, nu_ref, x_ref, qg_ref, kept_ref, sent_ref, gq, pair):
    @first_step
    def _():
        in_order(core_ref, own_ref, other_ref, pair)
        gq[...] = jnp.zeros_like(gq)

    query_grad = rounded(times_transpose(bp_ref[...], pair[:256, :]) + times_transpose(br_ref[...], nu_ref[...]))
    qg_ref[...] = query_grad
    gq[...] += token_sum(x_ref[...], query_grad)

    @last_step
    def _():
        share_rows(core_ref[0], gq, kept_ref, sent_ref, 0)


def query_grads(core, back_p, back_r, n_own, n_other, n_up, inputs):
    tokens = inputs.shape[0]
    return pl.pallas_call(
        query_grad_kernel,
        grid=(tokens // TILE,),
        in_specs=[SCALAR] + [rows_of(512)] * 2 + [whole(256, 512)] * 3 + [rows_of(768)],
        out_specs=[rows_of(256)] + [whole(4, 96, 256)] * 2,
        out_shape=[shape((tokens, 256), BF16)] + SHARES,
        scratch_shapes=[pltpu.VMEM((768, 256), F32), pltpu.VMEM((512, 512), BF16)],
        compiler_params=params(),
        cost_estimate=cost(950000000, 5000000),
        name="query_grads",
    )(core, back_p, back_r, n_own, n_other, n_up, inputs)


def back_kernel(core_ref, x_ref, k_ref, v_ref, s_ref, rate_ref, fi_ref, fu_ref, fo_ref, own_ref, other_ref, bu_ref, kg_ref, vg_ref, rate_out, kept_ref, sent_ref, sums, gk, gv, pair, wi_ref, wu_ref, wo_ref):
    in_order(core_ref, own_ref, other_ref, pair)
    wi_ref[...] = rounded(fi_ref[...])
    wu_ref[...] = rounded(fu_ref[...])
    wo_ref[...] = rounded(fo_ref[...])

    key_rows, scaled = k_ref[...], s_ref[...]
    b_in, b_up, b_out = pair[:256, :], bu_ref[...], pair[256:, :]
    pre_in = product(key_rows, wi_ref[...])
    pre_up = product(key_rows, wu_ref[...])
    upstream = times_transpose(scaled, wo_ref[...])
    press_in = product(key_rows, b_in)
    press_up = product(key_rows, b_up)
    back_hid = product(scaled, b_out)
    sigma = sigmoid(pre_in)
    activation = pre_in * sigma
    fall = 1.0 - sigma
    slope = sigma * (1.0 + pre_in * fall)
    curvature = sigma * fall * (2.0 + pre_in * (1.0 - 2.0 * sigma))
    hidden = rounded(activation * pre_up)
    rise = pre_up * slope
    steep = upstream * slope
    grad_in_rows = rounded(upstream * rise)
    grad_up_rows = rounded(upstream * activation)
    back_upstream = rounded(press_in * rise + press_up * activation)
    back_pre_up = rounded(press_in * steep + back_hid * activation)
    back_pre_in = rounded(press_in * upstream * pre_up * curvature + press_up * steep + back_hid * rise)
    both = token_sum(key_rows, jnp.concatenate([back_pre_in, back_pre_up], axis=1))
    put_sums(sums, (both[:, :512], both[:, 512:], token_sum(scaled, back_upstream)))
    back_scaled = times_transpose(hidden, b_out) + product(back_upstream, wo_ref[...])
    scores = jnp.sum(back_scaled * v_ref[...].astype(F32), axis=1, keepdims=True)
    rate_out[...] = jnp.broadcast_to(scores, (rate_ref.shape[1], 128)).T[:1, :]
    value_grad = rounded(column(rate_ref[...]) * back_scaled)
    vg_ref[...] = value_grad
    key_sum = times_transpose(grad_in_rows, b_in) + times_transpose(grad_up_rows, b_up)
    key_sum = key_sum + times_transpose(back_pre_in, wi_ref[...]) + times_transpose(back_pre_up, wu_ref[...])
    key_grad = rounded(key_sum)
    kg_ref[...] = key_grad
    both = token_sum(x_ref[...], jnp.concatenate([key_grad, value_grad], axis=1))
    gk[...] = both[:, :256]
    gv[...] = both[:, 256:]

    core = core_ref[0]
    for a in range(4):
        mine = sums[pl.ds(pl.multiple_of(core * 384 + 96 * a, 96), 96), :]
        theirs = rounded(sums[pl.ds(pl.multiple_of((1 - core) * 384 + 96 * a, 96), 96), :])
        for side in range(2):
            kept_ref[a, 96 * side : 96 * side + 96, :] = mine[:, 256 * side : 256 * side + 256]
            sent_ref[a, 96 * side : 96 * side + 96, :] = theirs[:, 256 * side : 256 * side + 256]
    share_rows(core, gk, kept_ref, sent_ref, 192)
    share_rows(core, gv, kept_ref, sent_ref, 288)


def update_back(core, inputs, key_rows, value_rows, scaled, rates, fast_in, fast_up, fast_out, b_own, b_other, b_up):
    tokens = key_rows.shape[0]
    return pl.pallas_call(
        back_kernel,
        in_specs=[SCALAR] + [IN_VMEM] * 11,
        out_specs=[IN_VMEM] * 5,
        out_shape=[shape((tokens, 256), BF16)] * 2
        + [shape((1, tokens), F32), shape((4, 384, 256), F32), shape((4, 384, 256), BF16)],
        scratch_shapes=[pltpu.VMEM((768, 512), F32), pltpu.VMEM((768, 256), F32), pltpu.VMEM((768, 256), F32), pltpu.VMEM((512, 512), BF16)]
        + [pltpu.VMEM(*w) for w in WEIGHTS],
        compiler_params=params(),
        cost_estimate=cost(5600000000, 10000000),
        name="update_back",
    )(core, inputs, key_rows, value_rows, scaled, rates, fast_in, fast_up, fast_out, b_own, b_other, b_up)


def input_kernel(q_ref, k_ref, v_ref, pq_ref, pk_ref, pv_ref, out_ref):
    total = times_transpose(q_ref[...], pq_ref[...]) + times_transpose(k_ref[...], pk_ref[...])
    out_ref[...] = rounded(total + times_transpose(v_ref[...], pv_ref[...]))


def input_back(query_grad, key_grad, value_grad, proj_query, proj_key, proj_value):
    tokens = query_grad.shape[0]
    return pl.pallas_call(
        input_kernel,
        grid=(tokens // TILE,),
        in_specs=[rows_of(256)] * 3 + [whole(768, 256)] * 3,
        out_specs=rows_of(768),
        out_shape=shape((tokens, 768), BF16),
        compiler_params=params(),
        cost_estimate=cost(1200000000, 4000000),
        name="input_back",
    )(query_grad, key_grad, value_grad, proj_query, proj_key, proj_value)


SHIFTS = (0.0, 0.05, 0.4, 0.9, 0.9)


def coefficients(shift):
    return 3.4445 - 4.775 * shift + 2.0315 * shift * shift, -4.775 + 2.0 * 2.0315 * shift, 2.0315


def on_diagonal(value):
    rows = lax.broadcasted_iota(jnp.int32, (256, 256), 0)
    columns = lax.broadcasted_iota(jnp.int32, (256, 256), 1)
    return jnp.where(rows == columns, value, 0.0)


def newton_schulz(current, shift):
    constant, linear, square = coefficients(shift)
    rows = rounded(current)
    excess = times_transpose(rows, rows)
    if shift:
        excess = excess - on_diagonal(shift)
    short = rounded(excess)
    poly = rounded(linear * excess + square * product(short, short))
    return constant * current + product(poly, rows), (rows, short, poly)


def newton_schulz_back(grad, rows, short, poly, shift):
    constant, linear, square = coefficients(shift)
    grad_rows = rounded(grad)
    outer = times_transpose(grad_rows, rows)
    outer = outer + outer.T
    inner = product(rounded(outer), short)
    inner = rounded(linear * outer + square * (inner + inner.T))
    return constant * grad + (product(poly, grad_rows) + product(inner, rows))


def norm_of(matrix):
    return jnp.sqrt(jnp.sum(matrix * matrix))


def two_matrices(core, half_ref, other_ref, middle):
    middle[pl.ds(pl.multiple_of(core * 128, 128), 128), :] = half_ref[pl.ds(pl.multiple_of((1 - core) * 256, 256), 128), :]
    middle[pl.ds(pl.multiple_of((1 - core) * 128, 128), 128), :] = other_ref[...]
    own = half_ref[pl.ds(pl.multiple_of(core * 128, 128), 256), :]
    return [own.astype(F32), middle[...].astype(F32)]


def ortho_kernel(core_ref, half_ref, other_ref, fast_own_ref, fast_up_ref, own_ref, up_ref, x_ref, a_ref, p_ref, middle):
    current = []
    for matrix in two_matrices(core_ref[0], half_ref, other_ref, middle):
        current.append(matrix * (1.0 / (norm_of(matrix) + 1e-07)))
    for sweep in range(NS_STEPS):
        for index in range(2):
            current[index], kept = newton_schulz(current[index], SHIFTS[sweep])
            for ref, value in zip((x_ref, a_ref, p_ref), kept):
                ref[sweep, index] = value
    own_ref[...] = rounded(fast_own_ref[...] + current[0])
    up_ref[...] = rounded(fast_up_ref[...] + current[1])


def ortho(core, half, other, fast_own, fast_up):
    return pl.pallas_call(
        ortho_kernel,
        in_specs=[SCALAR] + [IN_VMEM] * 4,
        out_specs=[IN_VMEM] * 5,
        out_shape=[shape((256, 512), BF16)] * 2 + [shape((NS_STEPS, 2, 256, columns), BF16) for columns in (512, 256, 256)],
        scratch_shapes=[pltpu.VMEM((256, 512), BF16)],
        compiler_params=params(),
        cost_estimate=cost(1700000000, 6000000),
        name="ortho",
    )(core, half, other, fast_own, fast_up)


def ortho_back_kernel(core_ref, th_ref, to_ref, half_ref, other_ref, x_ref, a_ref, p_ref, own_ref, up_ref, middle):
    grads = two_matrices(core_ref[0], half_ref, other_ref, middle)
    for sweep in reversed(range(NS_STEPS)):
        for index in range(2):
            kept = [ref[sweep, index] for ref in (x_ref, a_ref, p_ref)]
            grads[index] = newton_schulz_back(grads[index], *kept, SHIFTS[sweep])
    totals = two_matrices(core_ref[0], th_ref, to_ref, middle)
    for matrix, grad, out_ref in zip(totals, grads, (own_ref, up_ref)):
        norm = norm_of(matrix)
        scale = 1.0 / (norm + 1e-07)
        dot = jnp.sum(grad * matrix)
        out_ref[...] = rounded(grad * scale - matrix * (dot * scale * scale / norm))


def ortho_back(core, totals, adjoint, trail):
    return pl.pallas_call(
        ortho_back_kernel,
        in_specs=[SCALAR] + [IN_VMEM] * 7,
        out_specs=[IN_VMEM] * 2,
        out_shape=[shape((256, 512), BF16)] * 2,
        scratch_shapes=[pltpu.VMEM((256, 512), BF16)],
        compiler_params=params(),
        cost_estimate=cost(2700000000, 6000000),
        name="ortho_back",
    )(core, *totals, *adjoint, *trail)


def pack_kernel(place_ref, kept_ref, in_ref, one_ref, two_ref, three_ref, mine_ref):
    for offset, out_ref in enumerate((mine_ref, one_ref, two_ref, three_ref)):
        at = lax.rem(place_ref[0] + offset, 4)
        out_ref[...] = (kept_ref[at] + in_ref[at].astype(F32)).astype(out_ref.dtype)


def pack(place, kept, received):
    return pl.pallas_call(
        pack_kernel,
        in_specs=[SCALAR] + [IN_VMEM] * 2,
        out_specs=[IN_VMEM] * 4,
        out_shape=[shape(kept.shape[1:], BF16)] * 3 + [shape(kept.shape[1:], F32)],
        compiler_params=params(),
        cost_estimate=cost(1000000, 2000000),
        name="pack",
    )(place, kept, received)


def pack_both_kernel(place_ref, late_ref, late_in_ref, early_ref, early_in_ref, one_ref, two_ref, three_ref, mine_ref):
    for offset, out_ref in enumerate((mine_ref, one_ref, two_ref, three_ref)):
        at = lax.rem(place_ref[0] + offset, 4)
        out_ref[:384, :] = (late_ref[at] + late_in_ref[at].astype(F32)).astype(out_ref.dtype)
        out_ref[384:, :] = (early_ref[at] + early_in_ref[at].astype(F32)).astype(out_ref.dtype)


def pack_both(place, late, late_in, early, early_in):
    return pl.pallas_call(
        pack_both_kernel,
        in_specs=[SCALAR] + [IN_VMEM] * 4,
        out_specs=[IN_VMEM] * 4,
        out_shape=[shape((576, 256), BF16)] * 3 + [shape((576, 256), F32)],
        compiler_params=params(),
        cost_estimate=cost(1000000, 5000000),
        name="pack_both",
    )(place, late, late_in, early, early_in)


def unpack_kernel(second_ref, mine_ref, a_ref, b_ref, c_ref, one_ref, two_ref, three_ref, contrib_ref, own_ref, total):
    total[...] = mine_ref[...] + a_ref[...].astype(F32) + b_ref[...].astype(F32) + c_ref[...].astype(F32)
    contrib = rounded(total[:192, :])
    contrib_ref[...] = contrib
    for offset, out_ref in enumerate((own_ref, one_ref, two_ref, three_ref)):
        at = lax.rem(second_ref[0] + offset, 4) * 24
        shares = [total[pl.ds(pl.multiple_of(192 + 96 * index + at, 8), 24), :] for index in range(4)]
        if offset:
            out_ref[:192, :] = contrib
            for index in (0, 2):
                out_ref[192 + 24 * index : 240 + 24 * index, :] = rounded(jnp.concatenate(shares[index : index + 2], axis=0))
        else:
            for index in range(4):
                out_ref[24 * index : 24 * index + 24, :] = shares[index]


def unpack(second, mine, blocks):
    return pl.pallas_call(
        unpack_kernel,
        in_specs=[SCALAR] + [IN_VMEM] * 4,
        out_specs=[IN_VMEM] * 5,
        out_shape=[shape((288, 256), BF16)] * 3 + [shape((192, 256), BF16), shape((96, 256), F32)],
        scratch_shapes=[pltpu.VMEM((576, 256), F32)],
        compiler_params=params(),
        cost_estimate=cost(1000000, 2000000),
        name="unpack",
    )(second, mine, *blocks)


def finish_kernel(core_ref, half_ref, other_ref, gi_ref, gu_ref, go_ref, scratch):
    core = core_ref[0]
    scratch[pl.ds(pl.multiple_of(core * 384, 384), 384), :] = half_ref[...]
    scratch[pl.ds(pl.multiple_of((1 - core) * 384, 384), 384), :] = other_ref[...]
    gi_ref[...] = scratch[:256, :].astype(F32)
    gu_ref[...] = scratch[256:512, :].astype(F32)
    go_ref[...] = scratch[512:, :].astype(F32).T


def finish(core, half, other):
    return pl.pallas_call(
        finish_kernel,
        in_specs=[SCALAR] + [IN_VMEM] * 2,
        out_specs=[IN_VMEM] * 3,
        out_shape=[shape((256, 512), F32)] * 2 + [shape((512, 256), F32)],
        scratch_shapes=[pltpu.VMEM((768, 512), BF16)],
        compiler_params=params(),
        cost_estimate=cost(1000000, 3000000),
        name="finish",
    )(core, half, other)


def ring_pairs(first, offset):
    pairs = []
    for index in range(32):
        z, x, core = index // 8, (index // 2) % 4, index % 2
        if (core == 0) == first:
            x = (x + offset) % 4
        else:
            z = (z + offset) % 4
        pairs.append((index, z * 8 + x * 2 + core))
    return pairs


def swap_cores(value):
    return lax.ppermute(value, "seq", [(index, index ^ 1) for index in range(32)])


def places():
    me = lax.axis_index("seq")
    z, x, core = me // 8, (me // 2) % 4, me % 2
    return core, jnp.where(core == 0, x, z), jnp.where(core == 0, z, x)


def pick(which, parts):
    return lax.select_n(which, *parts)


def part_at(parts, which):
    return lax.dynamic_index_in_dim(parts, which % 4, 0, keepdims=False)


def scatter_four(parts, place, first):
    received = [
        lax.ppermute(rounded(part_at(parts, place + offset)), "seq", ring_pairs(first, offset)) for offset in (1, 2, 3)
    ]
    total = part_at(parts, place)
    for block in received:
        total = total + block.astype(jnp.float32)
    return total


def exchange_four(block, first):
    return [block] + [lax.ppermute(block, "seq", ring_pairs(first, offset)) for offset in (1, 2, 3)]


def sum_four(blocks):
    a, b, c, d = [block.astype(jnp.float32) for block in blocks]
    return (a + c) + (b + d)


def in_places(blocks, place):
    return jnp.concatenate([pick((place - j) % 4, blocks) for j in range(4)], axis=0)


def middle_half(half, core):
    return swap_cores(jnp.where(core == 0, half[256:], half[:128]))


def together(*values):
    return lax.optimization_barrier(values)


def body(
    inputs,
    token_rates,
    proj_query,
    proj_key,
    proj_value,
    proj_output,
    fast_in,
    fast_up,
    fast_out,
    cotangent,
):
    core_at, place, second = places()
    core = core_at.reshape(1)
    rates = token_rates.reshape(1, -1)

    query_rows, key_rows, value_rows, scaled, kept, sent = update_rows(
        core, inputs, rates, proj_query, proj_key, proj_value, fast_in, fast_up, fast_out
    )
    quarter = scatter_four((kept + swap_cores(sent).astype(F32)).reshape(4, 96, 512), place, True)
    shared = sum_four(exchange_four(rounded(quarter), False))
    back_output, fast_own = back_output_rows(core, together(shared, cotangent)[1], proj_output, fast_in, fast_out)
    blocks, back_output, fast_own = together(exchange_four(rounded(shared), True), back_output, fast_own)
    half = in_places(blocks, place)
    totals = half, middle_half(half, core_at)
    n_own, n_up, *trail = ortho(core, *totals, fast_own, fast_up)
    n_other = swap_cores(n_own)

    back_p, back_r, hidden_q, kept, sent = query_rows_back(core, query_rows, back_output, n_own, n_other, n_up)
    half = (kept + swap_cores(sent).astype(F32)).reshape(4, 96, 512)
    half, hidden_q, back_p, back_r = together(half, hidden_q, back_p, back_r)
    out_kept, out_sent = out_grads(core, hidden_q, n_own, n_other, cotangent)
    quarter, out_kept, out_sent, back_p, back_r = together(scatter_four(half, place, True), out_kept, out_sent, back_p, back_r)
    query_grad, query_kept, query_sent = query_grads(core, back_p, back_r, n_own, n_other, n_up, inputs)
    blocks, query_grad, query_kept, query_sent = together(
        exchange_four(rounded(quarter), False), query_grad, query_kept, query_sent
    )
    adjoint_share = sum_four(blocks)
    blocks = exchange_four(rounded(adjoint_share), True)
    early_sent = jnp.concatenate([query_sent, out_sent], axis=1)
    half = in_places(blocks, place)
    b_own, b_up = ortho_back(core, totals, (half, middle_half(half, core_at)), trail)
    b_other = swap_cores(b_own)
    early = jnp.concatenate([query_kept, out_kept], axis=1)
    early_in = swap_cores(early_sent)

    key_grad, value_grad, back_rate, kept, sent = update_back(
        core, inputs, key_rows, value_rows, scaled, rates, fast_in, fast_up, fast_out, b_own, b_other, b_up
    )
    back_inputs = input_back(query_grad, key_grad, value_grad, proj_query, proj_key, proj_value)
    *blocks, mine = pack_both(place.reshape(1), kept, swap_cores(sent), early, early_in)
    blocks = [lax.ppermute(block, "seq", ring_pairs(True, offset + 1)) for offset, block in enumerate(blocks)]
    *blocks, contrib, mine = unpack(second.reshape(1), mine, blocks)
    received = [lax.ppermute(block, "seq", ring_pairs(False, offset + 1)) for offset, block in enumerate(blocks)]
    summed = sum_four([contrib] + [block[:192] for block in received])
    for block in received:
        mine = mine + block[192:].astype(F32)
    grad_key, grad_value, grad_query, grad_output = [mine[24 * index : 24 * index + 24] for index in range(4)]
    share = adjoint_share + jnp.concatenate([summed[:96], summed[96:]], axis=1)
    blocks = exchange_four(rounded(share), True)
    half = in_places(blocks, place)
    grad_in, grad_up, grad_out = finish(core, half, swap_cores(half))
    return (
        back_inputs,
        back_rate.reshape(-1),
        grad_in,
        grad_up,
        grad_out,
        grad_query,
        grad_key,
        grad_value,
        grad_output.T,
    )


def solution(mesh):
    in_specs = (
        P(("batch", "seq"), None),
        P(("batch", "seq")),
        P(),
        P(),
        P(),
        P(),
        P(),
        P(),
        P(),
        P(("batch", "seq"), None),
    )
    out_specs = (
        P(("batch", "seq"), None),
        P(("batch", "seq")),
        P("batch", None),
        P("batch", None),
        P("batch", None),
        P("seq", "batch"),
        P("seq", "batch"),
        P("seq", "batch"),
        P("batch", "seq"),
    )
    return jax.shard_map(body, mesh=mesh, in_specs=in_specs, out_specs=out_specs, check_vma=False)
```

```python
import jax
import jax.numpy as jnp
from jax import lax
from jax.experimental import pallas as pl
from jax.experimental.pallas import tpu as pltpu
from jax.sharding import PartitionSpec as P

NS_STEPS = 5
TILE = 512
LARGE = 1024
F32 = jnp.float32
BF16 = jnp.bfloat16
VMEM_BYTES = 28 * 1024 * 1024


def rounded(value):
    return value.astype(jnp.bfloat16)


def product(left, right):
    return jnp.dot(left, right, preferred_element_type=jnp.float32)


def token_sum(left, right):
    return lax.dot_general(
        left, right, (((0,), (0,)), ((), ())), preferred_element_type=jnp.float32
    )


def times_transpose(left, right):
    return lax.dot_general(
        left, right, (((1,), (1,)), ((), ())), preferred_element_type=jnp.float32
    )


def sigmoid(value):
    return 1.0 / (1.0 + jnp.exp(-value))


def column(row):
    wide = jnp.broadcast_to(row, (128, row.shape[1])).T
    return jnp.concatenate([wide, wide], axis=1)


def rows_of(columns, tile=TILE):
    return pl.BlockSpec((tile, columns), lambda step: (step, 0))


def row_block(tile):
    return pl.BlockSpec((1, tile), lambda step: (0, step))


def whole(*shape):
    return pl.BlockSpec(shape, lambda step: (0,) * len(shape))


SCALAR = pl.BlockSpec(memory_space=pltpu.SMEM)
IN_VMEM = pl.BlockSpec(memory_space=pltpu.VMEM)


def params(limit=VMEM_BYTES):
    return pltpu.CompilerParams(vmem_limit_bytes=limit)


def cost(flops, moved):
    return pl.CostEstimate(flops=flops, bytes_accessed=moved, transcendentals=0)


def shape(dims, kind):
    return jax.ShapeDtypeStruct(dims, kind)


def add_sums(sums, parts):
    for index, part in enumerate(parts):
        rows = pl.ds(256 * index, 256)
        sums[rows, :] = sums[rows, :] + part


def put_sums(sums, parts):
    for index, part in enumerate(parts):
        sums[256 * index : 256 * index + 256, :] = part


def hand_halves(core_ref, sums, kept_ref, sent_ref):
    core = core_ref[0]
    kept_ref[...] = sums[pl.ds(pl.multiple_of(core * 384, 384), 384), :]
    sent_ref[...] = rounded(sums[pl.ds(pl.multiple_of((1 - core) * 384, 384), 384), :])


def first_step(action):
    pl.when(pl.program_id(0) == 0)(action)


def last_step(action):
    pl.when(pl.program_id(0) == pl.num_programs(0) - 1)(action)


def in_order(core_ref, own_ref, other_ref, pair):
    core = core_ref[0]
    pair[pl.ds(pl.multiple_of(core * 256, 256), 256), :] = own_ref[...]
    pair[pl.ds(pl.multiple_of((1 - core) * 256, 256), 256), :] = other_ref[...]


def share_rows(core, total, kept_ref, sent_ref, start):
    for a in range(4):
        for b in (0, 2):
            low = [pl.multiple_of(jnp.where(core == 0, (c * 4 + a) * 48, (a * 4 + c) * 48 + 24), 8) for c in (b, b + 1)]
            high = [pl.multiple_of(jnp.where(core == 0, (a * 4 + c) * 48 + 24, (c * 4 + a) * 48), 8) for c in (b, b + 1)]
            at = start + 24 * b
            kept_ref[a, at : at + 48, :] = jnp.concatenate([total[pl.ds(row, 24), :] for row in low], axis=0)
            sent_ref[a, at : at + 48, :] = rounded(jnp.concatenate([total[pl.ds(row, 24), :] for row in high], axis=0))


def update_kernel(core_ref, x_ref, rate_ref, pq_ref, pk_ref, pv_ref, fi_ref, fu_ref, fo_ref, q_ref, k_ref, v_ref, s_ref, kept_ref, sent_ref, sums, wi_ref, wu_ref, wo_ref):
    @first_step
    def _():
        sums[...] = jnp.zeros_like(sums)
        wi_ref[...] = rounded(fi_ref[...])
        wu_ref[...] = rounded(fu_ref[...])
        wo_ref[...] = rounded(fo_ref[...])

    x = x_ref[...]
    key_rows = rounded(product(x, pk_ref[...]))
    value_rows = rounded(product(x, pv_ref[...]))
    scaled = rounded(column(rate_ref[...]) * value_rows.astype(F32))
    q_ref[...] = rounded(product(x, pq_ref[...]))
    k_ref[...] = key_rows
    v_ref[...] = value_rows
    s_ref[...] = scaled
    pre_in = product(key_rows, wi_ref[...])
    pre_up = product(key_rows, wu_ref[...])
    upstream = times_transpose(scaled, wo_ref[...])
    sigma = sigmoid(pre_in)
    activation = pre_in * sigma
    slope = sigma * (1.0 + pre_in * (1.0 - sigma))
    hidden = rounded(activation * pre_up)
    grad_in_rows = rounded(upstream * pre_up * slope)
    grad_up_rows = rounded(upstream * activation)
    both = token_sum(key_rows, jnp.concatenate([grad_in_rows, grad_up_rows], axis=1))
    add_sums(sums, (both[:, :512], both[:, 512:], token_sum(scaled, hidden)))
    last_step(lambda: hand_halves(core_ref, sums, kept_ref, sent_ref))


WEIGHTS = [((256, 512), BF16), ((256, 512), BF16), ((512, 256), BF16)]


def update_rows(core, inputs, rates, proj_query, proj_key, proj_value, fast_in, fast_up, fast_out):
    tokens = inputs.shape[0]
    return pl.pallas_call(
        update_kernel,
        grid=(tokens // LARGE,),
        in_specs=[SCALAR, rows_of(768, LARGE), row_block(LARGE)] + [whole(768, 256)] * 3 + [ whole(256, 512), whole(256, 512), whole(512, 256)],
        out_specs=[rows_of(256, LARGE)] * 4 + [whole(384, 512)] * 2,
        out_shape=[shape((tokens, 256), BF16)] * 4 + [shape((384, 512), F32), shape((384, 512), BF16)],
        scratch_shapes=[pltpu.VMEM((768, 512), F32)] + [pltpu.VMEM(*w) for w in WEIGHTS],
        compiler_params=params(60 * 1024 * 1024),
        cost_estimate=cost(2400000000, 6000000),
        name="update_rows",
    )(core, inputs, rates, proj_query, proj_key, proj_value, fast_in, fast_up, fast_out)


def back_output_kernel(core_ref, c_ref, po_ref, fi_ref, fo_ref, out_ref, own_ref):
    core = core_ref[0]

    @first_step
    def _():
        own_ref[...] = jnp.where(core == 0, fi_ref[...], fo_ref[...].T)

    out_ref[...] = rounded(times_transpose(c_ref[...], po_ref[...]))


def back_output_rows(core, cotangent, proj_output, fast_in, fast_out):
    tokens = cotangent.shape[0]
    return pl.pallas_call(
        back_output_kernel,
        grid=(tokens // TILE,),
        in_specs=[SCALAR, rows_of(768), whole(256, 768), whole(256, 512), whole(512, 256)],
        out_specs=[rows_of(256), whole(256, 512)],
        out_shape=[shape((tokens, 256), BF16), shape((256, 512), F32)],
        compiler_params=params(),
        cost_estimate=cost(400000000, 4000000),
        name="back_output",
    )(core, cotangent, proj_output, fast_in, fast_out)


def query_kernel(core_ref, q_ref, bo_ref, own_ref, other_ref, nu_ref, bp_ref, br_ref, h_ref, kept_ref, sent_ref, sums, pair):
    in_order(core_ref, own_ref, other_ref, pair)
    query_rows, back_output = q_ref[...], bo_ref[...]
    pre_p = product(query_rows, pair[:256, :])
    pre_r = product(query_rows, nu_ref[...])
    back_hidden = product(back_output, pair[256:, :])
    sigma = sigmoid(pre_p)
    activation = pre_p * sigma
    slope = sigma * (1.0 + pre_p * (1.0 - sigma))
    hidden = rounded(activation * pre_r)
    back_p = rounded(back_hidden * pre_r * slope)
    back_r = rounded(back_hidden * activation)
    bp_ref[...] = back_p
    br_ref[...] = back_r
    h_ref[...] = hidden
    both = token_sum(query_rows, jnp.concatenate([back_p, back_r], axis=1))
    put_sums(sums, (both[:, :512], both[:, 512:], token_sum(back_output, hidden)))
    hand_halves(core_ref, sums, kept_ref, sent_ref)


def query_rows_back(core, query_rows, back_output, n_own, n_other, n_up):
    tokens = query_rows.shape[0]
    return pl.pallas_call(
        query_kernel,
        in_specs=[SCALAR] + [IN_VMEM] * 5,
        out_specs=[IN_VMEM] * 5,
        out_shape=[shape((tokens, 512), BF16)] * 3 + [shape((384, 512), F32), shape((384, 512), BF16)],
        scratch_shapes=[pltpu.VMEM((768, 512), F32), pltpu.VMEM((512, 512), BF16)],
        compiler_params=params(),
        cost_estimate=cost(1600000000, 6000000),
        name="query_rows_back",
    )(core, query_rows, back_output, n_own, n_other, n_up)


def out_grad_kernel(core_ref, h_ref, own_ref, other_ref, c_ref, kept_ref, sent_ref, go, pair):
    @first_step
    def _():
        in_order(core_ref, own_ref, other_ref, pair)
        go[...] = jnp.zeros_like(go)

    output_rows = rounded(times_transpose(h_ref[...], pair[256:, :]))
    go[...] += token_sum(c_ref[...], output_rows)

    @last_step
    def _():
        share_rows(core_ref[0], go, kept_ref, sent_ref, 0)


SHARES = [shape((4, 96, 256), F32), shape((4, 96, 256), BF16)]


def out_grads(core, hidden, n_own, n_other, cotangent):
    tokens = cotangent.shape[0]
    return pl.pallas_call(
        out_grad_kernel,
        grid=(tokens // TILE,),
        in_specs=[SCALAR, rows_of(512), whole(256, 512), whole(256, 512), rows_of(768)],
        out_specs=[whole(4, 96, 256)] * 2,
        out_shape=SHARES,
        scratch_shapes=[pltpu.VMEM((768, 256), F32), pltpu.VMEM((512, 512), BF16)],
        compiler_params=params(),
        cost_estimate=cost(700000000, 4000000),
        name="out_grads",
    )(core, hidden, n_own, n_other, cotangent)


def query_grad_kernel(core_ref, bp_ref, br_ref, own_ref, other_ref, nu_ref, x_ref, qg_ref, kept_ref, sent_ref, gq, pair):
    @first_step
    def _():
        in_order(core_ref, own_ref, other_ref, pair)
        gq[...] = jnp.zeros_like(gq)

    query_grad = rounded(times_transpose(bp_ref[...], pair[:256, :]) + times_transpose(br_ref[...], nu_ref[...]))
    qg_ref[...] = query_grad
    gq[...] += token_sum(x_ref[...], query_grad)

    @last_step
    def _():
        share_rows(core_ref[0], gq, kept_ref, sent_ref, 0)


def query_grads(core, back_p, back_r, n_own, n_other, n_up, inputs):
    tokens = inputs.shape[0]
    return pl.pallas_call(
        query_grad_kernel,
        grid=(tokens // TILE,),
        in_specs=[SCALAR] + [rows_of(512)] * 2 + [whole(256, 512)] * 3 + [rows_of(768)],
        out_specs=[rows_of(256)] + [whole(4, 96, 256)] * 2,
        out_shape=[shape((tokens, 256), BF16)] + SHARES,
        scratch_shapes=[pltpu.VMEM((768, 256), F32), pltpu.VMEM((512, 512), BF16)],
        compiler_params=params(),
        cost_estimate=cost(950000000, 5000000),
        name="query_grads",
    )(core, back_p, back_r, n_own, n_other, n_up, inputs)


def back_kernel(core_ref, x_ref, k_ref, v_ref, s_ref, rate_ref, fi_ref, fu_ref, fo_ref, own_ref, other_ref, bu_ref, kg_ref, vg_ref, rate_out, kept_ref, sent_ref, sums, gk, gv, pair, wi_ref, wu_ref, wo_ref):
    in_order(core_ref, own_ref, other_ref, pair)
    wi_ref[...] = rounded(fi_ref[...])
    wu_ref[...] = rounded(fu_ref[...])
    wo_ref[...] = rounded(fo_ref[...])

    key_rows, scaled = k_ref[...], s_ref[...]
    b_in, b_up, b_out = pair[:256, :], bu_ref[...], pair[256:, :]
    pre_in = product(key_rows, wi_ref[...])
    pre_up = product(key_rows, wu_ref[...])
    upstream = times_transpose(scaled, wo_ref[...])
    press_in = product(key_rows, b_in)
    press_up = product(key_rows, b_up)
    back_hid = product(scaled, b_out)
    sigma = sigmoid(pre_in)
    activation = pre_in * sigma
    fall = 1.0 - sigma
    slope = sigma * (1.0 + pre_in * fall)
    curvature = sigma * fall * (2.0 + pre_in * (1.0 - 2.0 * sigma))
    hidden = rounded(activation * pre_up)
    rise = pre_up * slope
    steep = upstream * slope
    grad_in_rows = rounded(upstream * rise)
    grad_up_rows = rounded(upstream * activation)
    back_upstream = rounded(press_in * rise + press_up * activation)
    back_pre_up = rounded(press_in * steep + back_hid * activation)
    back_pre_in = rounded(press_in * upstream * pre_up * curvature + press_up * steep + back_hid * rise)
    both = token_sum(key_rows, jnp.concatenate([back_pre_in, back_pre_up], axis=1))
    put_sums(sums, (both[:, :512], both[:, 512:], token_sum(scaled, back_upstream)))
    back_scaled = times_transpose(hidden, b_out) + product(back_upstream, wo_ref[...])
    scores = jnp.sum(back_scaled * v_ref[...].astype(F32), axis=1, keepdims=True)
    rate_out[...] = jnp.broadcast_to(scores, (rate_ref.shape[1], 128)).T[:1, :]
    value_grad = rounded(column(rate_ref[...]) * back_scaled)
    vg_ref[...] = value_grad
    key_sum = times_transpose(grad_in_rows, b_in) + times_transpose(grad_up_rows, b_up)
    key_sum = key_sum + times_transpose(back_pre_in, wi_ref[...]) + times_transpose(back_pre_up, wu_ref[...])
    key_grad = rounded(key_sum)
    kg_ref[...] = key_grad
    both = token_sum(x_ref[...], jnp.concatenate([key_grad, value_grad], axis=1))
    gk[...] = both[:, :256]
    gv[...] = both[:, 256:]

    core = core_ref[0]
    for a in range(4):
        mine = sums[pl.ds(pl.multiple_of(core * 384 + 96 * a, 96), 96), :]
        theirs = rounded(sums[pl.ds(pl.multiple_of((1 - core) * 384 + 96 * a, 96), 96), :])
        for side in range(2):
            kept_ref[a, 96 * side : 96 * side + 96, :] = mine[:, 256 * side : 256 * side + 256]
            sent_ref[a, 96 * side : 96 * side + 96, :] = theirs[:, 256 * side : 256 * side + 256]
    share_rows(core, gk, kept_ref, sent_ref, 192)
    share_rows(core, gv, kept_ref, sent_ref, 288)


def update_back(core, inputs, key_rows, value_rows, scaled, rates, fast_in, fast_up, fast_out, b_own, b_other, b_up):
    tokens = key_rows.shape[0]
    return pl.pallas_call(
        back_kernel,
        in_specs=[SCALAR] + [IN_VMEM] * 11,
        out_specs=[IN_VMEM] * 5,
        out_shape=[shape((tokens, 256), BF16)] * 2
        + [shape((1, tokens), F32), shape((4, 384, 256), F32), shape((4, 384, 256), BF16)],
        scratch_shapes=[pltpu.VMEM((768, 512), F32), pltpu.VMEM((768, 256), F32), pltpu.VMEM((768, 256), F32), pltpu.VMEM((512, 512), BF16)]
        + [pltpu.VMEM(*w) for w in WEIGHTS],
        compiler_params=params(),
        cost_estimate=cost(5600000000, 10000000),
        name="update_back",
    )(core, inputs, key_rows, value_rows, scaled, rates, fast_in, fast_up, fast_out, b_own, b_other, b_up)


def input_kernel(q_ref, k_ref, v_ref, pq_ref, pk_ref, pv_ref, out_ref):
    total = times_transpose(q_ref[...], pq_ref[...]) + times_transpose(k_ref[...], pk_ref[...])
    out_ref[...] = rounded(total + times_transpose(v_ref[...], pv_ref[...]))


def input_back(query_grad, key_grad, value_grad, proj_query, proj_key, proj_value):
    tokens = query_grad.shape[0]
    return pl.pallas_call(
        input_kernel,
        grid=(tokens // TILE,),
        in_specs=[rows_of(256)] * 3 + [whole(768, 256)] * 3,
        out_specs=rows_of(768),
        out_shape=shape((tokens, 768), BF16),
        compiler_params=params(),
        cost_estimate=cost(1200000000, 4000000),
        name="input_back",
    )(query_grad, key_grad, value_grad, proj_query, proj_key, proj_value)


SHIFTS = (0.0, 0.05, 0.4, 0.9, 0.9)


def shift_of(sweep):
    shift = jnp.float32(SHIFTS[0])
    for index, value in enumerate(SHIFTS[1:]):
        shift = jnp.where(sweep > index, jnp.float32(value), shift)
    return shift


def coefficients(shift):
    return 3.4445 - 4.775 * shift + 2.0315 * shift * shift, -4.775 + 2.0 * 2.0315 * shift, 2.0315


def on_diagonal(value):
    rows = lax.broadcasted_iota(jnp.int32, (256, 256), 0)
    columns = lax.broadcasted_iota(jnp.int32, (256, 256), 1)
    return jnp.where(rows == columns, value, 0.0)


def newton_schulz(current, shift):
    constant, linear, square = coefficients(shift)
    rows = rounded(current)
    excess = times_transpose(rows, rows)
    excess = excess - on_diagonal(shift)
    short = rounded(excess)
    poly = rounded(linear * excess + square * product(short, short))
    return constant * current + product(poly, rows), (rows, short, poly)


def newton_schulz_back(grad, rows, short, poly, shift):
    constant, linear, square = coefficients(shift)
    grad_rows = rounded(grad)
    outer = times_transpose(grad_rows, rows)
    outer = outer + outer.T
    inner = product(rounded(outer), short)
    inner = rounded(linear * outer + square * (inner + inner.T))
    return constant * grad + (product(poly, grad_rows) + product(inner, rows))


def norm_of(matrix):
    return jnp.sqrt(jnp.sum(matrix * matrix))


def two_matrices(core, half_ref, other_ref, middle):
    middle[pl.ds(pl.multiple_of(core * 128, 128), 128), :] = half_ref[pl.ds(pl.multiple_of((1 - core) * 256, 256), 128), :]
    middle[pl.ds(pl.multiple_of((1 - core) * 128, 128), 128), :] = other_ref[...]
    own = half_ref[pl.ds(pl.multiple_of(core * 128, 128), 256), :]
    return [own.astype(F32), middle[...].astype(F32)]


def ortho_kernel(core_ref, half_ref, other_ref, fast_own_ref, fast_up_ref, own_ref, up_ref, x_ref, a_ref, p_ref, middle, current):
    for index, matrix in enumerate(two_matrices(core_ref[0], half_ref, other_ref, middle)):
        current[index] = matrix * (1.0 / (norm_of(matrix) + 1e-07))

    def step(sweep, carry):
        shift = shift_of(sweep)
        results = [newton_schulz(current[index], shift) for index in range(2)]
        for index, (value, kept) in enumerate(results):
            current[index] = value
            for ref, part in zip((x_ref, a_ref, p_ref), kept):
                ref[sweep, index] = part
        return carry

    lax.fori_loop(0, NS_STEPS, step, 0)
    own_ref[...] = rounded(fast_own_ref[...] + current[0])
    up_ref[...] = rounded(fast_up_ref[...] + current[1])


def ortho(core, half, other, fast_own, fast_up):
    return pl.pallas_call(
        ortho_kernel,
        in_specs=[SCALAR] + [IN_VMEM] * 4,
        out_specs=[IN_VMEM] * 5,
        out_shape=[shape((256, 512), BF16)] * 2 + [shape((NS_STEPS, 2, 256, columns), BF16) for columns in (512, 256, 256)],
        scratch_shapes=[pltpu.VMEM((256, 512), BF16), pltpu.VMEM((2, 256, 512), F32)],
        compiler_params=params(),
        cost_estimate=cost(1700000000, 6000000),
        name="ortho",
    )(core, half, other, fast_own, fast_up)


def ortho_back_kernel(core_ref, th_ref, to_ref, half_ref, other_ref, x_ref, a_ref, p_ref, own_ref, up_ref, middle, grads):
    for index, matrix in enumerate(two_matrices(core_ref[0], half_ref, other_ref, middle)):
        grads[index] = matrix

    def step(done, carry):
        sweep = NS_STEPS - 1 - done
        shift = shift_of(sweep)
        results = []
        for index in range(2):
            kept = [ref[sweep, index] for ref in (x_ref, a_ref, p_ref)]
            results.append(newton_schulz_back(grads[index], *kept, shift))
        for index, value in enumerate(results):
            grads[index] = value
        return carry

    lax.fori_loop(0, NS_STEPS, step, 0)
    totals = two_matrices(core_ref[0], th_ref, to_ref, middle)
    for matrix, grad, out_ref in zip(totals, (grads[0], grads[1]), (own_ref, up_ref)):
        norm = norm_of(matrix)
        scale = 1.0 / (norm + 1e-07)
        dot = jnp.sum(grad * matrix)
        out_ref[...] = rounded(grad * scale - matrix * (dot * scale * scale / norm))


def ortho_back(core, totals, adjoint, trail):
    return pl.pallas_call(
        ortho_back_kernel,
        in_specs=[SCALAR] + [IN_VMEM] * 7,
        out_specs=[IN_VMEM] * 2,
        out_shape=[shape((256, 512), BF16)] * 2,
        scratch_shapes=[pltpu.VMEM((256, 512), BF16), pltpu.VMEM((2, 256, 512), F32)],
        compiler_params=params(),
        cost_estimate=cost(2700000000, 6000000),
        name="ortho_back",
    )(core, *totals, *adjoint, *trail)


def pack_kernel(place_ref, kept_ref, in_ref, one_ref, two_ref, three_ref, mine_ref):
    for offset, out_ref in enumerate((mine_ref, one_ref, two_ref, three_ref)):
        at = lax.rem(place_ref[0] + offset, 4)
        out_ref[...] = (kept_ref[at] + in_ref[at].astype(F32)).astype(out_ref.dtype)


def pack(place, kept, received):
    return pl.pallas_call(
        pack_kernel,
        in_specs=[SCALAR] + [IN_VMEM] * 2,
        out_specs=[IN_VMEM] * 4,
        out_shape=[shape(kept.shape[1:], BF16)] * 3 + [shape(kept.shape[1:], F32)],
        compiler_params=params(),
        cost_estimate=cost(1000000, 2000000),
        name="pack",
    )(place, kept, received)


def pack_both_kernel(place_ref, late_ref, late_in_ref, early_ref, early_in_ref, one_ref, two_ref, three_ref, mine_ref):
    for offset, out_ref in enumerate((mine_ref, one_ref, two_ref, three_ref)):
        at = lax.rem(place_ref[0] + offset, 4)
        out_ref[:384, :] = (late_ref[at] + late_in_ref[at].astype(F32)).astype(out_ref.dtype)
        out_ref[384:, :] = (early_ref[at] + early_in_ref[at].astype(F32)).astype(out_ref.dtype)


def pack_both(place, late, late_in, early, early_in):
    return pl.pallas_call(
        pack_both_kernel,
        in_specs=[SCALAR] + [IN_VMEM] * 4,
        out_specs=[IN_VMEM] * 4,
        out_shape=[shape((576, 256), BF16)] * 3 + [shape((576, 256), F32)],
        compiler_params=params(),
        cost_estimate=cost(1000000, 5000000),
        name="pack_both",
    )(place, late, late_in, early, early_in)


def unpack_kernel(second_ref, mine_ref, a_ref, b_ref, c_ref, one_ref, two_ref, three_ref, contrib_ref, own_ref, total):
    total[...] = mine_ref[...] + a_ref[...].astype(F32) + b_ref[...].astype(F32) + c_ref[...].astype(F32)
    contrib = rounded(total[:192, :])
    contrib_ref[...] = contrib
    for offset, out_ref in enumerate((own_ref, one_ref, two_ref, three_ref)):
        at = lax.rem(second_ref[0] + offset, 4) * 24
        shares = [total[pl.ds(pl.multiple_of(192 + 96 * index + at, 8), 24), :] for index in range(4)]
        if offset:
            out_ref[:192, :] = contrib
            for index in (0, 2):
                out_ref[192 + 24 * index : 240 + 24 * index, :] = rounded(jnp.concatenate(shares[index : index + 2], axis=0))
        else:
            for index in range(4):
                out_ref[24 * index : 24 * index + 24, :] = shares[index]


def unpack(second, mine, blocks):
    return pl.pallas_call(
        unpack_kernel,
        in_specs=[SCALAR] + [IN_VMEM] * 4,
        out_specs=[IN_VMEM] * 5,
        out_shape=[shape((288, 256), BF16)] * 3 + [shape((192, 256), BF16), shape((96, 256), F32)],
        scratch_shapes=[pltpu.VMEM((576, 256), F32)],
        compiler_params=params(),
        cost_estimate=cost(1000000, 2000000),
        name="unpack",
    )(second, mine, *blocks)


def finish_kernel(core_ref, half_ref, other_ref, gi_ref, gu_ref, go_ref, scratch):
    core = core_ref[0]
    scratch[pl.ds(pl.multiple_of(core * 384, 384), 384), :] = half_ref[...]
    scratch[pl.ds(pl.multiple_of((1 - core) * 384, 384), 384), :] = other_ref[...]
    gi_ref[...] = scratch[:256, :].astype(F32)
    gu_ref[...] = scratch[256:512, :].astype(F32)
    go_ref[...] = scratch[512:, :].astype(F32).T


def finish(core, half, other):
    return pl.pallas_call(
        finish_kernel,
        in_specs=[SCALAR] + [IN_VMEM] * 2,
        out_specs=[IN_VMEM] * 3,
        out_shape=[shape((256, 512), F32)] * 2 + [shape((512, 256), F32)],
        scratch_shapes=[pltpu.VMEM((768, 512), BF16)],
        compiler_params=params(),
        cost_estimate=cost(1000000, 3000000),
        name="finish",
    )(core, half, other)


def ring_pairs(first, offset):
    pairs = []
    for index in range(32):
        z, x, core = index // 8, (index // 2) % 4, index % 2
        if (core == 0) == first:
            x = (x + offset) % 4
        else:
            z = (z + offset) % 4
        pairs.append((index, z * 8 + x * 2 + core))
    return pairs


def swap_cores(value):
    return lax.ppermute(value, "seq", [(index, index ^ 1) for index in range(32)])


def places():
    me = lax.axis_index("seq")
    z, x, core = me // 8, (me // 2) % 4, me % 2
    return core, jnp.where(core == 0, x, z), jnp.where(core == 0, z, x)


def pick(which, parts):
    return lax.select_n(which, *parts)


def part_at(parts, which):
    return lax.dynamic_index_in_dim(parts, which % 4, 0, keepdims=False)


def scatter_four(parts, place, first):
    received = [
        lax.ppermute(rounded(part_at(parts, place + offset)), "seq", ring_pairs(first, offset)) for offset in (1, 2, 3)
    ]
    total = part_at(parts, place)
    for block in received:
        total = total + block.astype(jnp.float32)
    return total


def exchange_four(block, first):
    return [block] + [lax.ppermute(block, "seq", ring_pairs(first, offset)) for offset in (1, 2, 3)]


def sum_four(blocks):
    a, b, c, d = [block.astype(jnp.float32) for block in blocks]
    return (a + c) + (b + d)


def in_places(blocks, place):
    return jnp.concatenate([pick((place - j) % 4, blocks) for j in range(4)], axis=0)


def middle_half(half, core):
    return swap_cores(jnp.where(core == 0, half[256:], half[:128]))


def together(*values):
    return lax.optimization_barrier(values)


def body(
    inputs,
    token_rates,
    proj_query,
    proj_key,
    proj_value,
    proj_output,
    fast_in,
    fast_up,
    fast_out,
    cotangent,
):
    core_at, place, second = places()
    core = core_at.reshape(1)
    rates = token_rates.reshape(1, -1)

    query_rows, key_rows, value_rows, scaled, kept, sent = update_rows(
        core, inputs, rates, proj_query, proj_key, proj_value, fast_in, fast_up, fast_out
    )
    quarter = scatter_four((kept + swap_cores(sent).astype(F32)).reshape(4, 96, 512), place, True)
    shared = sum_four(exchange_four(rounded(quarter), False))
    back_output, fast_own = back_output_rows(core, together(shared, cotangent)[1], proj_output, fast_in, fast_out)
    blocks, back_output, fast_own = together(exchange_four(rounded(shared), True), back_output, fast_own)
    half = in_places(blocks, place)
    totals = half, middle_half(half, core_at)
    n_own, n_up, *trail = ortho(core, *totals, fast_own, fast_up)
    n_other = swap_cores(n_own)

    back_p, back_r, hidden_q, kept, sent = query_rows_back(core, query_rows, back_output, n_own, n_other, n_up)
    half = (kept + swap_cores(sent).astype(F32)).reshape(4, 96, 512)
    half, hidden_q, back_p, back_r = together(half, hidden_q, back_p, back_r)
    out_kept, out_sent = out_grads(core, hidden_q, n_own, n_other, cotangent)
    quarter, out_kept, out_sent, back_p, back_r = together(scatter_four(half, place, True), out_kept, out_sent, back_p, back_r)
    query_grad, query_kept, query_sent = query_grads(core, back_p, back_r, n_own, n_other, n_up, inputs)
    blocks, query_grad, query_kept, query_sent = together(
        exchange_four(rounded(quarter), False), query_grad, query_kept, query_sent
    )
    adjoint_share = sum_four(blocks)
    blocks = exchange_four(rounded(adjoint_share), True)
    early_sent = jnp.concatenate([query_sent, out_sent], axis=1)
    half = in_places(blocks, place)
    b_own, b_up = ortho_back(core, totals, (half, middle_half(half, core_at)), trail)
    b_other = swap_cores(b_own)
    early = jnp.concatenate([query_kept, out_kept], axis=1)
    early_in = swap_cores(early_sent)

    key_grad, value_grad, back_rate, kept, sent = update_back(
        core, inputs, key_rows, value_rows, scaled, rates, fast_in, fast_up, fast_out, b_own, b_other, b_up
    )
    back_inputs = input_back(query_grad, key_grad, value_grad, proj_query, proj_key, proj_value)
    *blocks, mine = pack_both(place.reshape(1), kept, swap_cores(sent), early, early_in)
    blocks = [lax.ppermute(block, "seq", ring_pairs(True, offset + 1)) for offset, block in enumerate(blocks)]
    *blocks, contrib, mine = unpack(second.reshape(1), mine, blocks)
    received = [lax.ppermute(block, "seq", ring_pairs(False, offset + 1)) for offset, block in enumerate(blocks)]
    summed = sum_four([contrib] + [block[:192] for block in received])
    for block in received:
        mine = mine + block[192:].astype(F32)
    grad_key, grad_value, grad_query, grad_output = [mine[24 * index : 24 * index + 24] for index in range(4)]
    share = adjoint_share + jnp.concatenate([summed[:96], summed[96:]], axis=1)
    blocks = exchange_four(rounded(share), True)
    half = in_places(blocks, place)
    grad_in, grad_up, grad_out = finish(core, half, swap_cores(half))
    return (
        back_inputs,
        back_rate.reshape(-1),
        grad_in,
        grad_up,
        grad_out,
        grad_query,
        grad_key,
        grad_value,
        grad_output.T,
    )


def solution(mesh):
    in_specs = (
        P(("batch", "seq"), None),
        P(("batch", "seq")),
        P(),
        P(),
        P(),
        P(),
        P(),
        P(),
        P(),
        P(("batch", "seq"), None),
    )
    out_specs = (
        P(("batch", "seq"), None),
        P(("batch", "seq")),
        P("batch", None),
        P("batch", None),
        P("batch", None),
        P("seq", "batch"),
        P("seq", "batch"),
        P("seq", "batch"),
        P("batch", "seq"),
    )
    return jax.shard_map(body, mesh=mesh, in_specs=in_specs, out_specs=out_specs, check_vma=False)
```

```python
import jax
import jax.numpy as jnp
from jax import lax
from jax.experimental import pallas as pl
from jax.experimental.pallas import tpu as pltpu
from jax.sharding import PartitionSpec as P

NS_STEPS = 5
TILE = 512
LARGE = 1024
F32 = jnp.float32
BF16 = jnp.bfloat16
VMEM_BYTES = 28 * 1024 * 1024


def rounded(value):
    return value.astype(jnp.bfloat16)


def product(left, right):
    return jnp.dot(left, right, preferred_element_type=jnp.float32)


def token_sum(left, right):
    return lax.dot_general(
        left, right, (((0,), (0,)), ((), ())), preferred_element_type=jnp.float32
    )


def times_transpose(left, right):
    return lax.dot_general(
        left, right, (((1,), (1,)), ((), ())), preferred_element_type=jnp.float32
    )


def sigmoid(value):
    return 1.0 / (1.0 + jnp.exp(-value))


def column(row):
    wide = jnp.broadcast_to(row, (128, row.shape[1])).T
    return jnp.concatenate([wide, wide], axis=1)


def rows_of(columns, tile=TILE):
    return pl.BlockSpec((tile, columns), lambda step: (step, 0))


def row_block(tile):
    return pl.BlockSpec((1, tile), lambda step: (0, step))


def whole(*shape):
    return pl.BlockSpec(shape, lambda step: (0,) * len(shape))


SCALAR = pl.BlockSpec(memory_space=pltpu.SMEM)
IN_VMEM = pl.BlockSpec(memory_space=pltpu.VMEM)


def params(limit=VMEM_BYTES):
    return pltpu.CompilerParams(vmem_limit_bytes=limit)


def cost(flops, moved):
    return pl.CostEstimate(flops=flops, bytes_accessed=moved, transcendentals=0)


def shape(dims, kind):
    return jax.ShapeDtypeStruct(dims, kind)


def add_sums(sums, parts):
    for index, part in enumerate(parts):
        rows = pl.ds(256 * index, 256)
        sums[rows, :] = sums[rows, :] + part


def put_sums(sums, parts):
    for index, part in enumerate(parts):
        sums[256 * index : 256 * index + 256, :] = part


def hand_halves(core_ref, sums, kept_ref, sent_ref):
    core = core_ref[0]
    kept_ref[...] = sums[pl.ds(pl.multiple_of(core * 384, 384), 384), :]
    sent_ref[...] = rounded(sums[pl.ds(pl.multiple_of((1 - core) * 384, 384), 384), :])


def first_step(action):
    pl.when(pl.program_id(0) == 0)(action)


def last_step(action):
    pl.when(pl.program_id(0) == pl.num_programs(0) - 1)(action)


def in_order(core_ref, own_ref, other_ref, pair):
    core = core_ref[0]
    pair[pl.ds(pl.multiple_of(core * 256, 256), 256), :] = own_ref[...]
    pair[pl.ds(pl.multiple_of((1 - core) * 256, 256), 256), :] = other_ref[...]


def share_rows(core, total, kept_ref, sent_ref, start):
    for a in range(4):
        for b in (0, 2):
            low = [pl.multiple_of(jnp.where(core == 0, (c * 4 + a) * 48, (a * 4 + c) * 48 + 24), 8) for c in (b, b + 1)]
            high = [pl.multiple_of(jnp.where(core == 0, (a * 4 + c) * 48 + 24, (c * 4 + a) * 48), 8) for c in (b, b + 1)]
            at = start + 24 * b
            kept_ref[a, at : at + 48, :] = jnp.concatenate([total[pl.ds(row, 24), :] for row in low], axis=0)
            sent_ref[a, at : at + 48, :] = rounded(jnp.concatenate([total[pl.ds(row, 24), :] for row in high], axis=0))


def update_kernel(core_ref, x_ref, rate_ref, pq_ref, pk_ref, pv_ref, fi_ref, fu_ref, fo_ref, q_ref, k_ref, v_ref, s_ref, kept_ref, sent_ref, sums, wi_ref, wu_ref, wo_ref):
    @first_step
    def _():
        sums[...] = jnp.zeros_like(sums)
        wi_ref[...] = rounded(fi_ref[...])
        wu_ref[...] = rounded(fu_ref[...])
        wo_ref[...] = rounded(fo_ref[...])

    x = x_ref[...]
    key_rows = rounded(product(x, pk_ref[...]))
    value_rows = rounded(product(x, pv_ref[...]))
    scaled = rounded(column(rate_ref[...]) * value_rows.astype(F32))
    q_ref[...] = rounded(product(x, pq_ref[...]))
    k_ref[...] = key_rows
    v_ref[...] = value_rows
    s_ref[...] = scaled
    pre_in = product(key_rows, wi_ref[...])
    pre_up = product(key_rows, wu_ref[...])
    upstream = times_transpose(scaled, wo_ref[...])
    sigma = sigmoid(pre_in)
    activation = pre_in * sigma
    slope = sigma * (1.0 + pre_in * (1.0 - sigma))
    hidden = rounded(activation * pre_up)
    grad_in_rows = rounded(upstream * pre_up * slope)
    grad_up_rows = rounded(upstream * activation)
    both = token_sum(key_rows, jnp.concatenate([grad_in_rows, grad_up_rows], axis=1))
    add_sums(sums, (both[:, :512], both[:, 512:], token_sum(scaled, hidden)))
    last_step(lambda: hand_halves(core_ref, sums, kept_ref, sent_ref))


WEIGHTS = [((256, 512), BF16), ((256, 512), BF16), ((512, 256), BF16)]


def update_rows(core, inputs, rates, proj_query, proj_key, proj_value, fast_in, fast_up, fast_out):
    tokens = inputs.shape[0]
    return pl.pallas_call(
        update_kernel,
        grid=(tokens // LARGE,),
        in_specs=[SCALAR, rows_of(768, LARGE), row_block(LARGE)] + [whole(768, 256)] * 3 + [ whole(256, 512), whole(256, 512), whole(512, 256)],
        out_specs=[rows_of(256, LARGE)] * 4 + [whole(384, 512)] * 2,
        out_shape=[shape((tokens, 256), BF16)] * 4 + [shape((384, 512), F32), shape((384, 512), BF16)],
        scratch_shapes=[pltpu.VMEM((768, 512), F32)] + [pltpu.VMEM(*w) for w in WEIGHTS],
        compiler_params=params(60 * 1024 * 1024),
        cost_estimate=cost(2400000000, 6000000),
        name="update_rows",
    )(core, inputs, rates, proj_query, proj_key, proj_value, fast_in, fast_up, fast_out)


def back_output_kernel(core_ref, c_ref, po_ref, fi_ref, fo_ref, out_ref, own_ref):
    core = core_ref[0]

    @first_step
    def _():
        own_ref[...] = jnp.where(core == 0, fi_ref[...], fo_ref[...].T)

    out_ref[...] = rounded(times_transpose(c_ref[...], po_ref[...]))


def back_output_rows(core, cotangent, proj_output, fast_in, fast_out):
    tokens = cotangent.shape[0]
    return pl.pallas_call(
        back_output_kernel,
        grid=(tokens // TILE,),
        in_specs=[SCALAR, rows_of(768), whole(256, 768), whole(256, 512), whole(512, 256)],
        out_specs=[rows_of(256), whole(256, 512)],
        out_shape=[shape((tokens, 256), BF16), shape((256, 512), F32)],
        compiler_params=params(),
        cost_estimate=cost(400000000, 4000000),
        name="back_output",
    )(core, cotangent, proj_output, fast_in, fast_out)


def query_kernel(core_ref, q_ref, bo_ref, own_ref, other_ref, nu_ref, bp_ref, br_ref, h_ref, kept_ref, sent_ref, sums, pair):
    in_order(core_ref, own_ref, other_ref, pair)
    query_rows, back_output = q_ref[...], bo_ref[...]
    pre_p = product(query_rows, pair[:256, :])
    pre_r = product(query_rows, nu_ref[...])
    back_hidden = product(back_output, pair[256:, :])
    sigma = sigmoid(pre_p)
    activation = pre_p * sigma
    slope = sigma * (1.0 + pre_p * (1.0 - sigma))
    hidden = rounded(activation * pre_r)
    back_p = rounded(back_hidden * pre_r * slope)
    back_r = rounded(back_hidden * activation)
    bp_ref[...] = back_p
    br_ref[...] = back_r
    h_ref[...] = hidden
    both = token_sum(query_rows, jnp.concatenate([back_p, back_r], axis=1))
    put_sums(sums, (both[:, :512], both[:, 512:], token_sum(back_output, hidden)))
    hand_halves(core_ref, sums, kept_ref, sent_ref)


def query_rows_back(core, query_rows, back_output, n_own, n_other, n_up):
    tokens = query_rows.shape[0]
    return pl.pallas_call(
        query_kernel,
        in_specs=[SCALAR] + [IN_VMEM] * 5,
        out_specs=[IN_VMEM] * 5,
        out_shape=[shape((tokens, 512), BF16)] * 3 + [shape((384, 512), F32), shape((384, 512), BF16)],
        scratch_shapes=[pltpu.VMEM((768, 512), F32), pltpu.VMEM((512, 512), BF16)],
        compiler_params=params(),
        cost_estimate=cost(1600000000, 6000000),
        name="query_rows_back",
    )(core, query_rows, back_output, n_own, n_other, n_up)


def out_grad_kernel(core_ref, h_ref, own_ref, other_ref, c_ref, kept_ref, sent_ref, go, pair):
    @first_step
    def _():
        in_order(core_ref, own_ref, other_ref, pair)
        go[...] = jnp.zeros_like(go)

    output_rows = rounded(times_transpose(h_ref[...], pair[256:, :]))
    go[...] += token_sum(c_ref[...], output_rows)

    @last_step
    def _():
        share_rows(core_ref[0], go, kept_ref, sent_ref, 0)


SHARES = [shape((4, 96, 256), F32), shape((4, 96, 256), BF16)]


def out_grads(core, hidden, n_own, n_other, cotangent):
    tokens = cotangent.shape[0]
    return pl.pallas_call(
        out_grad_kernel,
        grid=(tokens // TILE,),
        in_specs=[SCALAR, rows_of(512), whole(256, 512), whole(256, 512), rows_of(768)],
        out_specs=[whole(4, 96, 256)] * 2,
        out_shape=SHARES,
        scratch_shapes=[pltpu.VMEM((768, 256), F32), pltpu.VMEM((512, 512), BF16)],
        compiler_params=params(),
        cost_estimate=cost(700000000, 4000000),
        name="out_grads",
    )(core, hidden, n_own, n_other, cotangent)


def query_grad_kernel(core_ref, bp_ref, br_ref, own_ref, other_ref, nu_ref, x_ref, qg_ref, kept_ref, sent_ref, gq, pair):
    @first_step
    def _():
        in_order(core_ref, own_ref, other_ref, pair)
        gq[...] = jnp.zeros_like(gq)

    query_grad = rounded(times_transpose(bp_ref[...], pair[:256, :]) + times_transpose(br_ref[...], nu_ref[...]))
    qg_ref[...] = query_grad
    gq[...] += token_sum(x_ref[...], query_grad)

    @last_step
    def _():
        share_rows(core_ref[0], gq, kept_ref, sent_ref, 0)


def query_grads(core, back_p, back_r, n_own, n_other, n_up, inputs):
    tokens = inputs.shape[0]
    return pl.pallas_call(
        query_grad_kernel,
        grid=(tokens // TILE,),
        in_specs=[SCALAR] + [rows_of(512)] * 2 + [whole(256, 512)] * 3 + [rows_of(768)],
        out_specs=[rows_of(256)] + [whole(4, 96, 256)] * 2,
        out_shape=[shape((tokens, 256), BF16)] + SHARES,
        scratch_shapes=[pltpu.VMEM((768, 256), F32), pltpu.VMEM((512, 512), BF16)],
        compiler_params=params(),
        cost_estimate=cost(950000000, 5000000),
        name="query_grads",
    )(core, back_p, back_r, n_own, n_other, n_up, inputs)


def back_kernel(core_ref, x_ref, k_ref, v_ref, s_ref, rate_ref, fi_ref, fu_ref, fo_ref, own_ref, other_ref, bu_ref, kg_ref, vg_ref, rate_out, kept_ref, sent_ref, sums, gk, gv, pair, wi_ref, wu_ref, wo_ref):
    in_order(core_ref, own_ref, other_ref, pair)
    wi_ref[...] = rounded(fi_ref[...])
    wu_ref[...] = rounded(fu_ref[...])
    wo_ref[...] = rounded(fo_ref[...])

    key_rows, scaled = k_ref[...], s_ref[...]
    b_in, b_up, b_out = pair[:256, :], bu_ref[...], pair[256:, :]
    pre_in = product(key_rows, wi_ref[...])
    pre_up = product(key_rows, wu_ref[...])
    upstream = times_transpose(scaled, wo_ref[...])
    press_in = product(key_rows, b_in)
    press_up = product(key_rows, b_up)
    back_hid = product(scaled, b_out)
    sigma = sigmoid(pre_in)
    activation = pre_in * sigma
    fall = 1.0 - sigma
    slope = sigma * (1.0 + pre_in * fall)
    curvature = sigma * fall * (2.0 + pre_in * (1.0 - 2.0 * sigma))
    hidden = rounded(activation * pre_up)
    rise = pre_up * slope
    steep = upstream * slope
    grad_in_rows = rounded(upstream * rise)
    grad_up_rows = rounded(upstream * activation)
    back_upstream = rounded(press_in * rise + press_up * activation)
    back_pre_up = rounded(press_in * steep + back_hid * activation)
    back_pre_in = rounded(press_in * upstream * pre_up * curvature + press_up * steep + back_hid * rise)
    both = token_sum(key_rows, jnp.concatenate([back_pre_in, back_pre_up], axis=1))
    put_sums(sums, (both[:, :512], both[:, 512:], token_sum(scaled, back_upstream)))
    back_scaled = times_transpose(hidden, b_out) + product(back_upstream, wo_ref[...])
    scores = jnp.sum(back_scaled * v_ref[...].astype(F32), axis=1, keepdims=True)
    rate_out[...] = jnp.broadcast_to(scores, (rate_ref.shape[1], 128)).T[:1, :]
    value_grad = rounded(column(rate_ref[...]) * back_scaled)
    vg_ref[...] = value_grad
    key_sum = times_transpose(grad_in_rows, b_in) + times_transpose(grad_up_rows, b_up)
    key_sum = key_sum + times_transpose(back_pre_in, wi_ref[...]) + times_transpose(back_pre_up, wu_ref[...])
    key_grad = rounded(key_sum)
    kg_ref[...] = key_grad
    both = token_sum(x_ref[...], jnp.concatenate([key_grad, value_grad], axis=1))
    gk[...] = both[:, :256]
    gv[...] = both[:, 256:]

    core = core_ref[0]
    for a in range(4):
        mine = sums[pl.ds(pl.multiple_of(core * 384 + 96 * a, 96), 96), :]
        theirs = rounded(sums[pl.ds(pl.multiple_of((1 - core) * 384 + 96 * a, 96), 96), :])
        for side in range(2):
            kept_ref[a, 96 * side : 96 * side + 96, :] = mine[:, 256 * side : 256 * side + 256]
            sent_ref[a, 96 * side : 96 * side + 96, :] = theirs[:, 256 * side : 256 * side + 256]
    share_rows(core, gk, kept_ref, sent_ref, 192)
    share_rows(core, gv, kept_ref, sent_ref, 288)


def update_back(core, inputs, key_rows, value_rows, scaled, rates, fast_in, fast_up, fast_out, b_own, b_other, b_up):
    tokens = key_rows.shape[0]
    return pl.pallas_call(
        back_kernel,
        in_specs=[SCALAR] + [IN_VMEM] * 11,
        out_specs=[IN_VMEM] * 5,
        out_shape=[shape((tokens, 256), BF16)] * 2
        + [shape((1, tokens), F32), shape((4, 384, 256), F32), shape((4, 384, 256), BF16)],
        scratch_shapes=[pltpu.VMEM((768, 512), F32), pltpu.VMEM((768, 256), F32), pltpu.VMEM((768, 256), F32), pltpu.VMEM((512, 512), BF16)]
        + [pltpu.VMEM(*w) for w in WEIGHTS],
        compiler_params=params(),
        cost_estimate=cost(5600000000, 10000000),
        name="update_back",
    )(core, inputs, key_rows, value_rows, scaled, rates, fast_in, fast_up, fast_out, b_own, b_other, b_up)


def input_kernel(q_ref, k_ref, v_ref, pq_ref, pk_ref, pv_ref, out_ref):
    total = times_transpose(q_ref[...], pq_ref[...]) + times_transpose(k_ref[...], pk_ref[...])
    out_ref[...] = rounded(total + times_transpose(v_ref[...], pv_ref[...]))


def input_back(query_grad, key_grad, value_grad, proj_query, proj_key, proj_value):
    tokens = query_grad.shape[0]
    return pl.pallas_call(
        input_kernel,
        grid=(tokens // TILE,),
        in_specs=[rows_of(256)] * 3 + [whole(768, 256)] * 3,
        out_specs=rows_of(768),
        out_shape=shape((tokens, 768), BF16),
        compiler_params=params(),
        cost_estimate=cost(1200000000, 4000000),
        name="input_back",
    )(query_grad, key_grad, value_grad, proj_query, proj_key, proj_value)


SHIFTS = (0.0, 0.05, 0.4, 0.9, 0.9)


def shift_of(sweep):
    shift = jnp.float32(SHIFTS[0])
    for index, value in enumerate(SHIFTS[1:]):
        shift = jnp.where(sweep > index, jnp.float32(value), shift)
    return shift


def coefficients(shift):
    return 3.4445 - 4.775 * shift + 2.0315 * shift * shift, -4.775 + 2.0 * 2.0315 * shift, 2.0315


def on_diagonal(value):
    rows = lax.broadcasted_iota(jnp.int32, (256, 256), 0)
    columns = lax.broadcasted_iota(jnp.int32, (256, 256), 1)
    return jnp.where(rows == columns, value, 0.0)


def newton_schulz(current, shift):
    constant, linear, square = coefficients(shift)
    rows = rounded(current)
    excess = times_transpose(rows, rows)
    excess = excess - on_diagonal(shift)
    short = rounded(excess)
    poly = rounded(linear * excess + square * product(short, short))
    return constant * current + product(poly, rows), (rows, short, poly)


def newton_schulz_back(grad, rows, short, poly, shift):
    constant, linear, square = coefficients(shift)
    grad_rows = rounded(grad)
    outer = times_transpose(grad_rows, rows)
    outer = outer + outer.T
    inner = product(rounded(outer), short)
    inner = rounded(linear * outer + square * (inner + inner.T))
    return constant * grad + (product(poly, grad_rows) + product(inner, rows))


def norm_of(matrix):
    return jnp.sqrt(jnp.sum(matrix * matrix))


def two_matrices(core, half_ref, other_ref, middle):
    middle[pl.ds(pl.multiple_of(core * 128, 128), 128), :] = half_ref[pl.ds(pl.multiple_of((1 - core) * 256, 256), 128), :]
    middle[pl.ds(pl.multiple_of((1 - core) * 128, 128), 128), :] = other_ref[...]
    own = half_ref[pl.ds(pl.multiple_of(core * 128, 128), 256), :]
    return [own.astype(F32), middle[...].astype(F32)]


def ortho_kernel(core_ref, half_ref, other_ref, fast_own_ref, fast_up_ref, own_ref, up_ref, x_ref, a_ref, p_ref, middle, current):
    for index, matrix in enumerate(two_matrices(core_ref[0], half_ref, other_ref, middle)):
        current[index] = matrix * (1.0 / (norm_of(matrix) + 1e-07))

    def step(sweep, carry):
        shift = shift_of(sweep)
        results = [newton_schulz(current[index], shift) for index in range(2)]
        for index, (value, kept) in enumerate(results):
            current[index] = value
            for ref, part in zip((x_ref, a_ref, p_ref), kept):
                ref[sweep, index] = part
        return carry

    lax.fori_loop(0, NS_STEPS, step, 0)
    own_ref[...] = rounded(fast_own_ref[...] + current[0])
    up_ref[...] = rounded(fast_up_ref[...] + current[1])


def ortho(core, half, other, fast_own, fast_up):
    return pl.pallas_call(
        ortho_kernel,
        in_specs=[SCALAR] + [IN_VMEM] * 4,
        out_specs=[IN_VMEM] * 5,
        out_shape=[shape((256, 512), BF16)] * 2 + [shape((NS_STEPS, 2, 256, columns), BF16) for columns in (512, 256, 256)],
        scratch_shapes=[pltpu.VMEM((256, 512), BF16), pltpu.VMEM((2, 256, 512), F32)],
        compiler_params=params(),
        cost_estimate=cost(1700000000, 6000000),
        name="ortho",
    )(core, half, other, fast_own, fast_up)


def ortho_back_kernel(core_ref, th_ref, to_ref, half_ref, other_ref, x_ref, a_ref, p_ref, own_ref, up_ref, middle, grads):
    for index, matrix in enumerate(two_matrices(core_ref[0], half_ref, other_ref, middle)):
        grads[index] = matrix

    def step(done, carry):
        sweep = NS_STEPS - 1 - done
        shift = shift_of(sweep)
        results = []
        for index in range(2):
            kept = [ref[sweep, index] for ref in (x_ref, a_ref, p_ref)]
            results.append(newton_schulz_back(grads[index], *kept, shift))
        for index, value in enumerate(results):
            grads[index] = value
        return carry

    lax.fori_loop(0, NS_STEPS, step, 0)
    totals = two_matrices(core_ref[0], th_ref, to_ref, middle)
    for matrix, grad, out_ref in zip(totals, (grads[0], grads[1]), (own_ref, up_ref)):
        norm = norm_of(matrix)
        scale = 1.0 / (norm + 1e-07)
        dot = jnp.sum(grad * matrix)
        out_ref[...] = rounded(grad * scale - matrix * (dot * scale * scale / norm))


def ortho_back(core, totals, adjoint, trail):
    return pl.pallas_call(
        ortho_back_kernel,
        in_specs=[SCALAR] + [IN_VMEM] * 7,
        out_specs=[IN_VMEM] * 2,
        out_shape=[shape((256, 512), BF16)] * 2,
        scratch_shapes=[pltpu.VMEM((256, 512), BF16), pltpu.VMEM((2, 256, 512), F32)],
        compiler_params=params(),
        cost_estimate=cost(2700000000, 6000000),
        name="ortho_back",
    )(core, *totals, *adjoint, *trail)


def pack_kernel(place_ref, kept_ref, in_ref, one_ref, two_ref, three_ref, mine_ref):
    for offset, out_ref in enumerate((mine_ref, one_ref, two_ref, three_ref)):
        at = lax.rem(place_ref[0] + offset, 4)
        out_ref[...] = (kept_ref[at] + in_ref[at].astype(F32)).astype(out_ref.dtype)


def pack(place, kept, received):
    return pl.pallas_call(
        pack_kernel,
        in_specs=[SCALAR] + [IN_VMEM] * 2,
        out_specs=[IN_VMEM] * 4,
        out_shape=[shape(kept.shape[1:], BF16)] * 3 + [shape(kept.shape[1:], F32)],
        compiler_params=params(),
        cost_estimate=cost(1000000, 2000000),
        name="pack",
    )(place, kept, received)


def pack_both_kernel(place_ref, late_ref, late_in_ref, early_ref, early_in_ref, one_ref, two_ref, three_ref, mine_ref):
    for offset, out_ref in enumerate((mine_ref, one_ref, two_ref, three_ref)):
        at = lax.rem(place_ref[0] + offset, 4)
        out_ref[:384, :] = (late_ref[at] + late_in_ref[at].astype(F32)).astype(out_ref.dtype)
        out_ref[384:, :] = (early_ref[at] + early_in_ref[at].astype(F32)).astype(out_ref.dtype)


def pack_both(place, late, late_in, early, early_in):
    return pl.pallas_call(
        pack_both_kernel,
        in_specs=[SCALAR] + [IN_VMEM] * 4,
        out_specs=[IN_VMEM] * 4,
        out_shape=[shape((576, 256), BF16)] * 3 + [shape((576, 256), F32)],
        compiler_params=params(),
        cost_estimate=cost(1000000, 5000000),
        name="pack_both",
    )(place, late, late_in, early, early_in)


def unpack_kernel(second_ref, mine_ref, a_ref, b_ref, c_ref, one_ref, two_ref, three_ref, contrib_ref, own_ref, total):
    total[...] = mine_ref[...] + a_ref[...].astype(F32) + b_ref[...].astype(F32) + c_ref[...].astype(F32)
    contrib = rounded(total[:192, :])
    contrib_ref[...] = contrib
    for offset, out_ref in enumerate((own_ref, one_ref, two_ref, three_ref)):
        at = lax.rem(second_ref[0] + offset, 4) * 24
        shares = [total[pl.ds(pl.multiple_of(192 + 96 * index + at, 8), 24), :] for index in range(4)]
        if offset:
            out_ref[:192, :] = contrib
            for index in (0, 2):
                out_ref[192 + 24 * index : 240 + 24 * index, :] = rounded(jnp.concatenate(shares[index : index + 2], axis=0))
        else:
            for index in range(4):
                out_ref[24 * index : 24 * index + 24, :] = shares[index]


def unpack(second, mine, blocks):
    return pl.pallas_call(
        unpack_kernel,
        in_specs=[SCALAR] + [IN_VMEM] * 4,
        out_specs=[IN_VMEM] * 5,
        out_shape=[shape((288, 256), BF16)] * 3 + [shape((192, 256), BF16), shape((96, 256), F32)],
        scratch_shapes=[pltpu.VMEM((576, 256), F32)],
        compiler_params=params(),
        cost_estimate=cost(1000000, 2000000),
        name="unpack",
    )(second, mine, *blocks)


def finish_kernel(core_ref, half_ref, other_ref, gi_ref, gu_ref, go_ref, scratch):
    core = core_ref[0]
    scratch[pl.ds(pl.multiple_of(core * 384, 384), 384), :] = half_ref[...]
    scratch[pl.ds(pl.multiple_of((1 - core) * 384, 384), 384), :] = other_ref[...]
    gi_ref[...] = scratch[:256, :].astype(F32)
    gu_ref[...] = scratch[256:512, :].astype(F32)
    go_ref[...] = scratch[512:, :].astype(F32).T


def finish(core, half, other):
    return pl.pallas_call(
        finish_kernel,
        in_specs=[SCALAR] + [IN_VMEM] * 2,
        out_specs=[IN_VMEM] * 3,
        out_shape=[shape((256, 512), F32)] * 2 + [shape((512, 256), F32)],
        scratch_shapes=[pltpu.VMEM((768, 512), BF16)],
        compiler_params=params(),
        cost_estimate=cost(1000000, 3000000),
        name="finish",
    )(core, half, other)


def ring_pairs(first, offset):
    pairs = []
    for index in range(32):
        z, x, core = index // 8, (index // 2) % 4, index % 2
        if (core == 0) == first:
            x = (x + offset) % 4
        else:
            z = (z + offset) % 4
        pairs.append((index, z * 8 + x * 2 + core))
    return pairs


def swap_cores(value):
    return lax.ppermute(value, "seq", [(index, index ^ 1) for index in range(32)])


def places():
    me = lax.axis_index("seq")
    z, x, core = me // 8, (me // 2) % 4, me % 2
    return core, jnp.where(core == 0, x, z), jnp.where(core == 0, z, x)


def pick(which, parts):
    return lax.select_n(which, *parts)


def part_at(parts, which):
    return lax.dynamic_index_in_dim(parts, which % 4, 0, keepdims=False)


def scatter_four(parts, place, first):
    received = [
        lax.ppermute(rounded(part_at(parts, place + offset)), "seq", ring_pairs(first, offset)) for offset in (1, 2, 3)
    ]
    total = part_at(parts, place)
    for block in received:
        total = total + block.astype(jnp.float32)
    return total


def exchange_four(block, first):
    return [block] + [lax.ppermute(block, "seq", ring_pairs(first, offset)) for offset in (1, 2, 3)]


def sum_four(blocks):
    a, b, c, d = [block.astype(jnp.float32) for block in blocks]
    return (a + c) + (b + d)


def in_places(blocks, place):
    return jnp.concatenate([pick((place - j) % 4, blocks) for j in range(4)], axis=0)


def middle_half(half, core):
    return swap_cores(jnp.where(core == 0, half[256:], half[:128]))


def together(*values):
    return lax.optimization_barrier(values)


def body(
    inputs,
    token_rates,
    proj_query,
    proj_key,
    proj_value,
    proj_output,
    fast_in,
    fast_up,
    fast_out,
    cotangent,
):
    core_at, place, second = places()
    core = core_at.reshape(1)
    rates = token_rates.reshape(1, -1)

    query_rows, key_rows, value_rows, scaled, kept, sent = update_rows(
        core, inputs, rates, proj_query, proj_key, proj_value, fast_in, fast_up, fast_out
    )
    quarter = scatter_four((kept + swap_cores(sent).astype(F32)).reshape(4, 96, 512), place, True)
    shared = sum_four(exchange_four(rounded(quarter), False))
    back_output, fast_own = back_output_rows(core, together(shared, cotangent)[1], proj_output, fast_in, fast_out)
    blocks, back_output, fast_own = together(exchange_four(rounded(shared), True), back_output, fast_own)
    half = in_places(blocks, place)
    totals = half, middle_half(half, core_at)
    n_own, n_up, *trail = ortho(core, *totals, fast_own, fast_up)
    n_other = swap_cores(n_own)

    back_p, back_r, hidden_q, kept, sent = query_rows_back(core, query_rows, back_output, n_own, n_other, n_up)
    half = (kept + swap_cores(sent).astype(F32)).reshape(4, 96, 512)
    half, hidden_q, back_p, back_r = together(half, hidden_q, back_p, back_r)
    out_kept, out_sent = out_grads(core, hidden_q, n_own, n_other, cotangent)
    quarter, out_kept, out_sent, back_p, back_r = together(scatter_four(half, place, True), out_kept, out_sent, back_p, back_r)
    query_grad, query_kept, query_sent = query_grads(core, back_p, back_r, n_own, n_other, n_up, inputs)
    blocks, query_grad, query_kept, query_sent = together(
        exchange_four(rounded(quarter), False), query_grad, query_kept, query_sent
    )
    adjoint_share = sum_four(blocks)
    blocks = exchange_four(rounded(adjoint_share), True)
    early_sent = jnp.concatenate([query_sent, out_sent], axis=1)
    half = in_places(blocks, place)
    b_own, b_up = ortho_back(core, totals, (half, middle_half(half, core_at)), trail)
    b_other = swap_cores(b_own)
    early = jnp.concatenate([query_kept, out_kept], axis=1)
    early_in = swap_cores(early_sent)

    key_grad, value_grad, back_rate, kept, sent = update_back(
        core, inputs, key_rows, value_rows, scaled, rates, fast_in, fast_up, fast_out, b_own, b_other, b_up
    )
    back_inputs = input_back(query_grad, key_grad, value_grad, proj_query, proj_key, proj_value)
    place_at, back_inputs = together(place.reshape(1), back_inputs)
    *blocks, mine = pack_both(place_at, kept, swap_cores(sent), early, early_in)
    blocks = [lax.ppermute(block, "seq", ring_pairs(True, offset + 1)) for offset, block in enumerate(blocks)]
    *blocks, contrib, mine = unpack(second.reshape(1), mine, blocks)
    received = [lax.ppermute(block, "seq", ring_pairs(False, offset + 1)) for offset, block in enumerate(blocks)]
    summed = sum_four([contrib] + [block[:192] for block in received])
    for block in received:
        mine = mine + block[192:].astype(F32)
    grad_key, grad_value, grad_query, grad_output = [mine[24 * index : 24 * index + 24] for index in range(4)]
    share = adjoint_share + jnp.concatenate([summed[:96], summed[96:]], axis=1)
    blocks = exchange_four(rounded(share), True)
    half = in_places(blocks, place)
    grad_in, grad_up, grad_out = finish(core, half, swap_cores(half))
    return (
        back_inputs,
        back_rate.reshape(-1),
        grad_in,
        grad_up,
        grad_out,
        grad_query,
        grad_key,
        grad_value,
        grad_output.T,
    )


def solution(mesh):
    in_specs = (
        P(("batch", "seq"), None),
        P(("batch", "seq")),
        P(),
        P(),
        P(),
        P(),
        P(),
        P(),
        P(),
        P(("batch", "seq"), None),
    )
    out_specs = (
        P(("batch", "seq"), None),
        P(("batch", "seq")),
        P("batch", None),
        P("batch", None),
        P("batch", None),
        P("seq", "batch"),
        P("seq", "batch"),
        P("seq", "batch"),
        P("batch", "seq"),
    )
    return jax.shard_map(body, mesh=mesh, in_specs=in_specs, out_specs=out_specs, check_vma=False)
```
